32 devices in a mesh: lat: 8 (over z, x), tp: 4 (over y, core).
Axes of the slice: x: 2, y: 2, z: 4, core: 2. Of those that a mesh axis runs over, the one named last changes fastest.
Arguments:
- features: bfloat16 [42, 2, 96, 1024], P(None, None, 'lat', 'tp'), may hold values from -6 to 6
- target: bfloat16 [42, 2, 96, 1024], P(None, None, 'lat', 'tp'), may hold values from -6 to 6
- w_qkv: bfloat16 [1024, 3, 1024], P(None, None, 'tp'), may hold values from -1 to 1
- w_proj: bfloat16 [1024, 1024], P('tp'), may hold values from -0.1875 to 0.1875
- qkv_clip: float32 [2, 3, 1024], P(None, None, 'tp'), may hold values from 0.5 to 3
- proj_clip: float32 [2, 1024], replicated, may hold values from 0.5 to 3
- shift_offset: int32 [1], replicated, may hold values from 0 to 5
- region_ids: int32 [42, 2, 96], replicated, may hold values from 0 to 1
Outputs:
- mixed: bfloat16 [42, 2, 96, 1024], P(None, None, 'lat', 'tp')
- qkv_clip_grad: float32 [2, 3, 1024], P(None, None, 'tp')
- proj_clip_grad: float32 [2, 1024], replicated
The draws below stay inside these ranges and needn't reach their ends.
All inputs are finite; a program needn't handle non-finite values.
Results may differ from the reference program's by a relative error of at most 0.0058.
Values may be sent and summed in bfloat16 or wider, within the bound.
No kernel may reach another device: no remote copies, remote signals or barrier semaphores. Data moves between devices by JAX's collectives and lax.ppermute only.
A program may use at most 128 MiB of HBM per device.

```python
import jax
import jax.numpy as jnp
from jax import lax

D = 1024
HD = 64
WLAT = 6
WLON = 12
LEV = 2
LATR = 42
NLON = 96


def draw_features(key, part):
    key = jax.random.fold_in(key, 11)
    value = jax.random.truncated_normal(key, -6.0, 6.0, (LATR, LEV, NLON, D), jnp.float32)
    return value.astype(jnp.bfloat16)


def draw_w_qkv(key, part):
    key = jax.random.fold_in(key, 17)
    entry_key = jax.random.fold_in(key, 0)
    entries = jax.random.truncated_normal(entry_key, -4.0, 4.0, (D, 3, D), jnp.float32) * D ** (-0.5)
    value = entries
    return value.astype(jnp.bfloat16)


def plant(result, key, low, high):
    dims = result.shape
    index_at = [jax.random.randint(jax.random.fold_in(key, axis), (), 0, dims[axis]) for axis in range(len(dims))]
    result = result.at[tuple(index_at)].set(low)
    longest = dims.index(max(dims))
    index_at[longest] = (index_at[longest] + 1) % dims[longest]
    return result.at[tuple(index_at)].set(high)


def steps_of(key, dims, shards, low, largest):
    level, own = 1.0, jax.random.fold_in(key, 6)
    for position, blocks in shards:
        draws = jnp.exp(jax.random.uniform(jax.random.fold_in(own, position), (blocks,), jnp.float32, low / len(shards), largest / len(shards)))
        level = level * jnp.repeat(draws, dims[position] // blocks).reshape([-1 if axis == position else 1 for axis in range(len(dims))])
    return level


def scatter_about(key, extent, scale, most, pieces=(), kind=jnp.bfloat16):
    result = scale * jax.random.normal(key, extent, jnp.float32)
    if pieces:
        result = result * steps_of(key, extent, pieces, -0.22, 0.18)
    return jnp.clip(result, -most, most).astype(kind)


def setup_inputs(seed: int = 0) -> dict:
    arg_keys = jax.random.split(jax.random.key(seed), 9)
    features = draw_features(jax.random.fold_in(arg_keys[8], 71), 0)
    target = scatter_about(arg_keys[1], (LATR, LEV, NLON, D), 1.0, 6.0, ((2, 8), (3, 4)))
    w_qkv = draw_w_qkv(jax.random.fold_in(arg_keys[8], 71), 0)
    w_proj = scatter_about(arg_keys[3], (D, D), D ** -0.5, 0.1875, ((0, 4),))
    qkv_clip = jnp.clip(0.5 + 2.5 * jax.random.uniform(arg_keys[4], (2, 3, D), jnp.float32) ** steps_of(arg_keys[4], (2, 3, D), ((2, 4),), -0.2, 0.2), 0.5, 3.0)
    proj_clip = jnp.clip(jax.random.uniform(arg_keys[5], (2, D), jnp.float32, 0.5, 3.0), 0.5, 3.0)
    shift_offset = jax.random.randint(arg_keys[6], (1,), 0, WLAT).astype(jnp.int32)
    region_ids = plant(jax.random.randint(arg_keys[7], (LATR, LEV, NLON), 0, 2), jax.random.fold_in(arg_keys[7], 1), 0, 1).astype(jnp.int32)
    return dict(features=features, target=target, w_qkv=w_qkv, w_proj=w_proj, qkv_clip=qkv_clip, proj_clip=proj_clip, shift_offset=shift_offset, region_ids=region_ids)


EPS = 1e-05
NEG = -1e+30

def to_bf(value):
    return lax.optimization_barrier(value.astype(jnp.bfloat16)).astype(jnp.float32)

def clipped(weight, hi_logit, lo_logit, top, low):
    hi_gate = jax.nn.sigmoid(hi_logit)
    lo_gate = jax.nn.sigmoid(lo_logit)
    upper = hi_gate * top
    lower = lo_gate * low
    return (jnp.minimum(jnp.maximum(weight, lower), upper), upper, lower, hi_gate, lo_gate)

def clip_grads(grad_w, weight, upper, lower, hi_gate, lo_gate, top, low):
    g_hi = lax.optimization_barrier(jnp.sum(jnp.where(weight > upper, grad_w, 0.0), axis=0)) * hi_gate * (1.0 - hi_gate) * top
    g_lo = lax.optimization_barrier(jnp.sum(jnp.where(weight < lower, grad_w, 0.0), axis=0)) * lo_gate * (1.0 - lo_gate) * low
    return jnp.stack([g_hi, g_lo])

def to_windows(block, rows_w, lon_w):
    rows, lev, lon, width = block.shape
    heads = width // HD
    block = block.reshape(rows // rows_w, rows_w, lev, lon // lon_w, lon_w, heads, HD)
    block = block.transpose(0, 3, 5, 1, 2, 4, 6)
    return block.reshape(rows // rows_w * (lon // lon_w), heads, rows_w * lev * lon_w, HD)

def from_windows(block, rows, lev, lon, rows_w, lon_w):
    nwin, heads, count, size = block.shape
    block = block.reshape(rows // rows_w, lon // lon_w, heads, rows_w, lev, lon_w, size)
    block = block.transpose(0, 3, 4, 1, 5, 2, 6)
    return block.reshape(rows, lev, lon, heads * size)

def id_windows(ids, rows_w, lon_w):
    rows, lev, lon = ids.shape
    ids = ids.reshape(rows // rows_w, rows_w, lev, lon // lon_w, lon_w).transpose(0, 3, 1, 2, 4)
    return ids.reshape(rows // rows_w * (lon // lon_w), rows_w * lev * lon_w)

def shift_rows(block, offset, fill):
    widths = [(WLAT, WLAT)] + [(0, 0)] * (block.ndim - 1)
    padded = jnp.pad(block, widths, constant_values=fill)
    return lax.dynamic_slice_in_dim(padded, (WLAT - offset).astype(jnp.int32), block.shape[0] + WLAT, 0)

def unshift_rows(block, offset, count):
    return lax.dynamic_slice_in_dim(block, offset.astype(jnp.int32), count, 0)

def probabilities(query, key, q_ids, k_ids):
    scores = jnp.einsum('whqe,whke->whqk', query.astype(jnp.float32), key.astype(jnp.float32)) * HD ** (-0.5)
    allowed = (q_ids[:, None, :, None] == k_ids[:, None, None, :]) & (k_ids[:, None, None, :] >= 0)
    scores = jnp.where(allowed, scores, NEG)
    peak = lax.optimization_barrier(jnp.max(scores, axis=-1, keepdims=True))
    expd = jnp.exp(scores - peak)
    return expd / lax.optimization_barrier(jnp.sum(expd, axis=-1, keepdims=True))

def reference(features, target, w_qkv, w_proj, qkv_clip, proj_clip, shift_offset, region_ids):
    f32 = jnp.float32
    bf = jnp.bfloat16
    half = WLON // 2
    offset = shift_offset[0].astype(jnp.int32)
    wq = w_qkv.astype(f32)
    q_top = lax.optimization_barrier(jnp.max(wq, axis=0))
    q_low = lax.optimization_barrier(jnp.min(wq, axis=0))
    wq_clip, q_up, q_lw, q_hg, q_lg = clipped(wq, qkv_clip[0], qkv_clip[1], q_top, q_low)
    wq_b = wq_clip.astype(bf)
    wp = w_proj.astype(f32)
    p_top = lax.optimization_barrier(jnp.max(wp, axis=0))
    p_low = lax.optimization_barrier(jnp.min(wp, axis=0))
    wp_clip, p_up, p_lw, p_hg, p_lg = clipped(wp, proj_clip[0], proj_clip[1], p_top, p_low)
    wp_b = wp_clip.astype(bf)
    x = features.astype(f32)
    mean = lax.optimization_barrier(jnp.mean(x, axis=-1, keepdims=True))
    var = lax.optimization_barrier(jnp.mean(jnp.square(x - mean), axis=-1, keepdims=True))
    normed = ((x - mean) * lax.rsqrt(var + EPS)).astype(bf)
    qkv = jnp.einsum('rlcd,dke->rlcke', normed.astype(f32), wq_b.astype(f32)).astype(bf)
    qkv = shift_rows(jnp.roll(qkv, -half, axis=2), offset, 0)
    ids = shift_rows(jnp.roll(region_ids, -half, axis=2), offset, -1)
    starts = jnp.arange(LATR // WLAT + 1, dtype=jnp.int32) * WLAT

    def window_inputs(start):
        block = lax.dynamic_slice_in_dim(qkv, start.astype(jnp.int32), WLAT, 0)
        idw = id_windows(lax.dynamic_slice_in_dim(ids, start.astype(jnp.int32), WLAT, 0), WLAT, WLON)
        query = to_windows(block[:, :, :, 0], WLAT, WLON)
        key = to_windows(block[:, :, :, 1], WLAT, WLON)
        value = to_windows(block[:, :, :, 2], WLAT, WLON)
        return (query, key, value, idw)

    def forward_window(start):
        query, key, value, idw = window_inputs(start)
        probs = probabilities(query, key, idw, idw)
        out = jnp.einsum('whqk,whke->whqe', to_bf(probs), value.astype(f32)).astype(bf)
        return from_windows(out, WLAT, LEV, NLON, WLAT, WLON)
    attn = lax.map(forward_window, starts).reshape(LATR + WLAT, LEV, NLON, D)
    attn = jnp.roll(unshift_rows(attn, offset, LATR), half, axis=2)
    proj = jnp.einsum('rlce,ef->rlcf', attn.astype(f32), wp_b.astype(f32))
    y = x + proj
    mixed = y.astype(bf)
    err = (y - target.astype(f32)).astype(bf)
    grad_wp = jnp.einsum('rlce,rlcf->ef', attn.astype(f32), err.astype(f32))
    d_attn = jnp.einsum('rlcf,ef->rlce', err.astype(f32), wp_b.astype(f32)).astype(bf)
    d_pad = shift_rows(jnp.roll(d_attn, -half, axis=2), offset, 0)

    def backward_window(start):
        query, key, value, idw = window_inputs(start)
        d_win = to_windows(lax.dynamic_slice_in_dim(d_pad, start.astype(jnp.int32), WLAT, 0), WLAT, WLON).astype(f32)
        probs = probabilities(query, key, idw, idw)
        grad_v = jnp.einsum('whqk,whqe->whke', to_bf(probs), d_win)
        grad_p = jnp.einsum('whqe,whke->whqk', d_win, value.astype(f32))
        grad_s = to_bf(probs * (grad_p - lax.optimization_barrier(jnp.sum(probs * grad_p, axis=-1, keepdims=True))))
        grad_q = jnp.einsum('whqk,whke->whqe', grad_s, key.astype(f32)) * HD ** (-0.5)
        grad_k = jnp.einsum('whqk,whqe->whke', grad_s, query.astype(f32)) * HD ** (-0.5)
        return jnp.stack([from_windows(grad_q, WLAT, LEV, NLON, WLAT, WLON), from_windows(grad_k, WLAT, LEV, NLON, WLAT, WLON), from_windows(grad_v, WLAT, LEV, NLON, WLAT, WLON)], axis=3)
    grads = lax.map(backward_window, starts).reshape(LATR + WLAT, LEV, NLON, 3, D)
    grad_qkv = jnp.roll(unshift_rows(grads, offset, LATR), half, axis=2).astype(bf)
    grad_wq = jnp.einsum('rlcd,rlcke->dke', normed.astype(f32), grad_qkv.astype(f32))
    qkv_clip_grad = clip_grads(grad_wq, wq, q_up, q_lw, q_hg, q_lg, q_top, q_low)
    proj_clip_grad = clip_grads(grad_wp, wp, p_up, p_lw, p_hg, p_lg, p_top, p_low)
    return (mixed, qkv_clip_grad, proj_clip_grad)
```

```python
import jax
import jax.numpy as jnp
from jax import lax
from jax.experimental import pallas as pl
from jax.experimental.pallas import tpu as pltpu
from jax.sharding import PartitionSpec as P

HD = 64
WLAT = 6
EPS = 1e-05
NEG = -1e30
F32 = jnp.float32
BF = jnp.bfloat16
SCALE = HD ** (-0.5)
NT = (((1,), (1,)), ((), ()))
TN = (((0,), (0,)), ((), ()))


def spec(n):
    return [pl.BlockSpec(memory_space=pltpu.VMEM)] * n


def params(mib):
    return pltpu.CompilerParams(vmem_limit_bytes=mib * 1024 * 1024)


def bounds_of(weight, logits_hi, logits_lo):
    top = jnp.max(weight, axis=0, keepdims=True)
    low = jnp.min(weight, axis=0, keepdims=True)
    hi = 1.0 / (1.0 + jnp.exp(-logits_hi))
    lo = 1.0 / (1.0 + jnp.exp(-logits_lo))
    return hi * top, lo * low, hi * (1.0 - hi) * top, lo * (1.0 - lo) * low


def clip_qkv_kernel(w_ref, c_ref, wc_ref, b_ref):
    def body(i, carry):
        w = w_ref[i].astype(F32)
        up, lw, fh, fl = bounds_of(w, c_ref[i, 0:1], c_ref[i, 1:2])
        wc_ref[i] = jnp.minimum(jnp.maximum(w, lw), up).astype(BF)
        b_ref[i, 0:1] = up
        b_ref[i, 1:2] = lw
        b_ref[i, 2:3] = fh
        b_ref[i, 3:4] = fl
        return carry

    lax.fori_loop(0, 3, body, 0)


def clip_qkv(w, clips):
    n, d, e = w.shape
    return pl.pallas_call(
        clip_qkv_kernel,
        out_shape=(
            jax.ShapeDtypeStruct((n, d, e), BF),
            jax.ShapeDtypeStruct((n, 8, e), F32),
        ),
        in_specs=spec(2),
        out_specs=tuple(spec(2)),
        compiler_params=params(24),
        cost_estimate=pl.CostEstimate(flops=10 * n * d * e, bytes_accessed=4 * n * d * e, transcendentals=0),
    )(w, clips)


def clip_proj_kernel(w0, w1, w2, w3, c_ref, wc_ref, b_ref):
    shards = (w0, w1, w2, w3)
    size = w0.shape[0]

    def body(i, carry):
        cols = pl.ds(pl.multiple_of(i * 256, 256), 256)
        w = jnp.concatenate([s[:, cols].astype(F32) for s in shards], axis=0)
        up, lw, fh, fl = bounds_of(w, c_ref[0:1, cols], c_ref[1:2, cols])
        wc = jnp.minimum(jnp.maximum(w, lw), up).astype(BF)
        wc_ref[:, cols] = wc
        b_ref[0:1, cols] = up
        b_ref[1:2, cols] = lw
        b_ref[2:3, cols] = fh
        b_ref[3:4, cols] = fl
        return carry

    lax.fori_loop(0, w0.shape[1] // 256, body, 0)


def clip_proj(shards, clips):
    e, d = shards[0].shape
    return pl.pallas_call(
        clip_proj_kernel,
        out_shape=(
            jax.ShapeDtypeStruct((4 * e, d), BF),
            jax.ShapeDtypeStruct((8, d), F32),
        ),
        in_specs=spec(5),
        out_specs=tuple(spec(2)),
        compiler_params=params(24),
        cost_estimate=pl.CostEstimate(flops=40 * e * d, bytes_accessed=16 * e * d, transcendentals=0),
    )(*shards, clips)


def stacked(block, mask_a, mask_b):
    return jnp.concatenate([block * mask_a, block * mask_b], axis=0)


def head_masks():
    lane = lax.broadcasted_iota(jnp.int32, (1, 2 * HD), 1)
    mask_a = jnp.where(lane < HD, 1.0, 0.0).astype(BF)
    mask_b = jnp.where(lane < HD, 0.0, 1.0).astype(BF)
    return mask_a, mask_b


def probs_t(k, q2, allowed):
    st = lax.dot_general(k, q2, NT, preferred_element_type=F32) * SCALE
    st = jnp.where(allowed, st, NEG)
    e = jnp.exp(st - jnp.max(st, axis=0, keepdims=True))
    return e * (1.0 / jnp.sum(e, axis=0, keepdims=True))


def merge_heads(t_block):
    both = t_block.T
    n = both.shape[0] // 2
    lane = lax.broadcasted_iota(jnp.int32, (n, 2 * HD), 1)
    return jnp.where(lane < HD, both[:n], both[n:])


def allowed_t(idk_ref, idq_ref, w, cells):
    rows = pl.ds(pl.multiple_of(w * cells, 16), cells)
    idk = idk_ref[rows, :]
    return (idk == idq_ref[w]) & (idk >= 0)


def forward_kernel(t_ref, *refs):
    pieces = refs[:8]
    wo_ref, wp_ref, idk_ref, idq_ref, normed_ref, qkv_ref, attn_ref, xs = refs[8:]
    t = t_ref[0]
    half = pieces[0].shape[0] // 4
    cells = 2 * half
    width = pieces[0].shape[1]
    for k in range(4):
        cols = pl.ds(pl.multiple_of((t ^ k) * width, width), width)
        for s in range(2):
            for p in range(2):
                block = pieces[4 * s + k][cells * p : cells * (p + 1), :].astype(F32)
                for i in range(2):
                    first = cells * (2 * p + i) + half * s
                    xs[first : first + half, cols] = block[half * i : half * (i + 1)]

    def norm(w, carry):
        rows = pl.ds(pl.multiple_of(w * 48, 16), 48)
        x = xs[rows, :]
        mean = jnp.mean(x, axis=-1, keepdims=True)
        x = x - mean
        var = jnp.mean(x * x, axis=-1, keepdims=True)
        normed_ref[rows, :] = (x * lax.rsqrt(var + EPS)).astype(BF)
        return carry

    lax.fori_loop(0, 12, norm, 0)

    def project(i, carry):
        for g, w_ref in enumerate((wo_ref, wp_ref)):
            qkv_ref[3 * g + i] = jnp.dot(
                normed_ref[...], w_ref[i], preferred_element_type=F32
            ).astype(BF)
        return carry

    lax.fori_loop(0, 3, project, 0)
    mask_a, mask_b = head_masks()

    def window(w, carry):
        rows = pl.ds(pl.multiple_of(w * cells, 16), cells)
        allowed = allowed_t(idk_ref, idq_ref, w, cells)
        for hp in range(4):
            g, lanes = hp // 2, slice(128 * (hp % 2), 128 * (hp % 2) + 128)
            q2 = stacked(qkv_ref[3 * g, rows, lanes], mask_a, mask_b)
            pt = probs_t(qkv_ref[3 * g + 1, rows, lanes], q2, allowed)
            ot = lax.dot_general(
                qkv_ref[3 * g + 2, rows, lanes], pt.astype(BF), TN, preferred_element_type=F32
            )
            attn_ref[rows, 128 * hp : 128 * hp + 128] = merge_heads(ot).astype(BF)
        return carry

    lax.fori_loop(0, 4, window, 0)


def forward(t, pieces, wo, wp, idk, idq):
    n, width = pieces[0].shape
    d = 4 * width
    return pl.pallas_call(
        forward_kernel,
        out_shape=(
            jax.ShapeDtypeStruct((2 * n, d), BF),
            jax.ShapeDtypeStruct((6, 2 * n, width), BF),
            jax.ShapeDtypeStruct((2 * n, 2 * width), BF),
        ),
        in_specs=[pl.BlockSpec(memory_space=pltpu.SMEM)] + spec(12),
        out_specs=tuple(spec(3)),
        scratch_shapes=[pltpu.VMEM((2 * n, d), F32)],
        compiler_params=params(40),
        cost_estimate=pl.CostEstimate(flops=8 * 10**9, bytes_accessed=10 * 10**6, transcendentals=10**6),
    )(t, *pieces, wo, wp, idk, idq)


def turn_kernel(normed_ref, attn_ref, normed_t, attn_t):
    d = normed_ref.shape[1]

    def body(i, carry):
        cols = pl.ds(pl.multiple_of(i * 256, 256), 256)
        normed_t[cols, :] = normed_ref[:, cols].T
        return carry

    lax.fori_loop(0, d // 256, body, 0)

    def body2(i, carry):
        cols = pl.ds(pl.multiple_of(i * 256, 256), 256)
        attn_t[cols, :] = attn_ref[:, cols].T
        return carry

    lax.fori_loop(0, attn_ref.shape[1] // 256, body2, 0)


def turn(normed, attn):
    n, d = normed.shape
    e = attn.shape[1]
    return pl.pallas_call(
        turn_kernel,
        out_shape=(jax.ShapeDtypeStruct((d, n), BF), jax.ShapeDtypeStruct((e, n), BF)),
        in_specs=spec(2),
        out_specs=tuple(spec(2)),
        compiler_params=params(24),
        cost_estimate=pl.CostEstimate(flops=10**9, bytes_accessed=4 * n * (d + e), transcendentals=0),
    )(normed, attn)


def output_kernel(t_ref, *refs):
    pieces, targets = refs[:8], refs[8:16]
    own_ref, other_ref, wc_ref, idk_ref = refs[16:20]
    mixed, err_ref, y_ref = refs[20:24], refs[24], refs[25]
    t = t_ref[0]
    half = pieces[0].shape[0] // 4
    cells = 2 * half
    width = pieces[0].shape[1]
    e = own_ref.shape[1]
    for k in range(4):
        cols = pl.ds(pl.multiple_of((t ^ k) * width, width), width)
        y_ref[...] = jnp.dot(own_ref[...], wc_ref[:e, cols], preferred_element_type=F32) + jnp.dot(
            other_ref[...], wc_ref[e:, cols], preferred_element_type=F32
        )
        for p in range(2):
            errs = [[None, None], [None, None]]
            for s in range(2):
                block = pieces[4 * s + k][cells * p : cells * (p + 1), :].astype(F32)
                wanted = targets[4 * s + k][cells * p : cells * (p + 1), :].astype(F32)
                ys = []
                for i in range(2):
                    first = cells * (2 * p + i) + half * s
                    part = slice(half * i, half * (i + 1))
                    y = block[part] + y_ref[first : first + half, :]
                    ys.append(y)
                    valid = idk_ref[first : first + half, :] >= 0
                    errs[i][s] = jnp.where(valid, y - wanted[part], 0.0)
                if k < 2:
                    mixed[2 * s + k][cells * p : cells * (p + 1), :] = jnp.concatenate(
                        ys, axis=0
                    ).astype(BF)
            for i in range(2):
                first = cells * (2 * p + i)
                err_ref[first : first + cells, cols] = jnp.concatenate(errs[i], axis=0).astype(BF)


def output(t, pieces, targets, own, other, wc, idk):
    n, width = pieces[0].shape
    d = 4 * width
    piece = jax.ShapeDtypeStruct((n, width), BF)
    return pl.pallas_call(
        output_kernel,
        out_shape=(piece, piece, piece, piece, jax.ShapeDtypeStruct((2 * n, d), BF)),
        in_specs=[pl.BlockSpec(memory_space=pltpu.SMEM)] + spec(20),
        out_specs=tuple(spec(5)),
        scratch_shapes=[pltpu.VMEM((2 * n, width), F32)],
        compiler_params=params(40),
        cost_estimate=pl.CostEstimate(flops=2 * 10**9, bytes_accessed=8 * 10**6, transcendentals=0),
    )(t, *pieces, *targets, own, other, wc, idk)


def masked_sums(grad, w, bounds):
    g_hi = jnp.sum(jnp.where(w > bounds[0:1], grad, 0.0), axis=0, keepdims=True) * bounds[2:3]
    g_lo = jnp.sum(jnp.where(w < bounds[1:2], grad, 0.0), axis=0, keepdims=True) * bounds[3:4]
    return g_hi, g_lo


def backward_kernel(
    err_ref, wc_ref, attn_t, qkv_ref, normed_t, wo_ref, wp_ref, bo_ref, bp_ref, po_ref, pp_ref, pb_ref,
    idk_ref, idq_ref, gq_ref, gp_ref, d_ref, g_ref
):
    e = attn_t.shape[0]
    cells = idk_ref.shape[0] // 4
    d_ref[...] = lax.dot_general(err_ref[...], wc_ref[:e], NT, preferred_element_type=F32).astype(BF)
    mask_a, mask_b = head_masks()

    def window(w, carry):
        rows = pl.ds(pl.multiple_of(w * cells, 16), cells)
        allowed = allowed_t(idk_ref, idq_ref, w, cells)
        for hp in range(4):
            g, lanes = hp // 2, slice(128 * (hp % 2), 128 * (hp % 2) + 128)
            q2 = stacked(qkv_ref[3 * g, rows, lanes], mask_a, mask_b)
            k = qkv_ref[3 * g + 1, rows, lanes]
            v = qkv_ref[3 * g + 2, rows, lanes]
            pt = probs_t(k, q2, allowed)
            d2 = stacked(d_ref[rows, 128 * hp : 128 * hp + 128], mask_a, mask_b)
            g_ref[3 * g + 2, rows, lanes] = jnp.dot(
                pt.astype(BF), d2, preferred_element_type=F32
            ).astype(BF)
            dpt = lax.dot_general(v, d2, NT, preferred_element_type=F32)
            gst = (pt * (dpt - jnp.sum(pt * dpt, axis=0, keepdims=True))).astype(BF)
            g_ref[3 * g + 1, rows, lanes] = (
                jnp.dot(gst, q2, preferred_element_type=F32) * SCALE
            ).astype(BF)
            gqt = lax.dot_general(k, gst, TN, preferred_element_type=F32) * SCALE
            g_ref[3 * g, rows, lanes] = merge_heads(gqt).astype(BF)
        return carry

    lax.fori_loop(0, 4, window, 0)

    def proj_part(i, carry):
        cols = pl.ds(pl.multiple_of(i * 256, 256), 256)
        grad = jnp.dot(attn_t[...], err_ref[:, cols], preferred_element_type=F32)
        n = po_ref.shape[0]
        b = pb_ref[:, cols]
        h0, l0 = masked_sums(grad[:n], po_ref[:, cols].astype(F32), b)
        h1, l1 = masked_sums(grad[n:], pp_ref[:, cols].astype(F32), b)
        gp_ref[0:1, cols] = h0 + h1
        gp_ref[1:2, cols] = l0 + l1
        return carry

    lax.fori_loop(0, err_ref.shape[1] // 256, proj_part, 0)

    def qkv_part(i, carry):
        for g, (w_ref, b_ref) in enumerate(((wo_ref, bo_ref), (wp_ref, bp_ref))):
            grad = jnp.dot(normed_t[...], g_ref[3 * g + i], preferred_element_type=F32)
            hi, lo = masked_sums(grad, w_ref[i].astype(F32), b_ref[i])
            gq_ref[3 * g + i, 0:1] = hi
            gq_ref[3 * g + i, 1:2] = lo
        return carry

    lax.fori_loop(0, 3, qkv_part, 0)


def backward(err, wc, attn_t, qkv, normed_t, wo, wp, bo, bp, po, pp, pb, idk, idq):
    n, d = err.shape
    width = qkv.shape[2]
    return pl.pallas_call(
        backward_kernel,
        out_shape=(jax.ShapeDtypeStruct((6, 2, width), F32), jax.ShapeDtypeStruct((2, d), F32)),
        in_specs=spec(14),
        out_specs=tuple(spec(2)),
        scratch_shapes=[pltpu.VMEM((n, attn_t.shape[0]), BF), pltpu.VMEM((6, n, width), BF)],
        compiler_params=params(40),
        cost_estimate=pl.CostEstimate(flops=8 * 10**9, bytes_accessed=10 * 10**6, transcendentals=10**6),
    )(err, wc, attn_t, qkv, normed_t, wo, wp, bo, bp, po, pp, pb, idk, idq)


def send(block, shift, flip):
    count, tp = lax.axis_size("lat"), lax.axis_size("tp")
    route = [
        (u * tp + t, ((u + shift) % count) * tp + (t ^ flip)) for u in range(count) for t in range(tp)
    ]
    return lax.ppermute(block, ("lat", "tp"), route)


def after(block, *others):
    return lax.optimization_barrier((block, *others))[0]


def local(features, target, w_qkv, w_proj, qkv_clip, proj_clip, shift_offset, region_ids):
    rows, lev, lon, width = features.shape
    half = lon // 2
    many = (rows + WLAT) // 2
    sector = lax.axis_index("lat")
    t = lax.axis_index("tp")
    core = t % 2
    offset = shift_offset[0]
    t_arr = jnp.reshape(t, (1,)).astype(jnp.int32)

    def row_parts(block):
        block = jnp.transpose(block, (0, 2, 1, 3))
        padded = jnp.pad(block, ((WLAT, WLAT), (0, 0), (0, 0), (0, 0)))
        parts = []
        for flip in range(2):
            first = WLAT - offset + many * (core ^ flip)
            part = lax.dynamic_slice_in_dim(padded, first, many, 0)
            parts.append(
                [
                    part[:, half:].reshape(many * half * lev, width),
                    part[:, :half].reshape(many * half * lev, width),
                ]
            )
        return parts

    def spread(parts):
        own = [parts[0][0]] + [send(parts[k % 2][0], 0, k) for k in range(1, 4)]
        nxt = [send(parts[k % 2][1], -1, k) for k in range(4)]
        return own + nxt

    w3 = jnp.transpose(w_qkv, (1, 0, 2))
    c3 = jnp.transpose(qkv_clip, (1, 0, 2))
    parts = row_parts(features)
    pieces = spread(parts)
    w3_peer = send(w3, 0, 1)
    c3_peer = send(c3, 0, 1)
    wc_own, b_own = clip_qkv(w3, c3)
    wc_peer, b_peer = clip_qkv(w3_peer, c3_peer)

    doubled = jnp.concatenate([region_ids, region_ids[:, :, :lon]], 2)
    ids = lax.dynamic_slice_in_dim(doubled, sector * lon + half, lon, 2)
    ids = jnp.pad(ids, ((WLAT, WLAT), (0, 0), (0, 0)), constant_values=-1)
    ids = lax.dynamic_slice_in_dim(ids, WLAT - offset + many * core, many, 0)
    ids = ids.reshape(many // WLAT, WLAT, lev, 2, half).transpose(0, 3, 1, 4, 2)
    ids = ids.reshape(many // WLAT, 1, WLAT * lev * lon)
    idk = ids.reshape(many * lev * lon, 1)
    idq = jnp.concatenate([ids, ids], axis=2)

    normed, qkv, attn = forward(t_arr, pieces, wc_own, wc_peer, idk, idq)
    attn_other = send(attn, 0, 2)

    first_in = after(target, pieces[2], pieces[3], pieces[6], pieces[7])
    targets = spread(row_parts(first_in))
    p1 = send(w_proj, 0, 1)
    p2 = send(after(w_proj, pieces[2], pieces[3], pieces[6], pieces[7]), 0, 2)
    p3 = send(p2, 0, 1)
    pc, pb = clip_proj([w_proj, p1, p2, p3], proj_clip)
    normed_t, attn_t = turn(normed, attn)

    m00, m01, m10, m11, err = output(t_arr, pieces, targets, attn, attn_other, pc, idk)
    m01 = send(m01, 0, 1)
    m10 = send(m10, 1, 0)
    m11 = send(m11, 1, 1)

    gq, gp = backward(
        err, pc, attn_t, qkv, normed_t, w3, w3_peer, b_own, b_peer, w_proj, p1, pb, idk, idq
    )

    def grid(block):
        return block.reshape(many, half, lev, width)

    own = jnp.concatenate([grid(m10), grid(m00)], axis=1)
    peer = jnp.concatenate([grid(m11), grid(m01)], axis=1)
    mixed = jnp.concatenate([own, peer, own], axis=0)
    mixed = lax.dynamic_slice_in_dim(mixed, many * core + offset, rows, 0)
    mixed = jnp.transpose(mixed, (0, 2, 1, 3))

    gq_own = gq[:3] + send(gq[3:], 0, 1)
    gp = gp + send(gp, 0, 1)
    gp = gp + send(gp, 0, 2)
    both = jnp.concatenate([gq_own.reshape(-1), gp.reshape(-1)])
    both = lax.psum(both, "lat")
    qkv_sum = jnp.transpose(both[: gq_own.size].reshape(gq_own.shape), (1, 0, 2))
    proj_sum = both[gq_own.size :].reshape(gp.shape)
    return (mixed, qkv_sum, proj_sum)


def solution(mesh):
    placed = (
        P(None, None, "lat", "tp"),
        P(None, None, "lat", "tp"),
        P(None, None, "tp"),
        P("tp", None),
        P(None, None, "tp"),
        P(),
        P(),
        P(),
    )
    return jax.shard_map(
        local,
        mesh=mesh,
        in_specs=placed,
        out_specs=(P(None, None, "lat", "tp"), P(None, None, "tp"), P()),
        check_vma=False,
    )
```

```python
import jax
import jax.numpy as jnp
from jax import lax
from jax.experimental import pallas as pl
from jax.experimental.pallas import tpu as pltpu
from jax.sharding import PartitionSpec as P

HD = 64
WLAT = 6
EPS = 1e-05
NEG = -1e30
F32 = jnp.float32
BF = jnp.bfloat16
SCALE = HD ** (-0.5)
NT = (((1,), (1,)), ((), ()))
TN = (((0,), (0,)), ((), ()))


def spec(n):
    return [pl.BlockSpec(memory_space=pltpu.VMEM)] * n


def params(mib):
    return pltpu.CompilerParams(vmem_limit_bytes=mib * 1024 * 1024)


def bounds_of(weight, logits_hi, logits_lo):
    top = jnp.max(weight, axis=0, keepdims=True)
    low = jnp.min(weight, axis=0, keepdims=True)
    hi = 1.0 / (1.0 + jnp.exp(-logits_hi))
    lo = 1.0 / (1.0 + jnp.exp(-logits_lo))
    return hi * top, lo * low, hi * (1.0 - hi) * top, lo * (1.0 - lo) * low


def clip_qkv_kernel(w_ref, c_ref, wc_ref, b_ref):
    def body(i, carry):
        w = w_ref[i].astype(F32)
        up, lw, fh, fl = bounds_of(w, c_ref[i, 0:1], c_ref[i, 1:2])
        wc_ref[i] = jnp.minimum(jnp.maximum(w, lw), up).astype(BF)
        b_ref[i, 0:1] = up
        b_ref[i, 1:2] = lw
        b_ref[i, 2:3] = fh
        b_ref[i, 3:4] = fl
        return carry

    lax.fori_loop(0, 3, body, 0)


def clip_qkv(w, clips):
    n, d, e = w.shape
    return pl.pallas_call(
        clip_qkv_kernel,
        out_shape=(
            jax.ShapeDtypeStruct((n, d, e), BF),
            jax.ShapeDtypeStruct((n, 8, e), F32),
        ),
        in_specs=spec(2),
        out_specs=tuple(spec(2)),
        compiler_params=params(24),
        cost_estimate=pl.CostEstimate(flops=10 * n * d * e, bytes_accessed=4 * n * d * e, transcendentals=0),
    )(w, clips)


def clip_proj_kernel(w0, w1, w2, w3, c_ref, wc_ref, b_ref):
    shards = (w0, w1, w2, w3)
    size = w0.shape[0]

    def body(i, carry):
        cols = pl.ds(pl.multiple_of(i * 256, 256), 256)
        w = jnp.concatenate([s[:, cols].astype(F32) for s in shards], axis=0)
        up, lw, fh, fl = bounds_of(w, c_ref[0:1, cols], c_ref[1:2, cols])
        wc = jnp.minimum(jnp.maximum(w, lw), up).astype(BF)
        wc_ref[:, cols] = wc
        b_ref[0:1, cols] = up
        b_ref[1:2, cols] = lw
        b_ref[2:3, cols] = fh
        b_ref[3:4, cols] = fl
        return carry

    lax.fori_loop(0, w0.shape[1] // 256, body, 0)


def clip_proj(shards, clips):
    e, d = shards[0].shape
    return pl.pallas_call(
        clip_proj_kernel,
        out_shape=(
            jax.ShapeDtypeStruct((4 * e, d), BF),
            jax.ShapeDtypeStruct((8, d), F32),
        ),
        in_specs=spec(5),
        out_specs=tuple(spec(2)),
        compiler_params=params(24),
        cost_estimate=pl.CostEstimate(flops=40 * e * d, bytes_accessed=16 * e * d, transcendentals=0),
    )(*shards, clips)


def stacked(block, mask_a, mask_b):
    return jnp.concatenate([block * mask_a, block * mask_b], axis=0)


def head_masks():
    lane = lax.broadcasted_iota(jnp.int32, (1, 2 * HD), 1)
    mask_a = jnp.where(lane < HD, 1.0, 0.0).astype(BF)
    mask_b = jnp.where(lane < HD, 0.0, 1.0).astype(BF)
    return mask_a, mask_b


def probs_t(k, q2, allowed):
    st = lax.dot_general(k, q2, NT, preferred_element_type=F32) * SCALE
    st = jnp.where(allowed, st, NEG)
    e = jnp.exp(st - jnp.max(st, axis=0, keepdims=True))
    return e * (1.0 / jnp.sum(e, axis=0, keepdims=True))


def merge_heads(t_block):
    both = t_block.T
    n = both.shape[0] // 2
    lane = lax.broadcasted_iota(jnp.int32, (n, 2 * HD), 1)
    return jnp.where(lane < HD, both[:n], both[n:])


def allowed_t(idk_ref, idq_ref, w, cells):
    rows = pl.ds(pl.multiple_of(w * cells, 16), cells)
    idk = idk_ref[rows, :]
    return (idk == idq_ref[w]) & (idk >= 0)


def forward_kernel(t_ref, *refs):
    pieces = refs[:8]
    wo_ref, wp_ref, idk_ref, idq_ref, normed_ref, qkv_ref, attn_ref, xs = refs[8:]
    t = t_ref[0]
    half = pieces[0].shape[0] // 4
    cells = 2 * half
    width = pieces[0].shape[1]
    for k in range(4):
        cols = pl.ds(pl.multiple_of((t ^ k) * width, width), width)
        for s in range(2):
            for p in range(2):
                block = pieces[4 * s + k][cells * p : cells * (p + 1), :].astype(F32)
                for i in range(2):
                    first = cells * (2 * p + i) + half * s
                    xs[first : first + half, cols] = block[half * i : half * (i + 1)]

    def norm(w, carry):
        rows = pl.ds(pl.multiple_of(w * 48, 16), 48)
        x = xs[rows, :]
        mean = jnp.mean(x, axis=-1, keepdims=True)
        x = x - mean
        var = jnp.mean(x * x, axis=-1, keepdims=True)
        normed_ref[rows, :] = (x * lax.rsqrt(var + EPS)).astype(BF)
        return carry

    lax.fori_loop(0, 12, norm, 0)

    def project(i, carry):
        for g, w_ref in enumerate((wo_ref, wp_ref)):
            qkv_ref[3 * g + i] = jnp.dot(
                normed_ref[...], w_ref[i], preferred_element_type=F32
            ).astype(BF)
        return carry

    lax.fori_loop(0, 3, project, 0)
    attend(qkv_ref, idk_ref, idq_ref, attn_ref, 0, 3)


def attend(qkv_ref, idk_ref, idq_ref, attn_ref, first, last):
    mask_a, mask_b = head_masks()
    cells = idk_ref.shape[0] // 4

    def window(w, carry):
        rows = pl.ds(pl.multiple_of(w * cells, 16), cells)
        to = pl.ds(pl.multiple_of((w - first) * cells, 16), cells)
        allowed = allowed_t(idk_ref, idq_ref, w, cells)
        for hp in range(4):
            g, lanes = hp // 2, slice(128 * (hp % 2), 128 * (hp % 2) + 128)
            q2 = stacked(qkv_ref[3 * g, rows, lanes], mask_a, mask_b)
            pt = probs_t(qkv_ref[3 * g + 1, rows, lanes], q2, allowed)
            ot = lax.dot_general(
                qkv_ref[3 * g + 2, rows, lanes], pt.astype(BF), TN, preferred_element_type=F32
            )
            attn_ref[to, 128 * hp : 128 * hp + 128] = merge_heads(ot).astype(BF)
        return carry

    lax.fori_loop(first, last, window, 0)


def last_kernel(qkv_ref, idk_ref, idq_ref, attn_ref):
    attend(qkv_ref, idk_ref, idq_ref, attn_ref, 3, 4)


def last_window(qkv, idk, idq):
    n, width = qkv.shape[1:]
    return pl.pallas_call(
        last_kernel,
        out_shape=jax.ShapeDtypeStruct((n // 4, 2 * width), BF),
        in_specs=spec(3),
        out_specs=spec(1)[0],
        compiler_params=params(16),
        cost_estimate=pl.CostEstimate(flops=10**9, bytes_accessed=2 * 10**6, transcendentals=10**6),
    )(qkv, idk, idq)


def forward(t, pieces, wo, wp, idk, idq):
    n, width = pieces[0].shape
    d = 4 * width
    return pl.pallas_call(
        forward_kernel,
        out_shape=(
            jax.ShapeDtypeStruct((2 * n, d), BF),
            jax.ShapeDtypeStruct((6, 2 * n, width), BF),
            jax.ShapeDtypeStruct((2 * n // 4 * 3, 2 * width), BF),
        ),
        in_specs=[pl.BlockSpec(memory_space=pltpu.SMEM)] + spec(12),
        out_specs=tuple(spec(3)),
        scratch_shapes=[pltpu.VMEM((2 * n, d), F32)],
        compiler_params=params(24),
        cost_estimate=pl.CostEstimate(flops=8 * 10**9, bytes_accessed=10 * 10**6, transcendentals=10**6),
    )(t, *pieces, wo, wp, idk, idq)


def turn_kernel(normed_ref, a_ref, b_ref, normed_t, attn_t):
    d = normed_ref.shape[1]

    def body(i, carry):
        cols = pl.ds(pl.multiple_of(i * 256, 256), 256)
        normed_t[cols, :] = normed_ref[:, cols].T
        return carry

    lax.fori_loop(0, d // 256, body, 0)

    def body2(i, carry):
        cols = pl.ds(pl.multiple_of(i * 256, 256), 256)
        attn_t[cols, :] = jnp.concatenate([a_ref[:, cols], b_ref[:, cols]], axis=0).T
        return carry

    lax.fori_loop(0, a_ref.shape[1] // 256, body2, 0)


def turn(normed, attn):
    n, d = normed.shape
    e = attn[0].shape[1]
    return pl.pallas_call(
        turn_kernel,
        out_shape=(jax.ShapeDtypeStruct((d, n), BF), jax.ShapeDtypeStruct((e, n), BF)),
        in_specs=spec(3),
        out_specs=tuple(spec(2)),
        compiler_params=params(16),
        cost_estimate=pl.CostEstimate(flops=10**9, bytes_accessed=4 * n * (d + e), transcendentals=0),
    )(normed, *attn)


def output_kernel(t_ref, *refs):
    pieces, targets = refs[:8], refs[8:16]
    attns, wc_ref, idk_ref = refs[16:20], refs[20], refs[21]
    mixed, err_ref, y_ref = refs[22:26], refs[26], refs[27]
    t = t_ref[0]
    half = pieces[0].shape[0] // 4
    cells = 2 * half
    width = pieces[0].shape[1]
    e = attns[0].shape[1]
    for k in range(4):
        cols = pl.ds(pl.multiple_of((t ^ k) * width, width), width)
        own = jnp.concatenate([attns[0][...], attns[1][...]], axis=0)
        other = jnp.concatenate([attns[2][...], attns[3][...]], axis=0)
        y_ref[...] = jnp.dot(own, wc_ref[:e, cols], preferred_element_type=F32) + jnp.dot(
            other, wc_ref[e:, cols], preferred_element_type=F32
        )
        for p in range(2):
            errs = [[None, None], [None, None]]
            for s in range(2):
                block = pieces[4 * s + k][cells * p : cells * (p + 1), :].astype(F32)
                wanted = targets[4 * s + k][cells * p : cells * (p + 1), :].astype(F32)
                ys = []
                for i in range(2):
                    first = cells * (2 * p + i) + half * s
                    part = slice(half * i, half * (i + 1))
                    y = block[part] + y_ref[first : first + half, :]
                    ys.append(y)
                    valid = idk_ref[first : first + half, :] >= 0
                    errs[i][s] = jnp.where(valid, y - wanted[part], 0.0)
                if k < 2:
                    mixed[2 * s + k][cells * p : cells * (p + 1), :] = jnp.concatenate(
                        ys, axis=0
                    ).astype(BF)
            for i in range(2):
                first = cells * (2 * p + i)
                err_ref[first : first + cells, cols] = jnp.concatenate(errs[i], axis=0).astype(BF)


def output(t, pieces, targets, own, other, wc, idk):
    n, width = pieces[0].shape
    d = 4 * width
    piece = jax.ShapeDtypeStruct((n, width), BF)
    return pl.pallas_call(
        output_kernel,
        out_shape=(piece, piece, piece, piece, jax.ShapeDtypeStruct((2 * n, d), BF)),
        in_specs=[pl.BlockSpec(memory_space=pltpu.SMEM)] + spec(22),
        out_specs=tuple(spec(5)),
        scratch_shapes=[pltpu.VMEM((2 * n, width), F32)],
        compiler_params=params(24),
        cost_estimate=pl.CostEstimate(flops=2 * 10**9, bytes_accessed=8 * 10**6, transcendentals=0),
    )(t, *pieces, *targets, *own, *other, wc, idk)


def masked_sums(grad, w, bounds):
    g_hi = jnp.sum(jnp.where(w > bounds[0:1], grad, 0.0), axis=0, keepdims=True) * bounds[2:3]
    g_lo = jnp.sum(jnp.where(w < bounds[1:2], grad, 0.0), axis=0, keepdims=True) * bounds[3:4]
    return g_hi, g_lo


def backward_kernel(
    err_ref, wc_ref, attn_t, qkv_ref, po_ref, pp_ref, pb_ref, idk_ref, idq_ref, g_ref, proj_ref, d_ref
):
    e = attn_t.shape[0]
    cells = idk_ref.shape[0] // 4
    d_ref[...] = lax.dot_general(err_ref[...], wc_ref[:e], NT, preferred_element_type=F32).astype(BF)
    mask_a, mask_b = head_masks()

    def window(w, carry):
        rows = pl.ds(pl.multiple_of(w * cells, 16), cells)
        allowed = allowed_t(idk_ref, idq_ref, w, cells)
        for hp in range(4):
            g, lanes = hp // 2, slice(128 * (hp % 2), 128 * (hp % 2) + 128)
            q2 = stacked(qkv_ref[3 * g, rows, lanes], mask_a, mask_b)
            k = qkv_ref[3 * g + 1, rows, lanes]
            v = qkv_ref[3 * g + 2, rows, lanes]
            pt = probs_t(k, q2, allowed)
            d2 = stacked(d_ref[rows, 128 * hp : 128 * hp + 128], mask_a, mask_b)
            g_ref[3 * g + 2, rows, lanes] = jnp.dot(
                pt.astype(BF), d2, preferred_element_type=F32
            ).astype(BF)
            dpt = lax.dot_general(v, d2, NT, preferred_element_type=F32)
            gst = (pt * (dpt - jnp.sum(pt * dpt, axis=0, keepdims=True))).astype(BF)
            g_ref[3 * g + 1, rows, lanes] = (
                jnp.dot(gst, q2, preferred_element_type=F32) * SCALE
            ).astype(BF)
            gqt = lax.dot_general(k, gst, TN, preferred_element_type=F32) * SCALE
            g_ref[3 * g, rows, lanes] = merge_heads(gqt).astype(BF)
        return carry

    lax.fori_loop(0, 4, window, 0)

    def proj_part(i, carry):
        cols = pl.ds(pl.multiple_of(i * 256, 256), 256)
        grad = jnp.dot(attn_t[...], err_ref[:, cols], preferred_element_type=F32)
        n = po_ref.shape[0]
        b = pb_ref[:, cols]
        h0, l0 = masked_sums(grad[:n], po_ref[:, cols].astype(F32), b)
        h1, l1 = masked_sums(grad[n:], pp_ref[:, cols].astype(F32), b)
        proj_ref[pl.ds(i, 1), :] = h0 + h1
        proj_ref[pl.ds(4 + i, 1), :] = l0 + l1
        return carry

    lax.fori_loop(0, err_ref.shape[1] // 256, proj_part, 0)


def backward(err, wc, attn_t, qkv, po, pp, pb, idk, idq):
    n, width = qkv.shape[1:]
    return pl.pallas_call(
        backward_kernel,
        out_shape=(jax.ShapeDtypeStruct((6, n, width), BF), jax.ShapeDtypeStruct((8, width), F32)),
        in_specs=spec(9),
        out_specs=tuple(spec(2)),
        scratch_shapes=[pltpu.VMEM((n, attn_t.shape[0]), BF)],
        compiler_params=params(20),
        cost_estimate=pl.CostEstimate(flops=8 * 10**9, bytes_accessed=10 * 10**6, transcendentals=10**6),
    )(err, wc, attn_t, qkv, po, pp, pb, idk, idq)


def qkv_sums_kernel(g_ref, normed_t, wo_ref, wp_ref, bo_ref, bp_ref, own_ref, peer_ref):
    def qkv_part(i, carry):
        for g, (w_ref, b_ref, to_ref) in enumerate(
            ((wo_ref, bo_ref, own_ref), (wp_ref, bp_ref, peer_ref))
        ):
            grad = jnp.dot(normed_t[...], g_ref[3 * g + i], preferred_element_type=F32)
            hi, lo = masked_sums(grad, w_ref[i].astype(F32), b_ref[i])
            to_ref[pl.ds(2 * i, 1), :] = hi
            to_ref[pl.ds(2 * i + 1, 1), :] = lo
        return carry

    lax.fori_loop(0, 3, qkv_part, 0)


def qkv_sums(g, normed_t, wo, wp, bo, bp):
    width = g.shape[2]
    return pl.pallas_call(
        qkv_sums_kernel,
        out_shape=(jax.ShapeDtypeStruct((6, width), F32),) * 2,
        in_specs=spec(6),
        out_specs=tuple(spec(2)),
        compiler_params=params(20),
        cost_estimate=pl.CostEstimate(flops=4 * 10**9, bytes_accessed=8 * 10**6, transcendentals=0),
    )(g, normed_t, wo, wp, bo, bp)


def split_kernel(s_ref, x_ref, m0, m1, p0, p1):
    offset, core = s_ref[0], s_ref[1]
    rows, lon, lev, width = x_ref.shape
    many = (rows + WLAT) // 2
    half = lon * lev // 2
    for rel, outs in ((0, (m0, m1)), (1, (p0, p1))):
        base = many * (core ^ rel) - offset

        def body(i, carry):
            parts = [[], []]
            for j in range(4):
                r = base + 4 * i + j
                v = x_ref[jnp.clip(r, 0, rows - 1)].astype(F32).reshape(lon * lev, width)
                v = jnp.where((r >= 0) & (r < rows), v, 0.0)
                parts[0].append(v[half:])
                parts[1].append(v[:half])
            at = pl.ds(pl.multiple_of(4 * half * i, 16), 4 * half)
            for s in range(2):
                outs[s][at, :] = jnp.concatenate(parts[s], axis=0).astype(BF)
            return carry

        lax.fori_loop(0, many // 4, body, 0)


def split(place, block):
    rows, lev, lon, width = block.shape
    block = jnp.transpose(block, (0, 2, 1, 3))
    piece = jax.ShapeDtypeStruct(((rows + WLAT) // 2 * lon * lev // 2, width), BF)
    return pl.pallas_call(
        split_kernel,
        out_shape=(piece,) * 4,
        in_specs=[pl.BlockSpec(memory_space=pltpu.SMEM)] + spec(1),
        out_specs=tuple(spec(4)),
        compiler_params=params(16),
        cost_estimate=pl.CostEstimate(flops=10**6, bytes_accessed=2 * 10**6, transcendentals=0),
    )(place, block)


def join_kernel(s_ref, a0, a1, b0, b1, out_ref, grid_ref):
    offset, core = s_ref[0], s_ref[1]
    rows, lon, lev, width = out_ref.shape
    many = (rows + WLAT) // 2
    half = lon * lev // 2
    for rel, ins in ((0, (a0, a1)), (1, (b0, b1))):
        base = many * (core ^ rel)
        for s in range(2):
            for i in range(many // 4):
                v = ins[s][4 * half * i : 4 * half * (i + 1), :].astype(F32)
                for j in range(4):
                    grid_ref[base + 4 * i + j, half * (1 - s) : half * (2 - s), :] = v[
                        half * j : half * (j + 1)
                    ]

    def body(i, carry):
        for j in range(2):
            r = 2 * i + j
            out_ref[r] = grid_ref[r + offset].reshape(lon, lev, width).astype(BF)
        return carry

    lax.fori_loop(0, rows // 2, body, 0)


def join(place, parts, rows, lon, lev):
    n, width = parts[0].shape
    out = pl.pallas_call(
        join_kernel,
        out_shape=jax.ShapeDtypeStruct((rows, lon, lev, width), BF),
        in_specs=[pl.BlockSpec(memory_space=pltpu.SMEM)] + spec(4),
        out_specs=spec(1)[0],
        scratch_shapes=[pltpu.VMEM((rows + WLAT, lon * lev, width), F32)],
        compiler_params=params(16),
        cost_estimate=pl.CostEstimate(flops=10**6, bytes_accessed=2 * 10**6, transcendentals=0),
    )(place, *parts)
    return jnp.transpose(out, (0, 2, 1, 3))


def send(block, shift, flip):
    count, tp = lax.axis_size("lat"), lax.axis_size("tp")
    route = [
        (u * tp + t, ((u + shift) % count) * tp + (t ^ flip)) for u in range(count) for t in range(tp)
    ]
    return lax.ppermute(block, ("lat", "tp"), route)


def after(block, *others):
    return lax.optimization_barrier((block, *others))[0]


def local(features, target, w_qkv, w_proj, qkv_clip, proj_clip, shift_offset, region_ids):
    rows, lev, lon, width = features.shape
    half = lon // 2
    many = (rows + WLAT) // 2
    sector = lax.axis_index("lat")
    count = lax.axis_size("lat")
    t = lax.axis_index("tp")
    core = t % 2
    offset = shift_offset[0]
    t_arr = jnp.reshape(t, (1,)).astype(jnp.int32)
    place = jnp.stack([offset, core]).astype(jnp.int32)

    m0, m1, p0, p1 = split(place, features)
    f02, f03 = send(m0, 0, 2), send(p0, 0, 3)
    f10, f11 = send(m1, -1, 0), send(p1, -1, 1)
    f01 = send(p0, 0, 1)
    f12, f13 = send(f10, 0, 2), send(f11, 0, 2)

    w3 = jnp.transpose(w_qkv, (1, 0, 2))
    c3 = jnp.transpose(qkv_clip, (1, 0, 2))
    w3_peer = send(w3, 0, 1)
    c3_peer = send(c3, 0, 1)
    wc_own, b_own = clip_qkv(w3, c3)
    wc_peer, b_peer = clip_qkv(w3_peer, c3_peer)

    doubled = jnp.concatenate([region_ids, region_ids[:, :, :lon]], 2)
    ids = lax.dynamic_slice_in_dim(doubled, sector * lon + half, lon, 2)
    ids = jnp.pad(ids, ((WLAT, WLAT), (0, 0), (0, 0)), constant_values=-1)
    ids = lax.dynamic_slice_in_dim(ids, WLAT - offset + many * core, many, 0)
    ids = ids.reshape(many // WLAT, WLAT, lev, 2, half).transpose(0, 3, 1, 4, 2)
    ids = ids.reshape(many // WLAT, 1, WLAT * lev * lon)
    idk = ids.reshape(many * lev * lon, 1)
    idq = jnp.concatenate([ids, ids], axis=2)

    g0, g1, q0, q1 = split(place, target)
    g1, q1, q0 = lax.optimization_barrier((g1, q1, q0, f02, f03, f10, f11))[:3]
    t10, t11 = send(g1, -1, 0), send(q1, -1, 1)
    t01 = send(q0, 0, 1)
    share = w_proj.shape[0] // count
    slab = send(lax.dynamic_slice_in_dim(w_proj, sector * share, share, 0), 0, 2)
    w2 = lax.all_gather(slab, "lat", axis=0, tiled=True)
    w1 = send(after(w_proj, f10, f11), 0, 1)

    ya, yb, yc, yd = lax.optimization_barrier((g0, t01, t10, t11, f12, f13))[:4]
    t02, t03, t12, t13 = send(ya, 0, 2), send(yb, 0, 2), send(yc, 0, 2), send(yd, 0, 2)
    targets = [g0, t01, t02, t03, t10, t11, t12, t13]
    f12, f13 = lax.optimization_barrier((f12, f13, t01, t10, t11))[:2]
    pieces = [m0, f01, f02, f03, f10, f11, f12, f13]
    normed, qkv, attn_a = forward(t_arr, pieces, wc_own, wc_peer, idk, idq)
    other_a = send(attn_a, 0, 2)
    attn_b = last_window(after(qkv, t02, t03, t12, t13), idk, idq)
    other_b = send(attn_b, 0, 2)
    attn, attn_other = (attn_a, attn_b), (other_a, other_b)
    w2 = after(w2, attn_b)
    w_3 = send(w2, 0, 1)
    pc, pb = clip_proj([w_proj, w1, w2, w_3], proj_clip)
    normed_t, attn_t = turn(normed, attn)

    m00, m01, m10, m11, err = output(t_arr, pieces, targets, attn, attn_other, pc, idk)
    m01 = send(m01, 0, 1)
    m10 = send(m10, 1, 0)
    m11 = send(m11, 1, 1)

    grads, proj = backward(err, pc, attn_t, qkv, w_proj, w1, pb, idk, idq)
    proj_peer = send(proj, 0, 1)
    grads = after(grads, m01, m10, m11)
    own, peer = qkv_sums(grads, normed_t, w3, w3_peer, b_own, b_peer)
    proj = proj + proj_peer
    proj_other = send(proj, 0, 2)
    peer = send(peer, 0, 1)
    sums = jnp.concatenate([own + peer, proj + proj_other], axis=0)
    sums = jnp.sum(lax.all_gather(sums, "lat", axis=0), axis=0)
    mixed = join(place, [m00, m10, m01, m11], rows, lon, lev)
    qkv_sum = jnp.transpose(sums[:6].reshape(3, 2, width), (1, 0, 2))
    proj_sum = sums[6:].reshape(2, 4 * width)
    return (mixed, qkv_sum, proj_sum)


def solution(mesh):
    placed = (
        P(None, None, "lat", "tp"),
        P(None, None, "lat", "tp"),
        P(None, None, "tp"),
        P("tp", None),
        P(None, None, "tp"),
        P(),
        P(),
        P(),
    )
    return jax.shard_map(
        local,
        mesh=mesh,
        in_specs=placed,
        out_specs=(P(None, None, "lat", "tp"), P(None, None, "tp"), P()),
        check_vma=False,
    )
```

```python
import jax
import jax.numpy as jnp
from jax import lax
from jax.experimental import pallas as pl
from jax.experimental.pallas import tpu as pltpu
from jax.sharding import PartitionSpec as P

HD = 64
WLAT = 6
EPS = 1e-05
NEG = -1e30
F32 = jnp.float32
BF = jnp.bfloat16
SCALE = HD ** (-0.5)
NT = (((1,), (1,)), ((), ()))
TN = (((0,), (0,)), ((), ()))


def spec(n):
    return [pl.BlockSpec(memory_space=pltpu.VMEM)] * n


def params(mib):
    return pltpu.CompilerParams(vmem_limit_bytes=mib * 1024 * 1024)


def bounds_of(weight, logits_hi, logits_lo):
    top = jnp.max(weight, axis=0, keepdims=True)
    low = jnp.min(weight, axis=0, keepdims=True)
    hi = 1.0 / (1.0 + jnp.exp(-logits_hi))
    lo = 1.0 / (1.0 + jnp.exp(-logits_lo))
    return hi * top, lo * low, hi * (1.0 - hi) * top, lo * (1.0 - lo) * low


def clip_qkv_kernel(w_ref, c_ref, wc_ref, b_ref):
    def body(i, carry):
        w = w_ref[i].astype(F32)
        up, lw, fh, fl = bounds_of(w, c_ref[i, 0:1], c_ref[i, 1:2])
        wc_ref[i] = jnp.minimum(jnp.maximum(w, lw), up).astype(BF)
        b_ref[i, 0:1] = up
        b_ref[i, 1:2] = lw
        b_ref[i, 2:3] = fh
        b_ref[i, 3:4] = fl
        return carry

    lax.fori_loop(0, 3, body, 0)


def clip_qkv(w, clips):
    n, d, e = w.shape
    return pl.pallas_call(
        clip_qkv_kernel,
        out_shape=(
            jax.ShapeDtypeStruct((n, d, e), BF),
            jax.ShapeDtypeStruct((n, 8, e), F32),
        ),
        in_specs=spec(2),
        out_specs=tuple(spec(2)),
        compiler_params=params(24),
        cost_estimate=pl.CostEstimate(flops=10 * n * d * e, bytes_accessed=4 * n * d * e, transcendentals=0),
    )(w, clips)


def clip_proj_kernel(w0, w1, w2, w3, c_ref, wc_ref, b_ref):
    shards = (w0, w1, w2, w3)
    size = w0.shape[0]

    def body(i, carry):
        cols = pl.ds(pl.multiple_of(i * 256, 256), 256)
        w = jnp.concatenate([s[:, cols].astype(F32) for s in shards], axis=0)
        up, lw, fh, fl = bounds_of(w, c_ref[0:1, cols], c_ref[1:2, cols])
        wc = jnp.minimum(jnp.maximum(w, lw), up).astype(BF)
        wc_ref[:, cols] = wc
        b_ref[0:1, cols] = up
        b_ref[1:2, cols] = lw
        b_ref[2:3, cols] = fh
        b_ref[3:4, cols] = fl
        return carry

    lax.fori_loop(0, w0.shape[1] // 256, body, 0)


def clip_proj(shards, clips):
    e, d = shards[0].shape
    return pl.pallas_call(
        clip_proj_kernel,
        out_shape=(
            jax.ShapeDtypeStruct((4 * e, d), BF),
            jax.ShapeDtypeStruct((8, d), F32),
        ),
        in_specs=spec(5),
        out_specs=tuple(spec(2)),
        compiler_params=params(24),
        cost_estimate=pl.CostEstimate(flops=40 * e * d, bytes_accessed=16 * e * d, transcendentals=0),
    )(*shards, clips)


def stacked(block, mask_a, mask_b):
    return jnp.concatenate([block * mask_a, block * mask_b], axis=0)


def head_masks():
    lane = lax.broadcasted_iota(jnp.int32, (1, 2 * HD), 1)
    mask_a = jnp.where(lane < HD, 1.0, 0.0).astype(BF)
    mask_b = jnp.where(lane < HD, 0.0, 1.0).astype(BF)
    return mask_a, mask_b


def probs_t(k, q2, allowed):
    st = lax.dot_general(k, q2, NT, preferred_element_type=F32) * SCALE
    st = jnp.where(allowed, st, NEG)
    e = jnp.exp(st - jnp.max(st, axis=0, keepdims=True))
    return e * (1.0 / jnp.sum(e, axis=0, keepdims=True))


def merge_heads(t_block):
    both = t_block.T
    n = both.shape[0] // 2
    lane = lax.broadcasted_iota(jnp.int32, (n, 2 * HD), 1)
    return jnp.where(lane < HD, both[:n], both[n:])


def allowed_t(idk_ref, idq_ref, w, cells):
    rows = pl.ds(pl.multiple_of(w * cells, 16), cells)
    idk = idk_ref[rows, :]
    return (idk == idq_ref[w]) & (idk >= 0)


def forward_kernel(t_ref, *refs):
    pieces = refs[:8]
    wo_ref, wp_ref, idk_ref, idq_ref, normed_ref, qkv_ref, attn_ref, xs = refs[8:]
    t = t_ref[0]
    half = pieces[0].shape[0] // 4
    cells = 2 * half
    width = pieces[0].shape[1]
    for k in range(4):
        cols = pl.ds(pl.multiple_of((t ^ k) * width, width), width)
        for s in range(2):
            for p in range(2):
                block = pieces[4 * s + k][cells * p : cells * (p + 1), :].astype(F32)
                for i in range(2):
                    first = cells * (2 * p + i) + half * s
                    xs[first : first + half, cols] = block[half * i : half * (i + 1)]

    def norm(w, carry):
        rows = pl.ds(pl.multiple_of(w * 48, 16), 48)
        x = xs[rows, :]
        mean = jnp.mean(x, axis=-1, keepdims=True)
        x = x - mean
        var = jnp.mean(x * x, axis=-1, keepdims=True)
        normed_ref[rows, :] = (x * lax.rsqrt(var + EPS)).astype(BF)
        return carry

    lax.fori_loop(0, 12, norm, 0)

    def project(i, carry):
        for g, w_ref in enumerate((wo_ref, wp_ref)):
            qkv_ref[3 * g + i] = jnp.dot(
                normed_ref[...], w_ref[i], preferred_element_type=F32
            ).astype(BF)
        return carry

    lax.fori_loop(0, 3, project, 0)
    attend(qkv_ref, idk_ref, idq_ref, attn_ref, 0, 3)


def attend(qkv_ref, idk_ref, idq_ref, attn_ref, first, last):
    mask_a, mask_b = head_masks()
    cells = idk_ref.shape[0] // 4

    def window(w, carry):
        rows = pl.ds(pl.multiple_of(w * cells, 16), cells)
        to = pl.ds(pl.multiple_of((w - first) * cells, 16), cells)
        allowed = allowed_t(idk_ref, idq_ref, w, cells)
        for hp in range(4):
            g, lanes = hp // 2, slice(128 * (hp % 2), 128 * (hp % 2) + 128)
            q2 = stacked(qkv_ref[3 * g, rows, lanes], mask_a, mask_b)
            pt = probs_t(qkv_ref[3 * g + 1, rows, lanes], q2, allowed)
            ot = lax.dot_general(
                qkv_ref[3 * g + 2, rows, lanes], pt.astype(BF), TN, preferred_element_type=F32
            )
            attn_ref[to, 128 * hp : 128 * hp + 128] = merge_heads(ot).astype(BF)
        return carry

    lax.fori_loop(first, last, window, 0)


def last_kernel(qkv_ref, idk_ref, idq_ref, attn_ref):
    attend(qkv_ref, idk_ref, idq_ref, attn_ref, 3, 4)


def last_window(qkv, idk, idq):
    n, width = qkv.shape[1:]
    return pl.pallas_call(
        last_kernel,
        out_shape=jax.ShapeDtypeStruct((n // 4, 2 * width), BF),
        in_specs=spec(3),
        out_specs=spec(1)[0],
        compiler_params=params(16),
        cost_estimate=pl.CostEstimate(flops=10**9, bytes_accessed=2 * 10**6, transcendentals=10**6),
    )(qkv, idk, idq)


def forward(t, pieces, wo, wp, idk, idq):
    n, width = pieces[0].shape
    d = 4 * width
    return pl.pallas_call(
        forward_kernel,
        out_shape=(
            jax.ShapeDtypeStruct((2 * n, d), BF),
            jax.ShapeDtypeStruct((6, 2 * n, width), BF),
            jax.ShapeDtypeStruct((2 * n // 4 * 3, 2 * width), BF),
        ),
        in_specs=[pl.BlockSpec(memory_space=pltpu.SMEM)] + spec(12),
        out_specs=tuple(spec(3)),
        scratch_shapes=[pltpu.VMEM((2 * n, d), F32)],
        compiler_params=params(24),
        cost_estimate=pl.CostEstimate(flops=8 * 10**9, bytes_accessed=10 * 10**6, transcendentals=10**6),
    )(t, *pieces, wo, wp, idk, idq)


def turn_kernel(normed_ref, a_ref, b_ref, normed_t, attn_t):
    d = normed_ref.shape[1]

    def body(i, carry):
        cols = pl.ds(pl.multiple_of(i * 256, 256), 256)
        normed_t[cols, :] = normed_ref[:, cols].T
        return carry

    lax.fori_loop(0, d // 256, body, 0)

    def body2(i, carry):
        cols = pl.ds(pl.multiple_of(i * 256, 256), 256)
        attn_t[cols, :] = jnp.concatenate([a_ref[:, cols], b_ref[:, cols]], axis=0).T
        return carry

    lax.fori_loop(0, a_ref.shape[1] // 256, body2, 0)


def turn(normed, attn):
    n, d = normed.shape
    e = attn[0].shape[1]
    return pl.pallas_call(
        turn_kernel,
        out_shape=(jax.ShapeDtypeStruct((d, n), BF), jax.ShapeDtypeStruct((e, n), BF)),
        in_specs=spec(3),
        out_specs=tuple(spec(2)),
        compiler_params=params(16),
        cost_estimate=pl.CostEstimate(flops=10**9, bytes_accessed=4 * n * (d + e), transcendentals=0),
    )(normed, *attn)


def output_kernel(t_ref, *refs):
    pieces, targets = refs[:8], refs[8:16]
    attns, wc_ref, idk_ref = refs[16:20], refs[20], refs[21]
    mixed, err_ref, y_ref = refs[22:26], refs[26], refs[27]
    t = t_ref[0]
    half = pieces[0].shape[0] // 4
    cells = 2 * half
    width = pieces[0].shape[1]
    e = attns[0].shape[1]
    for k in range(4):
        cols = pl.ds(pl.multiple_of((t ^ k) * width, width), width)
        own = jnp.concatenate([attns[0][...], attns[1][...]], axis=0)
        other = jnp.concatenate([attns[2][...], attns[3][...]], axis=0)
        y_ref[...] = jnp.dot(own, wc_ref[:e, cols], preferred_element_type=F32) + jnp.dot(
            other, wc_ref[e:, cols], preferred_element_type=F32
        )
        for p in range(2):
            errs = [[None, None], [None, None]]
            for s in range(2):
                block = pieces[4 * s + k][cells * p : cells * (p + 1), :].astype(F32)
                wanted = targets[4 * s + k][cells * p : cells * (p + 1), :].astype(F32)
                ys = []
                for i in range(2):
                    first = cells * (2 * p + i) + half * s
                    part = slice(half * i, half * (i + 1))
                    y = block[part] + y_ref[first : first + half, :]
                    ys.append(y)
                    valid = idk_ref[first : first + half, :] >= 0
                    errs[i][s] = jnp.where(valid, y - wanted[part], 0.0)
                if k < 2:
                    mixed[2 * s + k][cells * p : cells * (p + 1), :] = jnp.concatenate(
                        ys, axis=0
                    ).astype(BF)
            for i in range(2):
                first = cells * (2 * p + i)
                err_ref[first : first + cells, cols] = jnp.concatenate(errs[i], axis=0).astype(BF)


def output(t, pieces, targets, own, other, wc, idk):
    n, width = pieces[0].shape
    d = 4 * width
    piece = jax.ShapeDtypeStruct((n, width), BF)
    return pl.pallas_call(
        output_kernel,
        out_shape=(piece, piece, piece, piece, jax.ShapeDtypeStruct((2 * n, d), BF)),
        in_specs=[pl.BlockSpec(memory_space=pltpu.SMEM)] + spec(22),
        out_specs=tuple(spec(5)),
        scratch_shapes=[pltpu.VMEM((2 * n, width), F32)],
        compiler_params=params(24),
        cost_estimate=pl.CostEstimate(flops=2 * 10**9, bytes_accessed=8 * 10**6, transcendentals=0),
    )(t, *pieces, *targets, *own, *other, wc, idk)


def masked_sums(grad, w, bounds):
    g_hi = jnp.sum(jnp.where(w > bounds[0:1], grad, 0.0), axis=0, keepdims=True) * bounds[2:3]
    g_lo = jnp.sum(jnp.where(w < bounds[1:2], grad, 0.0), axis=0, keepdims=True) * bounds[3:4]
    return g_hi, g_lo


def backward_kernel(
    err_ref, wc_ref, attn_t, qkv_ref, po_ref, pp_ref, pb_ref, idk_ref, idq_ref, g_ref, proj_ref, d_ref
):
    e = attn_t.shape[0]
    cells = idk_ref.shape[0] // 4
    d_ref[...] = lax.dot_general(err_ref[...], wc_ref[:e], NT, preferred_element_type=F32).astype(BF)
    mask_a, mask_b = head_masks()

    def window(w, carry):
        rows = pl.ds(pl.multiple_of(w * cells, 16), cells)
        allowed = allowed_t(idk_ref, idq_ref, w, cells)
        for hp in range(4):
            g, lanes = hp // 2, slice(128 * (hp % 2), 128 * (hp % 2) + 128)
            q2 = stacked(qkv_ref[3 * g, rows, lanes], mask_a, mask_b)
            k = qkv_ref[3 * g + 1, rows, lanes]
            v = qkv_ref[3 * g + 2, rows, lanes]
            pt = probs_t(k, q2, allowed)
            d2 = stacked(d_ref[rows, 128 * hp : 128 * hp + 128], mask_a, mask_b)
            g_ref[3 * g + 2, rows, lanes] = jnp.dot(
                pt.astype(BF), d2, preferred_element_type=F32
            ).astype(BF)
            dpt = lax.dot_general(v, d2, NT, preferred_element_type=F32)
            gst = (pt * (dpt - jnp.sum(pt * dpt, axis=0, keepdims=True))).astype(BF)
            g_ref[3 * g + 1, rows, lanes] = (
                jnp.dot(gst, q2, preferred_element_type=F32) * SCALE
            ).astype(BF)
            gqt = lax.dot_general(k, gst, TN, preferred_element_type=F32) * SCALE
            g_ref[3 * g, rows, lanes] = merge_heads(gqt).astype(BF)
        return carry

    lax.fori_loop(0, 4, window, 0)

    def proj_part(i, carry):
        cols = pl.ds(pl.multiple_of(i * 256, 256), 256)
        grad = jnp.dot(attn_t[...], err_ref[:, cols], preferred_element_type=F32)
        n = po_ref.shape[0]
        b = pb_ref[:, cols]
        h0, l0 = masked_sums(grad[:n], po_ref[:, cols].astype(F32), b)
        h1, l1 = masked_sums(grad[n:], pp_ref[:, cols].astype(F32), b)
        proj_ref[pl.ds(i, 1), :] = h0 + h1
        proj_ref[pl.ds(4 + i, 1), :] = l0 + l1
        return carry

    lax.fori_loop(0, err_ref.shape[1] // 256, proj_part, 0)


def backward(err, wc, attn_t, qkv, po, pp, pb, idk, idq):
    n, width = qkv.shape[1:]
    return pl.pallas_call(
        backward_kernel,
        out_shape=(jax.ShapeDtypeStruct((6, n, width), BF), jax.ShapeDtypeStruct((8, width), F32)),
        in_specs=spec(9),
        out_specs=tuple(spec(2)),
        scratch_shapes=[pltpu.VMEM((n, attn_t.shape[0]), BF)],
        compiler_params=params(20),
        cost_estimate=pl.CostEstimate(flops=8 * 10**9, bytes_accessed=10 * 10**6, transcendentals=10**6),
    )(err, wc, attn_t, qkv, po, pp, pb, idk, idq)


def qkv_sums_kernel(g_ref, normed_t, wo_ref, wp_ref, bo_ref, bp_ref, own_ref, peer_ref):
    def qkv_part(i, carry):
        for g, (w_ref, b_ref, to_ref) in enumerate(
            ((wo_ref, bo_ref, own_ref), (wp_ref, bp_ref, peer_ref))
        ):
            grad = jnp.dot(normed_t[...], g_ref[3 * g + i], preferred_element_type=F32)
            hi, lo = masked_sums(grad, w_ref[i].astype(F32), b_ref[i])
            to_ref[pl.ds(2 * i, 1), :] = hi
            to_ref[pl.ds(2 * i + 1, 1), :] = lo
        return carry

    lax.fori_loop(0, 3, qkv_part, 0)


def qkv_sums(g, normed_t, wo, wp, bo, bp):
    width = g.shape[2]
    return pl.pallas_call(
        qkv_sums_kernel,
        out_shape=(jax.ShapeDtypeStruct((6, width), F32),) * 2,
        in_specs=spec(6),
        out_specs=tuple(spec(2)),
        compiler_params=params(20),
        cost_estimate=pl.CostEstimate(flops=4 * 10**9, bytes_accessed=8 * 10**6, transcendentals=0),
    )(g, normed_t, wo, wp, bo, bp)


def split_kernel(s_ref, x_ref, m0, m1, p0, p1):
    offset, core = s_ref[0], s_ref[1]
    rows, lon, lev, width = x_ref.shape
    many = (rows + WLAT) // 2
    half = lon * lev // 2
    for rel, outs in ((0, (m0, m1)), (1, (p0, p1))):
        base = many * (core ^ rel) - offset

        def body(i, carry):
            parts = [[], []]
            for j in range(4):
                r = base + 4 * i + j
                v = x_ref[jnp.clip(r, 0, rows - 1)].astype(F32).reshape(lon * lev, width)
                v = jnp.where((r >= 0) & (r < rows), v, 0.0)
                parts[0].append(v[half:])
                parts[1].append(v[:half])
            at = pl.ds(pl.multiple_of(4 * half * i, 16), 4 * half)
            for s in range(2):
                outs[s][at, :] = jnp.concatenate(parts[s], axis=0).astype(BF)
            return carry

        lax.fori_loop(0, many // 4, body, 0)


def split(place, block):
    rows, lev, lon, width = block.shape
    block = jnp.transpose(block, (0, 2, 1, 3))
    piece = jax.ShapeDtypeStruct(((rows + WLAT) // 2 * lon * lev // 2, width), BF)
    return pl.pallas_call(
        split_kernel,
        out_shape=(piece,) * 4,
        in_specs=[pl.BlockSpec(memory_space=pltpu.SMEM)] + spec(1),
        out_specs=tuple(spec(4)),
        compiler_params=params(16),
        cost_estimate=pl.CostEstimate(flops=10**6, bytes_accessed=2 * 10**6, transcendentals=0),
    )(place, block)


def join_kernel(s_ref, a0, a1, b0, b1, out_ref, grid_ref):
    offset, core = s_ref[0], s_ref[1]
    rows, lon, lev, width = out_ref.shape
    many = (rows + WLAT) // 2
    half = lon * lev // 2
    for rel, ins in ((0, (a0, a1)), (1, (b0, b1))):
        base = many * (core ^ rel)
        for s in range(2):
            for i in range(many // 4):
                v = ins[s][4 * half * i : 4 * half * (i + 1), :].astype(F32)
                for j in range(4):
                    grid_ref[base + 4 * i + j, half * (1 - s) : half * (2 - s), :] = v[
                        half * j : half * (j + 1)
                    ]

    def body(i, carry):
        for j in range(2):
            r = 2 * i + j
            out_ref[r] = grid_ref[r + offset].reshape(lon, lev, width).astype(BF)
        return carry

    lax.fori_loop(0, rows // 2, body, 0)


def join(place, parts, rows, lon, lev):
    n, width = parts[0].shape
    out = pl.pallas_call(
        join_kernel,
        out_shape=jax.ShapeDtypeStruct((rows, lon, lev, width), BF),
        in_specs=[pl.BlockSpec(memory_space=pltpu.SMEM)] + spec(4),
        out_specs=spec(1)[0],
        scratch_shapes=[pltpu.VMEM((rows + WLAT, lon * lev, width), F32)],
        compiler_params=params(16),
        cost_estimate=pl.CostEstimate(flops=10**6, bytes_accessed=2 * 10**6, transcendentals=0),
    )(place, *parts)
    return jnp.transpose(out, (0, 2, 1, 3))


def send(block, shift, flip):
    count, tp = lax.axis_size("lat"), lax.axis_size("tp")
    route = [
        (u * tp + t, ((u + shift) % count) * tp + (t ^ flip)) for u in range(count) for t in range(tp)
    ]
    return lax.ppermute(block, ("lat", "tp"), route)


def swap(block, other, flip):
    count, tp = lax.axis_size("lat"), lax.axis_size("tp")
    route = [(u * tp + t, (u ^ other) * tp + (t ^ flip)) for u in range(count) for t in range(tp)]
    return lax.ppermute(block, ("lat", "tp"), route)


def lat_sum(block, bit):
    count = lax.axis_size("lat")
    while bit < count:
        if 4 * bit <= count:
            a, b, c = swap(block, bit, 0), swap(block, 2 * bit, 0), swap(block, 3 * bit, 0)
            block = (block + a) + (b + c)
            bit *= 4
        else:
            block = block + swap(block, bit, 0)
            bit *= 2
    return block


def after(block, *others):
    return lax.optimization_barrier((block, *others))[0]


def local(features, target, w_qkv, w_proj, qkv_clip, proj_clip, shift_offset, region_ids):
    rows, lev, lon, width = features.shape
    half = lon // 2
    many = (rows + WLAT) // 2
    sector = lax.axis_index("lat")
    count = lax.axis_size("lat")
    t = lax.axis_index("tp")
    core = t % 2
    offset = shift_offset[0]
    t_arr = jnp.reshape(t, (1,)).astype(jnp.int32)
    place = jnp.stack([offset, core]).astype(jnp.int32)

    share = w_proj.shape[0] // 2
    first = share * (sector % 2)
    slab = send(lax.dynamic_slice_in_dim(w_proj, first, share, 0), 0, 2)

    m0, m1, p0, p1 = split(place, features)
    f02, f03 = send(m0, 0, 2), send(p0, 0, 3)
    f10, f11 = send(m1, -1, 0), send(p1, -1, 1)
    f01 = send(p0, 0, 1)
    f12, f13 = send(f10, 0, 2), send(f11, 0, 2)

    w3 = jnp.transpose(w_qkv, (1, 0, 2))
    c3 = jnp.transpose(qkv_clip, (1, 0, 2))
    w3_peer = send(w3, 0, 1)
    c3_peer = send(c3, 0, 1)
    wc_own, b_own = clip_qkv(w3, c3)
    wc_peer, b_peer = clip_qkv(w3_peer, c3_peer)

    doubled = jnp.concatenate([region_ids, region_ids[:, :, :lon]], 2)
    ids = lax.dynamic_slice_in_dim(doubled, sector * lon + half, lon, 2)
    ids = jnp.pad(ids, ((WLAT, WLAT), (0, 0), (0, 0)), constant_values=-1)
    ids = lax.dynamic_slice_in_dim(ids, WLAT - offset + many * core, many, 0)
    ids = ids.reshape(many // WLAT, WLAT, lev, 2, half).transpose(0, 3, 1, 4, 2)
    ids = ids.reshape(many // WLAT, 1, WLAT * lev * lon)
    idk = ids.reshape(many * lev * lon, 1)
    idq = jnp.concatenate([ids, ids], axis=2)

    g0, g1, q0, q1 = split(place, target)
    more = swap(after(slab, f10, f11), 1, 0)
    w1 = send(after(w_proj, f10, f11), 0, 1)
    g1, q1, q0 = lax.optimization_barrier((g1, q1, q0, f02, f03, f10, f11))[:3]
    t10, t11 = send(g1, -1, 0), send(q1, -1, 1)
    t01 = send(q0, 0, 1)
    ya, yb, yc, yd = lax.optimization_barrier((g0, t01, t10, t11, f12, f13))[:4]
    t02, t03, t12, t13 = send(ya, 0, 2), send(yb, 0, 2), send(yc, 0, 2), send(yd, 0, 2)
    targets = [g0, t01, t02, t03, t10, t11, t12, t13]
    f12, f13 = lax.optimization_barrier((f12, f13, t01, t10, t11))[:2]
    pieces = [m0, f01, f02, f03, f10, f11, f12, f13]
    normed, qkv, attn_a = forward(t_arr, pieces, wc_own, wc_peer, idk, idq)
    other_a = send(attn_a, 0, 2)
    attn_b = last_window(after(qkv, t02, t03, t12, t13), idk, idq)
    other_b = send(attn_b, 0, 2)
    attn, attn_other = (attn_a, attn_b), (other_a, other_b)
    slab, more = lax.optimization_barrier((slab, more, attn_b))[:2]
    w2 = lax.dynamic_slice_in_dim(jnp.concatenate([slab, more, slab], axis=0), first, 2 * share, 0)
    w_3 = send(w2, 0, 1)
    pc, pb = clip_proj([w_proj, w1, w2, w_3], proj_clip)
    normed_t, attn_t = turn(normed, attn)

    m00, m01, m10, m11, err = output(t_arr, pieces, targets, attn, attn_other, pc, idk)
    m01 = send(m01, 0, 1)
    m10 = send(m10, 1, 0)
    m11 = send(m11, 1, 1)

    grads, proj = backward(err, pc, attn_t, qkv, w_proj, w1, pb, idk, idq)
    proj_1, proj_2, proj_3 = send(proj, 0, 1), send(proj, 0, 2), send(proj, 0, 3)
    grads = after(grads, m01, m10, m11)
    own, peer = qkv_sums(grads, normed_t, w3, w3_peer, b_own, b_peer)
    proj = (proj + proj_1) + (proj_2 + proj_3)
    a, b, c = send(peer, 0, 1), swap(jnp.concatenate([own, proj], axis=0), 1, 0), swap(peer, 1, 1)
    sums = jnp.concatenate([(own + a) + (b[:6] + c), proj + b[6:]], axis=0)
    sums = lat_sum(sums, 2)
    mixed = join(place, [m00, m10, m01, m11], rows, lon, lev)
    qkv_sum = jnp.transpose(sums[:6].reshape(3, 2, width), (1, 0, 2))
    proj_sum = sums[6:].reshape(2, 4 * width)
    return (mixed, qkv_sum, proj_sum)


def solution(mesh):
    placed = (
        P(None, None, "lat", "tp"),
        P(None, None, "lat", "tp"),
        P(None, None, "tp"),
        P("tp", None),
        P(None, None, "tp"),
        P(),
        P(),
        P(),
    )
    return jax.shard_map(
        local,
        mesh=mesh,
        in_specs=placed,
        out_specs=(P(None, None, "lat", "tp"), P(None, None, "tp"), P()),
        check_vma=False,
    )
```

```python
import jax
import jax.numpy as jnp
from jax import lax
from jax.experimental import pallas as pl
from jax.experimental.pallas import tpu as pltpu
from jax.sharding import PartitionSpec as P

HD = 64
WLAT = 6
EPS = 1e-05
NEG = -1e30
F32 = jnp.float32
BF = jnp.bfloat16
SCALE = HD ** (-0.5)
NT = (((1,), (1,)), ((), ()))
TN = (((0,), (0,)), ((), ()))


def spec(n):
    return [pl.BlockSpec(memory_space=pltpu.VMEM)] * n


def params(mib):
    return pltpu.CompilerParams(vmem_limit_bytes=mib * 1024 * 1024)


def bounds_of(weight, logits_hi, logits_lo):
    top = jnp.max(weight, axis=0, keepdims=True)
    low = jnp.min(weight, axis=0, keepdims=True)
    hi = 1.0 / (1.0 + jnp.exp(-logits_hi))
    lo = 1.0 / (1.0 + jnp.exp(-logits_lo))
    return hi * top, lo * low, hi * (1.0 - hi) * top, lo * (1.0 - lo) * low


def clip_qkv_kernel(w_ref, c_ref, wc_ref, b_ref):
    def body(i, carry):
        w = w_ref[i].astype(F32)
        up, lw, fh, fl = bounds_of(w, c_ref[i, 0:1], c_ref[i, 1:2])
        wc_ref[i] = jnp.minimum(jnp.maximum(w, lw), up).astype(BF)
        b_ref[i, 0:1] = up
        b_ref[i, 1:2] = lw
        b_ref[i, 2:3] = fh
        b_ref[i, 3:4] = fl
        return carry

    lax.fori_loop(0, 3, body, 0)


def clip_qkv(w, clips):
    n, d, e = w.shape
    return pl.pallas_call(
        clip_qkv_kernel,
        out_shape=(
            jax.ShapeDtypeStruct((n, d, e), BF),
            jax.ShapeDtypeStruct((n, 8, e), F32),
        ),
        in_specs=spec(2),
        out_specs=tuple(spec(2)),
        compiler_params=params(24),
        cost_estimate=pl.CostEstimate(flops=10 * n * d * e, bytes_accessed=4 * n * d * e, transcendentals=0),
    )(w, clips)


def clip_proj_kernel(w0, w1, w2, w3, c_ref, wc_ref, b_ref):
    shards = (w0, w1, w2, w3)
    size = w0.shape[0]

    def body(i, carry):
        cols = pl.ds(pl.multiple_of(i * 256, 256), 256)
        w = jnp.concatenate([s[:, cols].astype(F32) for s in shards], axis=0)
        up, lw, fh, fl = bounds_of(w, c_ref[0:1, cols], c_ref[1:2, cols])
        wc = jnp.minimum(jnp.maximum(w, lw), up).astype(BF)
        wc_ref[:, cols] = wc
        b_ref[0:1, cols] = up
        b_ref[1:2, cols] = lw
        b_ref[2:3, cols] = fh
        b_ref[3:4, cols] = fl
        return carry

    lax.fori_loop(0, w0.shape[1] // 256, body, 0)


def clip_proj(shards, clips):
    e, d = shards[0].shape
    return pl.pallas_call(
        clip_proj_kernel,
        out_shape=(
            jax.ShapeDtypeStruct((4 * e, d), BF),
            jax.ShapeDtypeStruct((8, d), F32),
        ),
        in_specs=spec(5),
        out_specs=tuple(spec(2)),
        compiler_params=params(24),
        cost_estimate=pl.CostEstimate(flops=40 * e * d, bytes_accessed=16 * e * d, transcendentals=0),
    )(*shards, clips)


def stacked(block, mask_a, mask_b):
    return jnp.concatenate([block * mask_a, block * mask_b], axis=0)


def head_masks():
    lane = lax.broadcasted_iota(jnp.int32, (1, 2 * HD), 1)
    mask_a = jnp.where(lane < HD, 1.0, 0.0).astype(BF)
    mask_b = jnp.where(lane < HD, 0.0, 1.0).astype(BF)
    return mask_a, mask_b


def probs_t(k, q2, allowed):
    st = lax.dot_general(k, q2, NT, preferred_element_type=F32) * SCALE
    st = jnp.where(allowed, st, NEG)
    e = jnp.exp(st - jnp.max(st, axis=0, keepdims=True))
    return e * (1.0 / jnp.sum(e, axis=0, keepdims=True))


def merge_heads(t_block):
    both = t_block.T
    n = both.shape[0] // 2
    lane = lax.broadcasted_iota(jnp.int32, (n, 2 * HD), 1)
    return jnp.where(lane < HD, both[:n], both[n:])


def allowed_t(idk_ref, idq_ref, w, cells):
    rows = pl.ds(pl.multiple_of(w * cells, 16), cells)
    idk = idk_ref[rows, :]
    return (idk == idq_ref[w]) & (idk >= 0)


def forward_kernel(t_ref, *refs):
    pieces = refs[:4]
    wo_ref, wp_ref, idk_ref, idq_ref, normed_ref, qkv_ref, attn_ref = refs[4:]
    t = t_ref[0]
    n, width = pieces[0].shape
    d = 4 * width

    def norm(w, carry):
        rows = pl.ds(pl.multiple_of(w * 48, 16), 48)
        x = [r[rows, :].astype(F32) for r in pieces]
        mean = sum(jnp.sum(b, axis=-1, keepdims=True) for b in x) / d
        x = [b - mean for b in x]
        var = sum(jnp.sum(b * b, axis=-1, keepdims=True) for b in x) / d
        scale = lax.rsqrt(var + EPS)
        for k in range(4):
            cols = pl.ds(pl.multiple_of((t ^ k) * width, width), width)
            normed_ref[rows, cols] = (x[k] * scale).astype(BF)
        return carry

    lax.fori_loop(0, n // 48, norm, 0)

    def project(i, carry):
        for g, w_ref in enumerate((wo_ref, wp_ref)):
            qkv_ref[3 * g + i] = jnp.dot(
                normed_ref[...], w_ref[i], preferred_element_type=F32
            ).astype(BF)
        return carry

    lax.fori_loop(0, 3, project, 0)
    attend(qkv_ref, idk_ref, idq_ref, attn_ref, 0, 3)


def attend(qkv_ref, idk_ref, idq_ref, attn_ref, first, last):
    mask_a, mask_b = head_masks()
    cells = idk_ref.shape[0] // 4

    def window(w, carry):
        rows = pl.ds(pl.multiple_of(w * cells, 16), cells)
        to = pl.ds(pl.multiple_of((w - first) * cells, 16), cells)
        allowed = allowed_t(idk_ref, idq_ref, w, cells)
        for hp in range(4):
            g, lanes = hp // 2, slice(128 * (hp % 2), 128 * (hp % 2) + 128)
            q2 = stacked(qkv_ref[3 * g, rows, lanes], mask_a, mask_b)
            pt = probs_t(qkv_ref[3 * g + 1, rows, lanes], q2, allowed)
            ot = lax.dot_general(
                qkv_ref[3 * g + 2, rows, lanes], pt.astype(BF), TN, preferred_element_type=F32
            )
            attn_ref[to, 128 * hp : 128 * hp + 128] = merge_heads(ot).astype(BF)
        return carry

    lax.fori_loop(first, last, window, 0)


def last_kernel(qkv_ref, idk_ref, idq_ref, attn_ref):
    attend(qkv_ref, idk_ref, idq_ref, attn_ref, 3, 4)


def last_window(qkv, idk, idq):
    n, width = qkv.shape[1:]
    return pl.pallas_call(
        last_kernel,
        out_shape=jax.ShapeDtypeStruct((n // 4, 2 * width), BF),
        in_specs=spec(3),
        out_specs=spec(1)[0],
        compiler_params=params(16),
        cost_estimate=pl.CostEstimate(flops=10**9, bytes_accessed=2 * 10**6, transcendentals=10**6),
    )(qkv, idk, idq)


def forward(t, pieces, wo, wp, idk, idq):
    n, width = pieces[0].shape
    d = 4 * width
    return pl.pallas_call(
        forward_kernel,
        out_shape=(
            jax.ShapeDtypeStruct((n, d), BF),
            jax.ShapeDtypeStruct((6, n, width), BF),
            jax.ShapeDtypeStruct((n // 4 * 3, 2 * width), BF),
        ),
        in_specs=[pl.BlockSpec(memory_space=pltpu.SMEM)] + spec(8),
        out_specs=tuple(spec(3)),
        compiler_params=params(20),
        cost_estimate=pl.CostEstimate(flops=8 * 10**9, bytes_accessed=10 * 10**6, transcendentals=10**6),
    )(t, *pieces, wo, wp, idk, idq)


def turn_kernel(normed_ref, a_ref, b_ref, normed_t, attn_t):
    d = normed_ref.shape[1]

    def body(i, carry):
        cols = pl.ds(pl.multiple_of(i * 256, 256), 256)
        normed_t[cols, :] = normed_ref[:, cols].T
        return carry

    lax.fori_loop(0, d // 256, body, 0)

    def body2(i, carry):
        cols = pl.ds(pl.multiple_of(i * 256, 256), 256)
        attn_t[cols, :] = jnp.concatenate([a_ref[:, cols], b_ref[:, cols]], axis=0).T
        return carry

    lax.fori_loop(0, a_ref.shape[1] // 256, body2, 0)


def turn(normed, attn):
    n, d = normed.shape
    e = attn[0].shape[1]
    return pl.pallas_call(
        turn_kernel,
        out_shape=(jax.ShapeDtypeStruct((d, n), BF), jax.ShapeDtypeStruct((e, n), BF)),
        in_specs=spec(3),
        out_specs=tuple(spec(2)),
        compiler_params=params(16),
        cost_estimate=pl.CostEstimate(flops=1, bytes_accessed=1, transcendentals=0),
    )(normed, *attn)


def output_kernel(t_ref, *refs):
    pieces, targets = refs[:4], refs[4:8]
    a0, a1, b0, b1, wc_ref, idk_ref = refs[8:14]
    mixed, err_ref, y_ref = refs[14:18], refs[18], refs[19]
    t = t_ref[0]
    n, width = pieces[0].shape
    cells = n // 4
    half = cells // 2
    e = a0.shape[1]
    valid = idk_ref[...] >= 0
    for k in range(4):
        x_ref, want_ref = pieces[k], targets[k]
        cols = pl.ds(pl.multiple_of((t ^ k) * width, width), width)
        own = jnp.concatenate([a0[...], a1[...]], axis=0)
        other = jnp.concatenate([b0[...], b1[...]], axis=0)
        y_ref[...] = jnp.dot(own, wc_ref[:e, cols], preferred_element_type=F32) + jnp.dot(
            other, wc_ref[e:, cols], preferred_element_type=F32
        )
        for p in range(2):
            ys = []
            for i in range(2):
                rows = slice(cells * (2 * p + i), cells * (2 * p + i + 1))
                y = x_ref[rows, :].astype(F32) + y_ref[rows, :]
                ys.append(y)
                err = y - want_ref[rows, :].astype(F32)
                err_ref[rows, cols] = jnp.where(valid[rows], err, 0.0).astype(BF)
            if k < 2:
                at = slice(cells * p, cells * (p + 1))
                for s in range(2):
                    part = slice(half * s, half * (s + 1))
                    mixed[2 * s + k][at, :] = jnp.concatenate([y[part] for y in ys], axis=0).astype(BF)


def output(t, pieces, targets, own, other, wc, idk):
    n, width = pieces[0].shape
    piece = jax.ShapeDtypeStruct((n // 2, width), BF)
    return pl.pallas_call(
        output_kernel,
        out_shape=(piece, piece, piece, piece, jax.ShapeDtypeStruct((n, 4 * width), BF)),
        in_specs=[pl.BlockSpec(memory_space=pltpu.SMEM)] + spec(14),
        out_specs=tuple(spec(5)),
        scratch_shapes=[pltpu.VMEM((n, width), F32)],
        compiler_params=params(20),
        cost_estimate=pl.CostEstimate(flops=2 * 10**9, bytes_accessed=8 * 10**6, transcendentals=0),
    )(t, *pieces, *targets, *own, *other, wc, idk)


def masked_sums(grad, w, bounds):
    g_hi = jnp.sum(jnp.where(w > bounds[0:1], grad, 0.0), axis=0, keepdims=True) * bounds[2:3]
    g_lo = jnp.sum(jnp.where(w < bounds[1:2], grad, 0.0), axis=0, keepdims=True) * bounds[3:4]
    return g_hi, g_lo


def proj_sums_kernel(err_ref, attn_t, po_ref, pp_ref, pb_ref, proj_ref):
    def proj_part(i, carry):
        cols = pl.ds(pl.multiple_of(i * 256, 256), 256)
        grad = jnp.dot(attn_t[...], err_ref[:, cols], preferred_element_type=F32)
        n = po_ref.shape[0]
        b = pb_ref[:, cols]
        h0, l0 = masked_sums(grad[:n], po_ref[:, cols].astype(F32), b)
        h1, l1 = masked_sums(grad[n:], pp_ref[:, cols].astype(F32), b)
        proj_ref[pl.ds(i, 1), :] = h0 + h1
        proj_ref[pl.ds(4 + i, 1), :] = l0 + l1
        return carry

    lax.fori_loop(0, 4, proj_part, 0)


def proj_sums(err, attn_t, po, pp, pb):
    return pl.pallas_call(
        proj_sums_kernel,
        out_shape=jax.ShapeDtypeStruct((8, 256), F32),
        in_specs=spec(5),
        out_specs=spec(1)[0],
        compiler_params=params(16),
        cost_estimate=pl.CostEstimate(flops=10**9, bytes_accessed=3 * 10**6, transcendentals=0),
    )(err, attn_t, po, pp, pb)


def backward_kernel(err_ref, wc_ref, qkv_ref, idk_ref, idq_ref, g_ref, d_ref):
    e = d_ref.shape[1]
    cells = idk_ref.shape[0] // 4
    d_ref[...] = lax.dot_general(err_ref[...], wc_ref[:e], NT, preferred_element_type=F32).astype(BF)
    mask_a, mask_b = head_masks()

    def window(w, carry):
        rows = pl.ds(pl.multiple_of(w * cells, 16), cells)
        allowed = allowed_t(idk_ref, idq_ref, w, cells)
        for hp in range(4):
            g, lanes = hp // 2, slice(128 * (hp % 2), 128 * (hp % 2) + 128)
            q2 = stacked(qkv_ref[3 * g, rows, lanes], mask_a, mask_b)
            k = qkv_ref[3 * g + 1, rows, lanes]
            v = qkv_ref[3 * g + 2, rows, lanes]
            pt = probs_t(k, q2, allowed)
            d2 = stacked(d_ref[rows, 128 * hp : 128 * hp + 128], mask_a, mask_b)
            g_ref[3 * g + 2, rows, lanes] = jnp.dot(
                pt.astype(BF), d2, preferred_element_type=F32
            ).astype(BF)
            dpt = lax.dot_general(v, d2, NT, preferred_element_type=F32)
            gst = (pt * (dpt - jnp.sum(pt * dpt, axis=0, keepdims=True))).astype(BF)
            g_ref[3 * g + 1, rows, lanes] = (
                jnp.dot(gst, q2, preferred_element_type=F32) * SCALE
            ).astype(BF)
            gqt = lax.dot_general(k, gst, TN, preferred_element_type=F32) * SCALE
            g_ref[3 * g, rows, lanes] = merge_heads(gqt).astype(BF)
        return carry

    lax.fori_loop(0, 4, window, 0)


def backward(err, wc, qkv, idk, idq):
    n, width = qkv.shape[1:]
    return pl.pallas_call(
        backward_kernel,
        out_shape=jax.ShapeDtypeStruct((6, n, width), BF),
        in_specs=spec(5),
        out_specs=spec(1)[0],
        scratch_shapes=[pltpu.VMEM((n, 2 * width), BF)],
        compiler_params=params(20),
        cost_estimate=pl.CostEstimate(flops=8 * 10**9, bytes_accessed=10 * 10**6, transcendentals=10**6),
    )(err, wc, qkv, idk, idq)


def qkv_sums_kernel(g_ref, normed_t, wo_ref, wp_ref, bo_ref, bp_ref, own_ref, peer_ref):
    def qkv_part(i, carry):
        for g, (w_ref, b_ref, to_ref) in enumerate(
            ((wo_ref, bo_ref, own_ref), (wp_ref, bp_ref, peer_ref))
        ):
            grad = jnp.dot(normed_t[...], g_ref[3 * g + i], preferred_element_type=F32)
            hi, lo = masked_sums(grad, w_ref[i].astype(F32), b_ref[i])
            to_ref[pl.ds(2 * i, 1), :] = hi
            to_ref[pl.ds(2 * i + 1, 1), :] = lo
        return carry

    lax.fori_loop(0, 3, qkv_part, 0)


def qkv_sums(g, normed_t, wo, wp, bo, bp):
    width = g.shape[2]
    return pl.pallas_call(
        qkv_sums_kernel,
        out_shape=(jax.ShapeDtypeStruct((6, width), F32),) * 2,
        in_specs=spec(6),
        out_specs=tuple(spec(2)),
        compiler_params=params(20),
        cost_estimate=pl.CostEstimate(flops=4 * 10**9, bytes_accessed=8 * 10**6, transcendentals=0),
    )(g, normed_t, wo, wp, bo, bp)


def split_kernel(s_ref, up_ref, low_ref, mine_ref, peer_ref):
    offset, core = s_ref[0], s_ref[1]
    rows, lon, lev, width = up_ref.shape
    many = (rows + WLAT) // 2
    half = lon * lev
    cells = 2 * WLAT * half
    for rel, out_ref in ((0, mine_ref), (1, peer_ref)):
        base = many * (core ^ rel) - offset

        def body(w, carry):
            parts = []
            for ref in (up_ref, low_ref):
                for j in range(WLAT):
                    r = base + WLAT * w + j
                    v = ref[jnp.clip(r, 0, rows - 1)].astype(F32).reshape(half, width)
                    parts.append(jnp.where((r >= 0) & (r < rows), v, 0.0))
            at = pl.ds(pl.multiple_of(w * cells, 16), cells)
            out_ref[at, :] = jnp.concatenate(parts, axis=0).astype(BF)
            return carry

        lax.fori_loop(0, many // WLAT, body, 0)


def split(place, upper, lower):
    rows, lon, lev, width = upper.shape
    piece = jax.ShapeDtypeStruct(((rows + WLAT) * lon * lev, width), BF)
    return pl.pallas_call(
        split_kernel,
        out_shape=(piece, piece),
        in_specs=[pl.BlockSpec(memory_space=pltpu.SMEM)] + spec(2),
        out_specs=tuple(spec(2)),
        compiler_params=params(16),
        cost_estimate=pl.CostEstimate(flops=10**6, bytes_accessed=2 * 10**6, transcendentals=0),
    )(place, upper, lower)


def cell_at(c, window):
    cells = 2 * WLAT * window
    w = sum((c >= i * cells).astype(jnp.int32) for i in range(1, 4))
    c = c - w * cells
    s = (c >= WLAT * window).astype(jnp.int32)
    c = c - s * WLAT * window
    r = sum((c >= i * window).astype(jnp.int32) for i in range(1, WLAT))
    c = c - r * window
    return w * WLAT + r, s * (window // 2) + (c >> 1), c & 1


def ids_kernel(s_ref, ids_ref, idk_ref, idq_ref):
    offset, core, sector = s_ref[0], s_ref[1], s_ref[2]
    rows, lev, total = ids_ref.shape
    n = idk_ref.shape[0]
    cells = n // 4
    window = cells // (2 * WLAT)
    many = (rows + WLAT) // 2
    ids = ids_ref[...].astype(F32).reshape(rows * lev, total)

    def find(c):
        r, lon, level = cell_at(c, window)
        r = r + many * core - offset
        lon = lon + sector * window + window // 2
        lon = jnp.where(lon >= total, lon - total, lon)
        valid = (r >= 0) & (r < rows)
        return jnp.where(valid, 2 * r + level, -1), lon, valid

    spot, lon, valid = find(lax.broadcasted_iota(jnp.int32, (n, 1), 0))
    at = lax.broadcasted_iota(jnp.int32, (n, rows * lev), 1) == spot
    found = jnp.dot(jnp.where(at, 1.0, 0.0), ids, preferred_element_type=F32)
    there = lax.broadcasted_iota(jnp.int32, (n, total), 1) == lon
    found = jnp.sum(jnp.where(there, found, 0.0), axis=1, keepdims=True)
    idk_ref[...] = jnp.where(valid, found, -1.0).astype(jnp.int32)
    for w in range(4):
        lane = lax.broadcasted_iota(jnp.int32, (1, 2 * cells), 1)
        spot, lon, valid = find(w * cells + jnp.where(lane >= cells, lane - cells, lane))
        there = lax.broadcasted_iota(jnp.int32, (total, 2 * cells), 0) == lon
        found = jnp.dot(ids, jnp.where(there, 1.0, 0.0), preferred_element_type=F32)
        at = lax.broadcasted_iota(jnp.int32, (rows * lev, 2 * cells), 0) == spot
        found = jnp.sum(jnp.where(at, found, 0.0), axis=0, keepdims=True)
        idq_ref[w] = jnp.where(valid, found, -1.0).astype(jnp.int32)


def window_ids(place, ids, cells):
    return pl.pallas_call(
        ids_kernel,
        out_shape=(
            jax.ShapeDtypeStruct((4 * cells, 1), jnp.int32),
            jax.ShapeDtypeStruct((4, 1, 2 * cells), jnp.int32),
        ),
        in_specs=[pl.BlockSpec(memory_space=pltpu.SMEM)] + spec(1),
        out_specs=tuple(spec(2)),
        compiler_params=params(16),
        cost_estimate=pl.CostEstimate(flops=10**6, bytes_accessed=10**6, transcendentals=0),
    )(place, ids)


def join_kernel(s_ref, a0, a1, b0, b1, out_ref, grid_ref):
    offset, core = s_ref[0], s_ref[1]
    rows, lon, lev, width = out_ref.shape
    many = (rows + WLAT) // 2
    half = lon * lev // 2
    for rel, ins in ((0, (a0, a1)), (1, (b0, b1))):
        base = many * (core ^ rel)
        for s in range(2):
            for i in range(many // 4):
                v = ins[s][4 * half * i : 4 * half * (i + 1), :].astype(F32)
                for j in range(4):
                    grid_ref[base + 4 * i + j, half * (1 - s) : half * (2 - s), :] = v[
                        half * j : half * (j + 1)
                    ]

    def body(i, carry):
        for j in range(2):
            r = 2 * i + j
            out_ref[r] = grid_ref[r + offset].reshape(lon, lev, width).astype(BF)
        return carry

    lax.fori_loop(0, rows // 2, body, 0)


def join(place, parts, rows, lon, lev):
    n, width = parts[0].shape
    out = pl.pallas_call(
        join_kernel,
        out_shape=jax.ShapeDtypeStruct((rows, lon, lev, width), BF),
        in_specs=[pl.BlockSpec(memory_space=pltpu.SMEM)] + spec(4),
        out_specs=spec(1)[0],
        scratch_shapes=[pltpu.VMEM((rows + WLAT, lon * lev, width), F32)],
        compiler_params=params(16),
        cost_estimate=pl.CostEstimate(flops=10**6, bytes_accessed=2 * 10**6, transcendentals=0),
    )(place, *parts)
    return jnp.transpose(out, (0, 2, 1, 3))


def send(block, shift, flip):
    count, tp = lax.axis_size("lat"), lax.axis_size("tp")
    route = [
        (u * tp + t, ((u + shift) % count) * tp + (t ^ flip)) for u in range(count) for t in range(tp)
    ]
    return lax.ppermute(block, ("lat", "tp"), route)


def swap(block, other, flip):
    count, tp = lax.axis_size("lat"), lax.axis_size("tp")
    route = [(u * tp + t, (u ^ other) * tp + (t ^ flip)) for u in range(count) for t in range(tp)]
    return lax.ppermute(block, ("lat", "tp"), route)


def lat_terms(block, bit):
    count = lax.axis_size("lat")
    terms = [block]
    while bit < count:
        block = added(terms)
        terms = [block, swap(block, bit, 0)]
        if 4 * bit <= count:
            terms += [swap(block, 2 * bit, 0), swap(block, 3 * bit, 0)]
        bit *= len(terms)
    return terms


def added(terms):
    while len(terms) > 1:
        terms = [a + b for a, b in zip(terms[::2], terms[1::2])]
    return terms[0]


def last_sum_kernel(*refs):
    qkv_ref, proj_ref = refs[-2:]
    total = added([r[...] for r in refs[:-2]])
    width = total.shape[1]
    for i in range(3):
        qkv_ref[i] = total[2 * i : 2 * i + 2]
    for i in range(4):
        for j in range(2):
            proj_ref[j : j + 1, width * i : width * (i + 1)] = total[6 + 4 * j + i : 7 + 4 * j + i]


def last_sum(terms):
    width = terms[0].shape[1]
    return pl.pallas_call(
        last_sum_kernel,
        out_shape=(jax.ShapeDtypeStruct((3, 2, width), F32), jax.ShapeDtypeStruct((2, 4 * width), F32)),
        in_specs=spec(len(terms)),
        out_specs=tuple(spec(2)),
    )(*terms)


def after(block, *others):
    return lax.optimization_barrier((block, *others))[0]


def local(features, target, w_qkv, w_proj, qkv_clip, proj_clip, shift_offset, region_ids):
    rows, lev, lon, width = features.shape
    half = lon // 2
    sector = lax.axis_index("lat")
    t = lax.axis_index("tp")
    t_arr = jnp.reshape(t, (1,)).astype(jnp.int32)
    place = jnp.stack([shift_offset[0], t % 2, sector]).astype(jnp.int32)

    def halves(block):
        block = jnp.transpose(block, (0, 2, 1, 3))
        return block[:, half:], block[:, :half]

    w3 = jnp.transpose(w_qkv, (1, 0, 2))
    c3 = jnp.transpose(qkv_clip, (1, 0, 2))
    w3_peer = send(w3, 0, 1)
    c3_peer = send(c3, 0, 1)
    w1, w2 = send(w_proj, 0, 1), send(w_proj, 0, 2)
    wc_own, b_own = clip_qkv(w3, c3)
    wc_peer, b_peer = clip_qkv(w3_peer, c3_peer)
    idk, idq = window_ids(place, region_ids, WLAT * lev * lon)

    f_up, f_low = halves(features)
    t_up, t_low = halves(target)
    f_low = send(f_low, -1, 0)
    f_low, t_up, t_low, wc_own, wc_peer, idk, idq = lax.optimization_barrier(
        (f_low, t_up, t_low, wc_own, wc_peer, idk, idq)
    )
    t_low = send(t_low, -1, 0)
    mine, away = split(place, f_up, f_low)
    pieces = [mine, send(away, 0, 1), send(mine, 0, 2), send(away, 0, 3)]

    t_mine, t_away = split(place, t_up, t_low)
    w_3 = send(after(w2, t_mine), 0, 1)
    pc, pb = clip_proj([w_proj, w1, w2, w_3], proj_clip)
    t_mine, t_away, *pieces = lax.optimization_barrier((t_mine, t_away, *pieces, pc))[:-1]
    targets = [t_mine, send(t_away, 0, 1), send(t_mine, 0, 2), send(t_away, 0, 3)]

    normed, qkv, attn_a = forward(t_arr, pieces, wc_own, wc_peer, idk, idq)
    other_a = send(attn_a, 0, 2)
    attn_b = last_window(after(qkv, *targets), idk, idq)
    other_b = send(attn_b, 0, 2)
    normed_t, attn_t = turn(normed, (attn_a, attn_b))

    m00, m01, m10, m11, err = output(
        t_arr, pieces, targets, (attn_a, attn_b), (other_a, other_b), pc, idk
    )
    m01 = send(m01, 0, 1)
    m10 = send(m10, 1, 0)
    m11 = send(m11, 1, 1)

    proj = proj_sums(err, attn_t, w_proj, w1, pb)
    proj_y = send(proj, 0, 2)
    grads = backward(err, pc, qkv, idk, idq)
    grads = after(grads, m01, m10, m11, proj_y)
    own, peer = qkv_sums(grads, normed_t, w3, w3_peer, b_own, b_peer)
    proj = proj + proj_y
    own, peer = jnp.concatenate([own, proj], axis=0), jnp.concatenate([peer, proj], axis=0)
    sums = added([own, send(peer, 0, 1), swap(own, 1, 0), swap(peer, 1, 1)])
    qkv_sum, proj_sum = last_sum(lat_terms(sums, 2))
    mixed = join(place, [m00, m10, m01, m11], rows, lon, lev)
    return (mixed, jnp.transpose(qkv_sum, (1, 0, 2)), proj_sum)


def solution(mesh):
    placed = (
        P(None, None, "lat", "tp"),
        P(None, None, "lat", "tp"),
        P(None, None, "tp"),
        P("tp", None),
        P(None, None, "tp"),
        P(),
        P(),
        P(),
    )
    return jax.shard_map(
        local,
        mesh=mesh,
        in_specs=placed,
        out_specs=(P(None, None, "lat", "tp"), P(None, None, "tp"), P()),
        check_vma=False,
    )
```

```python
import functools

import jax
import jax.numpy as jnp
from jax import lax
from jax.experimental import pallas as pl
from jax.experimental.pallas import tpu as pltpu
from jax.sharding import PartitionSpec as P

HD = 64
WLAT = 6
EPS = 1e-05
NEG = -1e30
F32 = jnp.float32
BF = jnp.bfloat16
SCALE = HD ** (-0.5)
NT = (((1,), (1,)), ((), ()))
TN = (((0,), (0,)), ((), ()))
SMALL = pl.CostEstimate(flops=1, bytes_accessed=1, transcendentals=0)


def spec(n):
    return [pl.BlockSpec(memory_space=pltpu.VMEM)] * n


def params(mib):
    return pltpu.CompilerParams(vmem_limit_bytes=mib * 1024 * 1024)


def bounds_of(weight, logits_hi, logits_lo):
    top = jnp.max(weight, axis=0, keepdims=True)
    low = jnp.min(weight, axis=0, keepdims=True)
    hi = 1.0 / (1.0 + jnp.exp(-logits_hi))
    lo = 1.0 / (1.0 + jnp.exp(-logits_lo))
    return hi * top, lo * low, hi * (1.0 - hi) * top, lo * (1.0 - lo) * low


def clip_qkv_kernel(w_ref, c_ref, wc_ref, b_ref):
    def body(i, carry):
        w = w_ref[i].astype(F32)
        up, lw, fh, fl = bounds_of(w, c_ref[i, 0:1], c_ref[i, 1:2])
        wc_ref[i] = jnp.minimum(jnp.maximum(w, lw), up).astype(BF)
        b_ref[i, 0:1] = up
        b_ref[i, 1:2] = lw
        b_ref[i, 2:3] = fh
        b_ref[i, 3:4] = fl
        return carry

    lax.fori_loop(0, 3, body, 0)


def clip_qkv(w, clips):
    n, d, e = w.shape
    return pl.pallas_call(
        clip_qkv_kernel,
        out_shape=(
            jax.ShapeDtypeStruct((n, d, e), BF),
            jax.ShapeDtypeStruct((n, 8, e), F32),
        ),
        in_specs=spec(2),
        out_specs=tuple(spec(2)),
        compiler_params=params(24),
        cost_estimate=SMALL,
    )(w, clips)


def clip_proj_kernel(w0, w1, w2, w3, c_ref, wc_ref, b_ref):
    shards = (w0, w1, w2, w3)
    size = w0.shape[0]

    def body(i, carry):
        cols = pl.ds(pl.multiple_of(i * 256, 256), 256)
        w = jnp.concatenate([s[:, cols].astype(F32) for s in shards], axis=0)
        up, lw, fh, fl = bounds_of(w, c_ref[0:1, cols], c_ref[1:2, cols])
        wc = jnp.minimum(jnp.maximum(w, lw), up).astype(BF)
        wc_ref[:, cols] = wc
        b_ref[0:1, cols] = up
        b_ref[1:2, cols] = lw
        b_ref[2:3, cols] = fh
        b_ref[3:4, cols] = fl
        return carry

    lax.fori_loop(0, w0.shape[1] // 256, body, 0)


def clip_proj(shards, clips):
    e, d = shards[0].shape
    return pl.pallas_call(
        clip_proj_kernel,
        out_shape=(
            jax.ShapeDtypeStruct((4 * e, d), BF),
            jax.ShapeDtypeStruct((8, d), F32),
        ),
        in_specs=spec(5),
        out_specs=tuple(spec(2)),
        compiler_params=params(24),
        cost_estimate=SMALL,
    )(*shards, clips)


def stacked(block, mask_a, mask_b):
    return jnp.concatenate([block * mask_a, block * mask_b], axis=0)


def head_masks():
    lane = lax.broadcasted_iota(jnp.int32, (1, 2 * HD), 1)
    mask_a = jnp.where(lane < HD, 1.0, 0.0).astype(BF)
    mask_b = jnp.where(lane < HD, 0.0, 1.0).astype(BF)
    return mask_a, mask_b


def probs_t(k, q2, allowed):
    st = lax.dot_general(k, q2, NT, preferred_element_type=F32) * SCALE
    st = jnp.where(allowed, st, NEG)
    e = jnp.exp(st - jnp.max(st, axis=0, keepdims=True))
    return e * (1.0 / jnp.sum(e, axis=0, keepdims=True))


def merge_heads(t_block):
    both = t_block.T
    n = both.shape[0] // 2
    lane = lax.broadcasted_iota(jnp.int32, (n, 2 * HD), 1)
    return jnp.where(lane < HD, both[:n], both[n:])


def allowed_t(idk_ref, idq_ref, w, cells):
    rows = pl.ds(pl.multiple_of(w * cells, 16), cells)
    idk = idk_ref[rows, :]
    return (idk == idq_ref[w]) & (idk >= 0)


def forward_kernel(t_ref, *refs):
    pieces = refs[:4]
    wo_ref, wp_ref, idk_ref, idq_ref, normed_ref, qkv_ref, attn_ref = refs[4:]
    t = t_ref[0]
    n, width = pieces[0].shape
    d = 4 * width

    def norm(w, carry):
        rows = pl.ds(pl.multiple_of(w * 48, 16), 48)
        x = [r[rows, :].astype(F32) for r in pieces]
        mean = sum(jnp.sum(b, axis=-1, keepdims=True) for b in x) / d
        x = [b - mean for b in x]
        var = sum(jnp.sum(b * b, axis=-1, keepdims=True) for b in x) / d
        scale = lax.rsqrt(var + EPS)
        for k in range(4):
            cols = pl.ds(pl.multiple_of((t ^ k) * width, width), width)
            normed_ref[rows, cols] = (x[k] * scale).astype(BF)
        return carry

    lax.fori_loop(0, n // 48, norm, 0)

    def project(i, carry):
        for g, w_ref in enumerate((wo_ref, wp_ref)):
            qkv_ref[3 * g + i] = jnp.dot(
                normed_ref[...], w_ref[i], preferred_element_type=F32
            ).astype(BF)
        return carry

    lax.fori_loop(0, 3, project, 0)
    attend(qkv_ref, idk_ref, idq_ref, attn_ref, 0, 2)


def attend(qkv_ref, idk_ref, idq_ref, attn_ref, first, last):
    mask_a, mask_b = head_masks()
    cells = idk_ref.shape[0] // 4

    def window(w, carry):
        rows = pl.ds(pl.multiple_of(w * cells, 16), cells)
        to = pl.ds(pl.multiple_of((w - first) * cells, 16), cells)
        allowed = allowed_t(idk_ref, idq_ref, w, cells)
        for hp in range(4):
            g, lanes = hp // 2, slice(128 * (hp % 2), 128 * (hp % 2) + 128)
            q2 = stacked(qkv_ref[3 * g, rows, lanes], mask_a, mask_b)
            pt = probs_t(qkv_ref[3 * g + 1, rows, lanes], q2, allowed)
            ot = lax.dot_general(
                qkv_ref[3 * g + 2, rows, lanes], pt.astype(BF), TN, preferred_element_type=F32
            )
            attn_ref[to, 128 * hp : 128 * hp + 128] = merge_heads(ot).astype(BF)
        return carry

    lax.fori_loop(first, last, window, 0)


def last_kernel(qkv_ref, idk_ref, idq_ref, attn_ref):
    attend(qkv_ref, idk_ref, idq_ref, attn_ref, 2, 4)


def last_windows(qkv, idk, idq):
    n, width = qkv.shape[1:]
    return pl.pallas_call(
        last_kernel,
        out_shape=jax.ShapeDtypeStruct((n // 2, 2 * width), BF),
        in_specs=spec(3),
        out_specs=spec(1)[0],
        compiler_params=params(16),
        cost_estimate=pl.CostEstimate(flops=10**9, bytes_accessed=2 * 10**6, transcendentals=10**6),
    )(qkv, idk, idq)


def forward(t, pieces, wo, wp, idk, idq):
    n, width = pieces[0].shape
    d = 4 * width
    return pl.pallas_call(
        forward_kernel,
        out_shape=(
            jax.ShapeDtypeStruct((n, d), BF),
            jax.ShapeDtypeStruct((6, n, width), BF),
            jax.ShapeDtypeStruct((n // 2, 2 * width), BF),
        ),
        in_specs=[pl.BlockSpec(memory_space=pltpu.SMEM)] + spec(8),
        out_specs=tuple(spec(3)),
        compiler_params=params(20),
        cost_estimate=pl.CostEstimate(flops=8 * 10**9, bytes_accessed=10 * 10**6, transcendentals=10**6),
    )(t, *pieces, wo, wp, idk, idq)


def turn_kernel(normed_ref, a_ref, b_ref, normed_t, attn_t):
    d = normed_ref.shape[1]

    def body(i, carry):
        cols = pl.ds(pl.multiple_of(i * 256, 256), 256)
        normed_t[cols, :] = normed_ref[:, cols].T
        return carry

    lax.fori_loop(0, d // 256, body, 0)

    def body2(i, carry):
        cols = pl.ds(pl.multiple_of(i * 256, 256), 256)
        attn_t[cols, :] = jnp.concatenate([a_ref[:, cols], b_ref[:, cols]], axis=0).T
        return carry

    lax.fori_loop(0, a_ref.shape[1] // 256, body2, 0)


def turn(normed, attn):
    n, d = normed.shape
    e = attn[0].shape[1]
    return pl.pallas_call(
        turn_kernel,
        out_shape=(jax.ShapeDtypeStruct((d, n), BF), jax.ShapeDtypeStruct((e, n), BF)),
        in_specs=spec(3),
        out_specs=tuple(spec(2)),
        compiler_params=params(16),
        cost_estimate=SMALL,
    )(normed, *attn)


def output_kernel(group, t_ref, *refs):
    pieces, targets = refs[:4], (refs[4], refs[6].at[0], refs[5], refs[6].at[1])
    own_ref, other_ref, wc_ref, idk_ref = refs[7:11]
    before, refs = refs[11 : 11 + 4 * group], refs[11 + 4 * group :]
    mixed, err_ref, y_ref = refs[:4], refs[4], refs[5]
    t = t_ref[0]
    n, width = pieces[0].shape
    cells = n // 4
    half = cells // 2
    e = own_ref.shape[1]
    for old, new in zip(before, mixed):
        new[: group * cells, :] = old[...]
    for k in range(4):
        x_ref, want_ref = pieces[k], targets[k]
        cols = pl.ds(pl.multiple_of((t ^ k) * width, width), width)
        y_ref[...] = jnp.dot(own_ref[...], wc_ref[:e, cols], preferred_element_type=F32) + jnp.dot(
            other_ref[...], wc_ref[e:, cols], preferred_element_type=F32
        )
        ys = []
        for i in range(2):
            at = slice(cells * i, cells * (i + 1))
            rows = slice(cells * (2 * group + i), cells * (2 * group + i + 1))
            y = x_ref[rows, :].astype(F32) + y_ref[at, :]
            ys.append(y)
            err = y - want_ref[rows, :].astype(F32)
            valid = idk_ref[rows, :] >= 0
            err_ref[at, cols] = jnp.where(valid, err, 0.0).astype(BF)
        if k < 2:
            at = slice(cells * group, cells * (group + 1))
            for s in range(2):
                part = slice(half * s, half * (s + 1))
                mixed[2 * s + k][at, :] = jnp.concatenate([y[part] for y in ys], axis=0).astype(BF)


def output(t, pieces, targets, own, other, wc, idk, before=()):
    n, width = pieces[0].shape
    group = 1 if before else 0
    piece = jax.ShapeDtypeStruct((n // 4 * (1 + group), width), BF)
    return pl.pallas_call(
        functools.partial(output_kernel, group),
        out_shape=(piece, piece, piece, piece, jax.ShapeDtypeStruct((n // 2, 4 * width), BF)),
        in_specs=[pl.BlockSpec(memory_space=pltpu.SMEM)] + spec(11 + len(before)),
        out_specs=tuple(spec(5)),
        scratch_shapes=[pltpu.VMEM((n // 2, width), F32)],
        compiler_params=params(20),
        cost_estimate=pl.CostEstimate(flops=10**9, bytes_accessed=4 * 10**6, transcendentals=0),
    )(t, *pieces, *targets, own, other, wc, idk, *before)


def probs_kernel(group, qkv_ref, idk_ref, idq_ref, p_ref):
    cells = idk_ref.shape[0] // 4
    mask_a, mask_b = head_masks()

    def window(i, carry):
        w = 2 * group + i
        rows = pl.ds(pl.multiple_of(w * cells, 16), cells)
        allowed = allowed_t(idk_ref, idq_ref, w, cells)
        for hp in range(4):
            g, lanes = hp // 2, slice(128 * (hp % 2), 128 * (hp % 2) + 128)
            q2 = stacked(qkv_ref[3 * g, rows, lanes], mask_a, mask_b)
            p_ref[4 * i + hp] = probs_t(qkv_ref[3 * g + 1, rows, lanes], q2, allowed)
        return carry

    lax.fori_loop(0, 2, window, 0)


def probs_of(group, qkv, idk, idq):
    n, width = qkv.shape[1:]
    return pl.pallas_call(
        functools.partial(probs_kernel, group),
        out_shape=jax.ShapeDtypeStruct((8, n // 4, n // 2), F32),
        in_specs=spec(3),
        out_specs=spec(1)[0],
        compiler_params=params(16),
        cost_estimate=SMALL,
    )(qkv, idk, idq)


def masked_sums(grad, w, bounds):
    g_hi = jnp.sum(jnp.where(w > bounds[0:1], grad, 0.0), axis=0, keepdims=True) * bounds[2:3]
    g_lo = jnp.sum(jnp.where(w < bounds[1:2], grad, 0.0), axis=0, keepdims=True) * bounds[3:4]
    return g_hi, g_lo


def proj_sums_kernel(e0_ref, e1_ref, attn_t, po_ref, pp_ref, pb_ref, proj_ref):
    def proj_part(i, carry):
        cols = pl.ds(pl.multiple_of(i * 256, 256), 256)
        err = jnp.concatenate([e0_ref[:, cols], e1_ref[:, cols]], axis=0)
        grad = jnp.dot(attn_t[...], err, preferred_element_type=F32)
        n = po_ref.shape[0]
        b = pb_ref[:, cols]
        h0, l0 = masked_sums(grad[:n], po_ref[:, cols].astype(F32), b)
        h1, l1 = masked_sums(grad[n:], pp_ref[:, cols].astype(F32), b)
        proj_ref[pl.ds(i, 1), :] = h0 + h1
        proj_ref[pl.ds(4 + i, 1), :] = l0 + l1
        return carry

    lax.fori_loop(0, 4, proj_part, 0)


def proj_sums(errs, attn_t, po, pp, pb):
    return pl.pallas_call(
        proj_sums_kernel,
        out_shape=jax.ShapeDtypeStruct((8, 256), F32),
        in_specs=spec(6),
        out_specs=spec(1)[0],
        compiler_params=params(16),
        cost_estimate=pl.CostEstimate(flops=10**9, bytes_accessed=3 * 10**6, transcendentals=0),
    )(*errs, attn_t, po, pp, pb)


def backward_kernel(group, err_ref, wc_ref, qkv_ref, p_ref, g_ref, d_ref):
    e = d_ref.shape[1]
    cells = d_ref.shape[0] // 2
    d_ref[...] = lax.dot_general(err_ref[...], wc_ref[:e], NT, preferred_element_type=F32).astype(BF)
    mask_a, mask_b = head_masks()

    def window(i, carry):
        rows = pl.ds(pl.multiple_of((2 * group + i) * cells, 16), cells)
        at = pl.ds(pl.multiple_of(i * cells, 16), cells)
        for hp in range(4):
            g, lanes = hp // 2, slice(128 * (hp % 2), 128 * (hp % 2) + 128)
            q2 = stacked(qkv_ref[3 * g, rows, lanes], mask_a, mask_b)
            k = qkv_ref[3 * g + 1, rows, lanes]
            v = qkv_ref[3 * g + 2, rows, lanes]
            pt = p_ref[4 * i + hp]
            d2 = stacked(d_ref[at, 128 * hp : 128 * hp + 128], mask_a, mask_b)
            g_ref[3 * g + 2, at, lanes] = jnp.dot(
                pt.astype(BF), d2, preferred_element_type=F32
            ).astype(BF)
            dpt = lax.dot_general(v, d2, NT, preferred_element_type=F32)
            gst = (pt * (dpt - jnp.sum(pt * dpt, axis=0, keepdims=True))).astype(BF)
            g_ref[3 * g + 1, at, lanes] = (
                jnp.dot(gst, q2, preferred_element_type=F32) * SCALE
            ).astype(BF)
            gqt = lax.dot_general(k, gst, TN, preferred_element_type=F32) * SCALE
            g_ref[3 * g, at, lanes] = merge_heads(gqt).astype(BF)
        return carry

    lax.fori_loop(0, 2, window, 0)


def backward(group, err, wc, qkv, probs):
    n, width = qkv.shape[1:]
    return pl.pallas_call(
        functools.partial(backward_kernel, group),
        out_shape=jax.ShapeDtypeStruct((6, n // 2, width), BF),
        in_specs=spec(4),
        out_specs=spec(1)[0],
        scratch_shapes=[pltpu.VMEM((n // 2, 2 * width), BF)],
        compiler_params=params(20),
        cost_estimate=pl.CostEstimate(flops=4 * 10**9, bytes_accessed=5 * 10**6, transcendentals=10**6),
    )(err, wc, qkv, probs)


def qkv_sums_kernel(g0_ref, g1_ref, normed_t, wo_ref, wp_ref, bo_ref, bp_ref, own_ref, peer_ref):
    def qkv_part(i, carry):
        for g, (w_ref, b_ref, to_ref) in enumerate(
            ((wo_ref, bo_ref, own_ref), (wp_ref, bp_ref, peer_ref))
        ):
            cells = jnp.concatenate([g0_ref[3 * g + i], g1_ref[3 * g + i]], axis=0)
            grad = jnp.dot(normed_t[...], cells, preferred_element_type=F32)
            hi, lo = masked_sums(grad, w_ref[i].astype(F32), b_ref[i])
            to_ref[pl.ds(2 * i, 1), :] = hi
            to_ref[pl.ds(2 * i + 1, 1), :] = lo
        return carry

    lax.fori_loop(0, 3, qkv_part, 0)


def qkv_sums(g, normed_t, wo, wp, bo, bp):
    width = g[0].shape[2]
    return pl.pallas_call(
        qkv_sums_kernel,
        out_shape=(jax.ShapeDtypeStruct((6, width), F32),) * 2,
        in_specs=spec(7),
        out_specs=tuple(spec(2)),
        compiler_params=params(20),
        cost_estimate=pl.CostEstimate(flops=4 * 10**9, bytes_accessed=8 * 10**6, transcendentals=0),
    )(*g, normed_t, wo, wp, bo, bp)


def split_kernel(s_ref, *refs):
    offset, core = s_ref[0], s_ref[1]
    pairs = (len(refs) - 1) // 3
    rows, lon, lev, width = refs[1].shape
    many = (rows + WLAT) // 2
    half = lon * lev
    cells = 2 * WLAT * half
    for rel in range(2):
        base = many * (core ^ rel) - offset

        def body(w, carry):
            at = pl.ds(pl.multiple_of(w * cells, 16), cells)
            for i in range(pairs):
                up_ref, low_ref = refs[2 * i : 2 * i + 2]
                parts = []
                for ref, part in ((up_ref, slice(up_ref.shape[1] - lon, up_ref.shape[1])), (low_ref, slice(0, lon))):
                    for j in range(WLAT):
                        r = base + WLAT * w + j
                        v = ref[jnp.clip(r, 0, rows - 1), part].astype(F32).reshape(half, width)
                        parts.append(jnp.where((r >= 0) & (r < rows), v, 0.0))
                block = jnp.concatenate(parts, axis=0).astype(BF)
                if rel:
                    refs[-1][i, at, :] = block
                else:
                    refs[2 * pairs + i][at, :] = block
            return carry

        lax.fori_loop(0, many // WLAT, body, 0)


def split(place, *halves):
    rows, lon, lev, width = halves[1].shape
    pairs = len(halves) // 2
    n = (rows + WLAT) * lon * lev
    return pl.pallas_call(
        split_kernel,
        out_shape=(jax.ShapeDtypeStruct((n, width), BF),) * pairs
        + (jax.ShapeDtypeStruct((pairs, n, width), BF),),
        in_specs=[pl.BlockSpec(memory_space=pltpu.SMEM)] + spec(2 * pairs),
        out_specs=tuple(spec(pairs + 1)),
        compiler_params=params(16),
        cost_estimate=SMALL,
    )(place, *halves)


def cell_at(c, window):
    cells = 2 * WLAT * window
    w = sum((c >= i * cells).astype(jnp.int32) for i in range(1, 4))
    c = c - w * cells
    s = (c >= WLAT * window).astype(jnp.int32)
    c = c - s * WLAT * window
    r = sum((c >= i * window).astype(jnp.int32) for i in range(1, WLAT))
    c = c - r * window
    return w * WLAT + r, s * (window // 2) + (c >> 1), c & 1


def ids_kernel(s_ref, ids_ref, idk_ref, idq_ref):
    offset, core, sector = s_ref[0], s_ref[1], s_ref[2]
    rows, lev, total = ids_ref.shape
    n = idk_ref.shape[0]
    cells = n // 4
    window = cells // (2 * WLAT)
    many = (rows + WLAT) // 2
    ids = ids_ref[...].astype(F32).reshape(rows * lev, total)

    def find(c):
        r, lon, level = cell_at(c, window)
        r = r + many * core - offset
        lon = lon + sector * window + window // 2
        lon = jnp.where(lon >= total, lon - total, lon)
        valid = (r >= 0) & (r < rows)
        return jnp.where(valid, 2 * r + level, -1), lon, valid

    spot, lon, valid = find(lax.broadcasted_iota(jnp.int32, (n, 1), 0))
    at = lax.broadcasted_iota(jnp.int32, (n, rows * lev), 1) == spot
    found = jnp.dot(jnp.where(at, 1.0, 0.0), ids, preferred_element_type=F32)
    there = lax.broadcasted_iota(jnp.int32, (n, total), 1) == lon
    found = jnp.sum(jnp.where(there, found, 0.0), axis=1, keepdims=True)
    idk_ref[...] = jnp.where(valid, found, -1.0).astype(jnp.int32)
    for w in range(4):
        lane = lax.broadcasted_iota(jnp.int32, (1, 2 * cells), 1)
        spot, lon, valid = find(w * cells + jnp.where(lane >= cells, lane - cells, lane))
        there = lax.broadcasted_iota(jnp.int32, (total, 2 * cells), 0) == lon
        found = jnp.dot(ids, jnp.where(there, 1.0, 0.0), preferred_element_type=F32)
        at = lax.broadcasted_iota(jnp.int32, (rows * lev, 2 * cells), 0) == spot
        found = jnp.sum(jnp.where(at, found, 0.0), axis=0, keepdims=True)
        idq_ref[w] = jnp.where(valid, found, -1.0).astype(jnp.int32)


def window_ids(place, ids, cells):
    return pl.pallas_call(
        ids_kernel,
        out_shape=(
            jax.ShapeDtypeStruct((4 * cells, 1), jnp.int32),
            jax.ShapeDtypeStruct((4, 1, 2 * cells), jnp.int32),
        ),
        in_specs=[pl.BlockSpec(memory_space=pltpu.SMEM)] + spec(1),
        out_specs=tuple(spec(2)),
        compiler_params=params(16),
        cost_estimate=SMALL,
    )(place, ids)


def join_kernel(s_ref, a0, a1, b0, b1, out_ref, grid_ref):
    offset, core = s_ref[0], s_ref[1]
    rows, lon, lev, width = out_ref.shape
    many = (rows + WLAT) // 2
    half = lon * lev // 2
    for rel, ins in ((0, (a0, a1)), (1, (b0, b1))):
        base = many * (core ^ rel)
        for s in range(2):
            for i in range(many // 4):
                v = ins[s][4 * half * i : 4 * half * (i + 1), :].astype(F32)
                for j in range(4):
                    grid_ref[base + 4 * i + j, half * (1 - s) : half * (2 - s), :] = v[
                        half * j : half * (j + 1)
                    ]

    def body(i, carry):
        for j in range(2):
            r = 2 * i + j
            out_ref[r] = grid_ref[r + offset].reshape(lon, lev, width).astype(BF)
        return carry

    lax.fori_loop(0, rows // 2, body, 0)


def join(place, parts, rows, lon, lev):
    n, width = parts[0].shape
    out = pl.pallas_call(
        join_kernel,
        out_shape=jax.ShapeDtypeStruct((rows, lon, lev, width), BF),
        in_specs=[pl.BlockSpec(memory_space=pltpu.SMEM)] + spec(4),
        out_specs=spec(1)[0],
        scratch_shapes=[pltpu.VMEM((rows + WLAT, lon * lev, width), F32)],
        compiler_params=params(16),
        cost_estimate=SMALL,
    )(place, *parts)
    return jnp.transpose(out, (0, 2, 1, 3))


def send(block, shift, flip):
    count, tp = lax.axis_size("lat"), lax.axis_size("tp")
    route = [
        (u * tp + t, ((u + shift) % count) * tp + (t ^ flip)) for u in range(count) for t in range(tp)
    ]
    return lax.ppermute(block, ("lat", "tp"), route)


def swap(block, other, flip):
    count, tp = lax.axis_size("lat"), lax.axis_size("tp")
    route = [(u * tp + t, (u ^ other) * tp + (t ^ flip)) for u in range(count) for t in range(tp)]
    return lax.ppermute(block, ("lat", "tp"), route)


def lat_terms(block, bit):
    count = lax.axis_size("lat")
    terms = [block]
    while bit < count:
        block = added(terms)
        terms = [block, swap(block, bit, 0)]
        if 4 * bit <= count:
            terms += [swap(block, 2 * bit, 0), swap(block, 3 * bit, 0)]
        bit *= len(terms)
    return terms


def added(terms):
    while len(terms) > 1:
        terms = [a + b for a, b in zip(terms[::2], terms[1::2])]
    return terms[0]


def last_sum_kernel(*refs):
    qkv_ref, proj_ref = refs[-2:]
    total = added([r[...] for r in refs[:-2]])
    width = total.shape[1]
    for i in range(3):
        qkv_ref[i] = total[2 * i : 2 * i + 2]
    for i in range(4):
        for j in range(2):
            proj_ref[j : j + 1, width * i : width * (i + 1)] = total[6 + 4 * j + i : 7 + 4 * j + i]


def last_sum(terms):
    width = terms[0].shape[1]
    return pl.pallas_call(
        last_sum_kernel,
        out_shape=(jax.ShapeDtypeStruct((3, 2, width), F32), jax.ShapeDtypeStruct((2, 4 * width), F32)),
        in_specs=spec(len(terms)),
        out_specs=tuple(spec(2)),
    )(*terms)


def after(block, *others):
    return lax.optimization_barrier((block, *others))[0]


def local(features, target, w_qkv, w_proj, qkv_clip, proj_clip, shift_offset, region_ids):
    rows, lev, lon, width = features.shape
    half = lon // 2
    sector = lax.axis_index("lat")
    t = lax.axis_index("tp")
    t_arr = jnp.reshape(t, (1,)).astype(jnp.int32)
    place = jnp.stack([shift_offset[0], t % 2, sector]).astype(jnp.int32)

    f_raw, t_raw = (jnp.transpose(block, (0, 2, 1, 3)) for block in (features, target))
    f_low = send(f_raw[:, :half], -1, 0)

    w3 = jnp.transpose(w_qkv, (1, 0, 2))
    c3 = jnp.transpose(qkv_clip, (1, 0, 2))
    w3_peer = send(w3, 0, 1)
    c3_peer = send(c3, 0, 1)
    w1, w2 = send(w_proj, 0, 1), send(w_proj, 0, 2)
    wc_own, b_own = clip_qkv(w3, c3)
    wc_peer, b_peer = clip_qkv(w3_peer, c3_peer)
    idk, idq = window_ids(place, region_ids, WLAT * lev * lon)

    f_low, w1, wc_own, wc_peer, idk, idq = lax.optimization_barrier(
        (f_low, w1, wc_own, wc_peer, idk, idq)
    )
    mine, away = split(place, f_raw, f_low)
    away = away.reshape(mine.shape)
    pieces = [mine, send(away, 0, 1), send(mine, 0, 2), send(away, 0, 3)]
    w_3 = send(after(w2, mine), 0, 1)
    pc, pb = clip_proj([w_proj, w1, w2, w_3], proj_clip)

    t_low = send(after(t_raw, f_low)[:, :half], -1, 0)
    t_up, t_low, *pieces = lax.optimization_barrier((t_raw[:, half:], t_low, *pieces, pc))[:-1]
    t_up_y, t_low_y = send(t_up, 0, 2), send(t_low, 0, 2)

    normed, qkv, attn_0 = forward(t_arr, pieces, wc_own, wc_peer, idk, idq)
    other_0 = send(attn_0, 0, 2)
    probs_0 = probs_of(0, qkv, idk, idq)
    t_up_y, t_low_y = lax.optimization_barrier((t_up_y, t_low_y, probs_0))[:2]
    t_0, t_2, t_away = split(place, t_raw, t_low, t_up_y, t_low_y)
    targets = (t_0, t_2, send(t_away, 0, 1))
    attn_1 = last_windows(after(qkv, probs_0, t_away), idk, idq)
    other_1 = send(attn_1, 0, 2)
    normed_t, attn_t = turn(normed, (attn_0, attn_1))
    probs = (probs_0, probs_of(1, after(qkv, attn_1), idk, idq))

    *mixed, err_0 = output(t_arr, pieces, targets, attn_0, other_0, pc, idk)
    grads_0 = backward(0, err_0, pc, qkv, probs[0])
    other_1 = after(other_1, grads_0)
    m00, m01, m10, m11, err_1 = output(t_arr, pieces, targets, attn_1, other_1, pc, idk, mixed)
    m01 = send(m01, 0, 1)
    m10 = send(m10, 1, 0)
    m11 = send(m11, 1, 1)
    proj = proj_sums((err_0, err_1), attn_t, w_proj, w1, pb)
    proj_y = send(proj, 0, 2)
    grads_1 = backward(1, err_1, pc, qkv, probs[1])
    grads_1 = after(grads_1, m01, m10, m11, proj_y)
    grads = (grads_0, grads_1)
    own, peer = qkv_sums(grads, normed_t, w3, w3_peer, b_own, b_peer)
    proj = proj + proj_y
    own, peer = jnp.concatenate([own, proj], axis=0), jnp.concatenate([peer, proj], axis=0)
    sums = added([own, send(peer, 0, 1), swap(own, 1, 0), swap(peer, 1, 1)])
    qkv_sum, proj_sum = last_sum(lat_terms(sums, 2))
    mixed = join(place, [m00, m10, m01, m11], rows, lon, lev)
    return (mixed, jnp.transpose(qkv_sum, (1, 0, 2)), proj_sum)


def solution(mesh):
    placed = (
        P(None, None, "lat", "tp"),
        P(None, None, "lat", "tp"),
        P(None, None, "tp"),
        P("tp", None),
        P(None, None, "tp"),
        P(),
        P(),
        P(),
    )
    return jax.shard_map(
        local,
        mesh=mesh,
        in_specs=placed,
        out_specs=(P(None, None, "lat", "tp"), P(None, None, "tp"), P()),
        check_vma=False,
    )
```

```python
import functools

import jax
import jax.numpy as jnp
from jax import lax
from jax.experimental import pallas as pl
from jax.experimental.pallas import tpu as pltpu
from jax.sharding import PartitionSpec as P

HD = 64
WLAT = 6
EPS = 1e-05
NEG = -1e30
F32 = jnp.float32
BF = jnp.bfloat16
SCALE = HD ** (-0.5)
NT = (((1,), (1,)), ((), ()))
TN = (((0,), (0,)), ((), ()))
LARGE = pl.CostEstimate(flops=8 * 10**9, bytes_accessed=10**7, transcendentals=10**6)
SMALL = pl.CostEstimate(flops=1, bytes_accessed=1, transcendentals=0)


def spec(n):
    return [pl.BlockSpec(memory_space=pltpu.VMEM)] * n


def params(mib):
    return pltpu.CompilerParams(vmem_limit_bytes=mib * 1024 * 1024)


def bounds_of(weight, logits_hi, logits_lo):
    top = jnp.max(weight, axis=0, keepdims=True)
    low = jnp.min(weight, axis=0, keepdims=True)
    hi = 1.0 / (1.0 + jnp.exp(-logits_hi))
    lo = 1.0 / (1.0 + jnp.exp(-logits_lo))
    return hi * top, lo * low, hi * (1.0 - hi) * top, lo * (1.0 - lo) * low


def clip_qkv_kernel(w_ref, c_ref, wc_ref, b_ref):
    def body(i, carry):
        w = w_ref[i].astype(F32)
        up, lw, fh, fl = bounds_of(w, c_ref[i, 0:1], c_ref[i, 1:2])
        wc_ref[i] = jnp.minimum(jnp.maximum(w, lw), up).astype(BF)
        b_ref[i, 0:1] = up
        b_ref[i, 1:2] = lw
        b_ref[i, 2:3] = fh
        b_ref[i, 3:4] = fl
        return carry

    lax.fori_loop(0, 3, body, 0)


def clip_qkv(w, clips):
    n, d, e = w.shape
    return pl.pallas_call(
        clip_qkv_kernel,
        out_shape=(
            jax.ShapeDtypeStruct((n, d, e), BF),
            jax.ShapeDtypeStruct((n, 8, e), F32),
        ),
        in_specs=spec(2),
        out_specs=tuple(spec(2)),
        compiler_params=params(24),
        cost_estimate=SMALL,
    )(w, clips)


def clip_proj_kernel(s_ref, w0, w1, a2, b2, a3, b3, c_ref, wc_ref, b_ref):
    second = s_ref[2] % 2 == 1

    def body(i, carry):
        cols = pl.ds(pl.multiple_of(i * 256, 256), 256)
        parts = [w0[:, cols].astype(F32), w1[:, cols].astype(F32)]
        for first_ref, other_ref in ((a2, b2), (a3, b3)):
            a, b = first_ref[:, cols].astype(F32), other_ref[:, cols].astype(F32)
            parts += [jnp.where(second, b, a), jnp.where(second, a, b)]
        w = jnp.concatenate(parts, axis=0)
        up, lw, fh, fl = bounds_of(w, c_ref[0:1, cols], c_ref[1:2, cols])
        wc = jnp.minimum(jnp.maximum(w, lw), up).astype(BF)
        wc_ref[:, cols] = wc
        b_ref[0:1, cols] = up
        b_ref[1:2, cols] = lw
        b_ref[2:3, cols] = fh
        b_ref[3:4, cols] = fl
        return carry

    lax.fori_loop(0, w0.shape[1] // 256, body, 0)


def clip_proj(place, shards, clips):
    e, d = shards[0].shape
    return pl.pallas_call(
        clip_proj_kernel,
        out_shape=(
            jax.ShapeDtypeStruct((4 * e, d), BF),
            jax.ShapeDtypeStruct((8, d), F32),
        ),
        in_specs=[pl.BlockSpec(memory_space=pltpu.SMEM)] + spec(7),
        out_specs=tuple(spec(2)),
        compiler_params=params(24),
        cost_estimate=SMALL,
    )(place, *shards, clips)


def stacked(block, mask_a, mask_b):
    return jnp.concatenate([block * mask_a, block * mask_b], axis=0)


def head_masks():
    lane = lax.broadcasted_iota(jnp.int32, (1, 2 * HD), 1)
    mask_a = jnp.where(lane < HD, 1.0, 0.0).astype(BF)
    mask_b = jnp.where(lane < HD, 0.0, 1.0).astype(BF)
    return mask_a, mask_b


def probs_t(k, q2, allowed):
    st = lax.dot_general(k, q2, NT, preferred_element_type=F32) * SCALE
    st = jnp.where(allowed, st, NEG)
    e = jnp.exp(st - jnp.max(st, axis=0, keepdims=True))
    return e * (1.0 / jnp.sum(e, axis=0, keepdims=True))


def merge_heads(t_block):
    both = t_block.T
    n = both.shape[0] // 2
    lane = lax.broadcasted_iota(jnp.int32, (n, 2 * HD), 1)
    return jnp.where(lane < HD, both[:n], both[n:])


def allowed_t(idk_ref, idq_ref, w, cells):
    rows = pl.ds(pl.multiple_of(w * cells, 16), cells)
    idk = idk_ref[rows, :]
    return (idk == idq_ref[w]) & (idk >= 0)


def blocks(refs):
    own, other, away = refs
    return own, away.at[0], other, away.at[1]


def forward_kernel(t_ref, *refs):
    pieces = blocks(refs[:3])
    wo_ref, wp_ref, idk_ref, idq_ref, normed_ref, qkv_ref, attn_ref = refs[3:]
    t = t_ref[0]
    n, width = pieces[0].shape
    d = 4 * width

    def norm(w, carry):
        rows = pl.ds(pl.multiple_of(w * 48, 16), 48)
        x = [r[rows, :].astype(F32) for r in pieces]
        mean = sum(jnp.sum(b, axis=-1, keepdims=True) for b in x) / d
        x = [b - mean for b in x]
        var = sum(jnp.sum(b * b, axis=-1, keepdims=True) for b in x) / d
        scale = lax.rsqrt(var + EPS)
        for k in range(4):
            cols = pl.ds(pl.multiple_of((t ^ k) * width, width), width)
            normed_ref[rows, cols] = (x[k] * scale).astype(BF)
        return carry

    lax.fori_loop(0, n // 48, norm, 0)

    def project(i, carry):
        for g, w_ref in enumerate((wo_ref, wp_ref)):
            qkv_ref[3 * g + i] = jnp.dot(
                normed_ref[...], w_ref[i], preferred_element_type=F32
            ).astype(BF)
        return carry

    lax.fori_loop(0, 3, project, 0)
    attend(qkv_ref, idk_ref, idq_ref, attn_ref, 0, 2)


def attend(qkv_ref, idk_ref, idq_ref, attn_ref, first, last):
    mask_a, mask_b = head_masks()
    cells = idk_ref.shape[0] // 4

    def window(w, carry):
        rows = pl.ds(pl.multiple_of(w * cells, 16), cells)
        to = pl.ds(pl.multiple_of((w - first) * cells, 16), cells)
        allowed = allowed_t(idk_ref, idq_ref, w, cells)
        for hp in range(4):
            g, lanes = hp // 2, slice(128 * (hp % 2), 128 * (hp % 2) + 128)
            q2 = stacked(qkv_ref[3 * g, rows, lanes], mask_a, mask_b)
            pt = probs_t(qkv_ref[3 * g + 1, rows, lanes], q2, allowed)
            ot = lax.dot_general(
                qkv_ref[3 * g + 2, rows, lanes], pt.astype(BF), TN, preferred_element_type=F32
            )
            attn_ref[to, 128 * hp : 128 * hp + 128] = merge_heads(ot).astype(BF)
        return carry

    lax.fori_loop(first, last, window, 0)


def last_kernel(qkv_ref, idk_ref, idq_ref, attn_ref):
    attend(qkv_ref, idk_ref, idq_ref, attn_ref, 2, 4)


def last_windows(qkv, idk, idq):
    n, width = qkv.shape[1:]
    return pl.pallas_call(
        last_kernel,
        out_shape=jax.ShapeDtypeStruct((n // 2, 2 * width), BF),
        in_specs=spec(3),
        out_specs=spec(1)[0],
        compiler_params=params(16),
        cost_estimate=pl.CostEstimate(flops=8 * 10**9, bytes_accessed=2 * 10**6, transcendentals=10**6),
    )(qkv, idk, idq)


def forward(t, pieces, wo, wp, idk, idq):
    n, width = pieces[0].shape
    d = 4 * width
    return pl.pallas_call(
        forward_kernel,
        out_shape=(
            jax.ShapeDtypeStruct((n, d), BF),
            jax.ShapeDtypeStruct((6, n, width), BF),
            jax.ShapeDtypeStruct((n // 2, 2 * width), BF),
        ),
        in_specs=[pl.BlockSpec(memory_space=pltpu.SMEM)] + spec(7),
        out_specs=tuple(spec(3)),
        compiler_params=params(20),
        cost_estimate=pl.CostEstimate(flops=8 * 10**9, bytes_accessed=10 * 10**6, transcendentals=10**6),
    )(t, *pieces, wo, wp, idk, idq)


def turn_kernel(normed_ref, a_ref, b_ref, normed_t, attn_t):
    d = normed_ref.shape[1]

    def body(i, carry):
        cols = pl.ds(pl.multiple_of(i * 256, 256), 256)
        normed_t[cols, :] = normed_ref[:, cols].T
        return carry

    lax.fori_loop(0, d // 256, body, 0)

    def body2(i, carry):
        cols = pl.ds(pl.multiple_of(i * 256, 256), 256)
        attn_t[cols, :] = jnp.concatenate([a_ref[:, cols], b_ref[:, cols]], axis=0).T
        return carry

    lax.fori_loop(0, a_ref.shape[1] // 256, body2, 0)


def turn(normed, attn):
    n, d = normed.shape
    e = attn[0].shape[1]
    return pl.pallas_call(
        turn_kernel,
        out_shape=(jax.ShapeDtypeStruct((d, n), BF), jax.ShapeDtypeStruct((e, n), BF)),
        in_specs=spec(3),
        out_specs=tuple(spec(2)),
        compiler_params=params(16),
        cost_estimate=SMALL,
    )(normed, *attn)


def output_kernel(group, t_ref, *refs):
    pieces, targets = blocks(refs[:3]), blocks(refs[3:6])
    own_ref, other_ref, wc_ref, idk_ref = refs[6:10]
    before, refs = refs[10 : 10 + 4 * group], refs[10 + 4 * group :]
    mixed, err_ref, y_ref = refs[:4], refs[4], refs[5]
    t = t_ref[0]
    n, width = pieces[0].shape
    cells = n // 4
    half = cells // 2
    e = own_ref.shape[1]
    for old, new in zip(before, mixed):
        new[: group * cells, :] = old[...]
    for k in range(4):
        x_ref, want_ref = pieces[k], targets[k]
        cols = pl.ds(pl.multiple_of((t ^ k) * width, width), width)
        y_ref[...] = jnp.dot(own_ref[...], wc_ref[:e, cols], preferred_element_type=F32) + jnp.dot(
            other_ref[...], wc_ref[e:, cols], preferred_element_type=F32
        )
        ys = []
        for i in range(2):
            at = slice(cells * i, cells * (i + 1))
            rows = slice(cells * (2 * group + i), cells * (2 * group + i + 1))
            y = x_ref[rows, :].astype(F32) + y_ref[at, :]
            ys.append(y)
            err = y - want_ref[rows, :].astype(F32)
            valid = idk_ref[rows, :] >= 0
            err_ref[at, cols] = jnp.where(valid, err, 0.0).astype(BF)
        if k < 2:
            at = slice(cells * group, cells * (group + 1))
            for s in range(2):
                part = slice(half * s, half * (s + 1))
                mixed[2 * s + k][at, :] = jnp.concatenate([y[part] for y in ys], axis=0).astype(BF)


def output(t, pieces, targets, own, other, wc, idk, before=()):
    n, width = pieces[0].shape
    group = 1 if before else 0
    piece = jax.ShapeDtypeStruct((n // 4 * (1 + group), width), BF)
    return pl.pallas_call(
        functools.partial(output_kernel, group),
        out_shape=(piece, piece, piece, piece, jax.ShapeDtypeStruct((n // 2, 4 * width), BF)),
        in_specs=[pl.BlockSpec(memory_space=pltpu.SMEM)] + spec(10 + len(before)),
        out_specs=tuple(spec(5)),
        scratch_shapes=[pltpu.VMEM((n // 2, width), F32)],
        compiler_params=params(20),
        cost_estimate=SMALL,
    )(t, *pieces, *targets, own, other, wc, idk, *before)


def probs_kernel(group, qkv_ref, idk_ref, idq_ref, p_ref):
    cells = idk_ref.shape[0] // 4
    mask_a, mask_b = head_masks()

    def window(i, carry):
        w = 2 * group + i
        rows = pl.ds(pl.multiple_of(w * cells, 16), cells)
        allowed = allowed_t(idk_ref, idq_ref, w, cells)
        for hp in range(4):
            g, lanes = hp // 2, slice(128 * (hp % 2), 128 * (hp % 2) + 128)
            q2 = stacked(qkv_ref[3 * g, rows, lanes], mask_a, mask_b)
            p_ref[4 * i + hp] = probs_t(qkv_ref[3 * g + 1, rows, lanes], q2, allowed)
        return carry

    lax.fori_loop(0, 2, window, 0)


def probs_of(group, qkv, idk, idq):
    n, width = qkv.shape[1:]
    return pl.pallas_call(
        functools.partial(probs_kernel, group),
        out_shape=jax.ShapeDtypeStruct((8, n // 4, n // 2), F32),
        in_specs=spec(3),
        out_specs=spec(1)[0],
        compiler_params=params(16),
        cost_estimate=SMALL,
    )(qkv, idk, idq)


def masked_sums(grad, w, bounds):
    g_hi = jnp.sum(jnp.where(w > bounds[0:1], grad, 0.0), axis=0, keepdims=True) * bounds[2:3]
    g_lo = jnp.sum(jnp.where(w < bounds[1:2], grad, 0.0), axis=0, keepdims=True) * bounds[3:4]
    return g_hi, g_lo


def proj_sums_kernel(e0_ref, e1_ref, attn_t, po_ref, pp_ref, pb_ref, proj_ref):
    def proj_part(i, carry):
        cols = pl.ds(pl.multiple_of(i * 256, 256), 256)
        err = jnp.concatenate([e0_ref[:, cols], e1_ref[:, cols]], axis=0)
        grad = jnp.dot(attn_t[...], err, preferred_element_type=F32)
        n = po_ref.shape[0]
        b = pb_ref[:, cols]
        h0, l0 = masked_sums(grad[:n], po_ref[:, cols].astype(F32), b)
        h1, l1 = masked_sums(grad[n:], pp_ref[:, cols].astype(F32), b)
        proj_ref[0:1, cols] = h0 + h1
        proj_ref[1:2, cols] = l0 + l1
        return carry

    lax.fori_loop(0, 4, proj_part, 0)


def proj_sums(errs, attn_t, po, pp, pb):
    return pl.pallas_call(
        proj_sums_kernel,
        out_shape=jax.ShapeDtypeStruct((2, errs[0].shape[1]), F32),
        in_specs=spec(6),
        out_specs=spec(1)[0],
        compiler_params=params(16),
        cost_estimate=pl.CostEstimate(flops=10**9, bytes_accessed=3 * 10**6, transcendentals=0),
    )(*errs, attn_t, po, pp, pb)


def backward_kernel(group, err_ref, wc_ref, qkv_ref, p_ref, g_ref, d_ref):
    e = d_ref.shape[1]
    cells = d_ref.shape[0] // 2
    d_ref[...] = lax.dot_general(err_ref[...], wc_ref[:e], NT, preferred_element_type=F32).astype(BF)
    mask_a, mask_b = head_masks()

    def window(i, carry):
        rows = pl.ds(pl.multiple_of((2 * group + i) * cells, 16), cells)
        at = pl.ds(pl.multiple_of(i * cells, 16), cells)
        for hp in range(4):
            g, lanes = hp // 2, slice(128 * (hp % 2), 128 * (hp % 2) + 128)
            q2 = stacked(qkv_ref[3 * g, rows, lanes], mask_a, mask_b)
            k = qkv_ref[3 * g + 1, rows, lanes]
            v = qkv_ref[3 * g + 2, rows, lanes]
            pt = p_ref[4 * i + hp]
            d2 = stacked(d_ref[at, 128 * hp : 128 * hp + 128], mask_a, mask_b)
            g_ref[3 * g + 2, at, lanes] = jnp.dot(
                pt.astype(BF), d2, preferred_element_type=F32
            ).astype(BF)
            dpt = lax.dot_general(v, d2, NT, preferred_element_type=F32)
            gst = (pt * (dpt - jnp.sum(pt * dpt, axis=0, keepdims=True))).astype(BF)
            g_ref[3 * g + 1, at, lanes] = (
                jnp.dot(gst, q2, preferred_element_type=F32) * SCALE
            ).astype(BF)
            gqt = lax.dot_general(k, gst, TN, preferred_element_type=F32) * SCALE
            g_ref[3 * g, at, lanes] = merge_heads(gqt).astype(BF)
        return carry

    lax.fori_loop(0, 2, window, 0)


def backward(group, err, wc, qkv, probs):
    n, width = qkv.shape[1:]
    return pl.pallas_call(
        functools.partial(backward_kernel, group),
        out_shape=jax.ShapeDtypeStruct((6, n // 2, width), BF),
        in_specs=spec(4),
        out_specs=spec(1)[0],
        scratch_shapes=[pltpu.VMEM((n // 2, 2 * width), BF)],
        compiler_params=params(20),
        cost_estimate=LARGE if group else SMALL,
    )(err, wc, qkv, probs)


def qkv_sums_kernel(g0_ref, g1_ref, normed_t, wo_ref, wp_ref, bo_ref, bp_ref, own_ref, peer_ref):
    width = g0_ref.shape[2]

    def qkv_part(i, carry):
        for g, (w_ref, b_ref, to_ref) in enumerate(
            ((wo_ref, bo_ref, own_ref), (wp_ref, bp_ref, peer_ref))
        ):
            cells = jnp.concatenate([g0_ref[3 * g + i], g1_ref[3 * g + i]], axis=0)
            grad = jnp.dot(normed_t[...], cells, preferred_element_type=F32)
            hi, lo = masked_sums(grad, w_ref[i].astype(F32), b_ref[i])
            to_ref[0:1, pl.ds(pl.multiple_of(i * width, width), width)] = hi
            to_ref[1:2, pl.ds(pl.multiple_of(i * width, width), width)] = lo
        return carry

    lax.fori_loop(0, 3, qkv_part, 0)


def qkv_sums(g, normed_t, wo, wp, bo, bp):
    width = g[0].shape[2]
    return pl.pallas_call(
        qkv_sums_kernel,
        out_shape=(jax.ShapeDtypeStruct((2, 3 * width), F32),) * 2,
        in_specs=spec(7),
        out_specs=tuple(spec(2)),
        compiler_params=params(20),
        cost_estimate=pl.CostEstimate(flops=4 * 10**9, bytes_accessed=8 * 10**6, transcendentals=0),
    )(*g, normed_t, wo, wp, bo, bp)


def split_kernel(s_ref, *refs):
    offset, core = s_ref[0], s_ref[1]
    pairs = (len(refs) - 1) // 3
    rows, lon, lev, width = refs[1].shape
    many = (rows + WLAT) // 2
    half = lon * lev
    cells = 2 * WLAT * half
    for rel in range(2):
        base = many * (core ^ rel) - offset

        def body(w, carry):
            at = pl.ds(pl.multiple_of(w * cells, 16), cells)
            for i in range(pairs):
                up_ref, low_ref = refs[2 * i : 2 * i + 2]
                parts = []
                for ref, part in ((up_ref, slice(up_ref.shape[1] - lon, up_ref.shape[1])), (low_ref, slice(0, lon))):
                    for j in range(WLAT):
                        r = base + WLAT * w + j
                        v = ref[jnp.clip(r, 0, rows - 1), part].astype(F32).reshape(half, width)
                        parts.append(jnp.where((r >= 0) & (r < rows), v, 0.0))
                block = jnp.concatenate(parts, axis=0).astype(BF)
                if rel:
                    refs[-1][i, at, :] = block
                else:
                    refs[2 * pairs + i][at, :] = block
            return carry

        lax.fori_loop(0, many // WLAT, body, 0)


def split(place, *halves):
    rows, lon, lev, width = halves[1].shape
    pairs = len(halves) // 2
    n = (rows + WLAT) * lon * lev
    return pl.pallas_call(
        split_kernel,
        out_shape=(jax.ShapeDtypeStruct((n, width), BF),) * pairs
        + (jax.ShapeDtypeStruct((pairs, n, width), BF),),
        in_specs=[pl.BlockSpec(memory_space=pltpu.SMEM)] + spec(2 * pairs),
        out_specs=tuple(spec(pairs + 1)),
        compiler_params=params(16),
        cost_estimate=SMALL,
    )(place, *halves)


def cell_at(c, window):
    cells = 2 * WLAT * window
    w = sum((c >= i * cells).astype(jnp.int32) for i in range(1, 4))
    c = c - w * cells
    s = (c >= WLAT * window).astype(jnp.int32)
    c = c - s * WLAT * window
    r = sum((c >= i * window).astype(jnp.int32) for i in range(1, WLAT))
    c = c - r * window
    return w * WLAT + r, s * (window // 2) + (c >> 1), c & 1


def ids_kernel(s_ref, ids_ref, idk_ref, idq_ref):
    offset, core, sector = s_ref[0], s_ref[1], s_ref[2]
    rows, lev, total = ids_ref.shape
    n = idk_ref.shape[0]
    cells = n // 4
    window = cells // (2 * WLAT)
    many = (rows + WLAT) // 2
    ids = ids_ref[...].astype(F32).reshape(rows * lev, total)

    def find(c):
        r, lon, level = cell_at(c, window)
        r = r + many * core - offset
        lon = lon + sector * window + window // 2
        lon = jnp.where(lon >= total, lon - total, lon)
        valid = (r >= 0) & (r < rows)
        return jnp.where(valid, 2 * r + level, -1), lon, valid

    spot, lon, valid = find(lax.broadcasted_iota(jnp.int32, (n, 1), 0))
    at = lax.broadcasted_iota(jnp.int32, (n, rows * lev), 1) == spot
    found = jnp.dot(jnp.where(at, 1.0, 0.0), ids, preferred_element_type=F32)
    there = lax.broadcasted_iota(jnp.int32, (n, total), 1) == lon
    found = jnp.sum(jnp.where(there, found, 0.0), axis=1, keepdims=True)
    idk_ref[...] = jnp.where(valid, found, -1.0).astype(jnp.int32)
    for w in range(4):
        lane = lax.broadcasted_iota(jnp.int32, (1, 2 * cells), 1)
        spot, lon, valid = find(w * cells + jnp.where(lane >= cells, lane - cells, lane))
        there = lax.broadcasted_iota(jnp.int32, (total, 2 * cells), 0) == lon
        found = jnp.dot(ids, jnp.where(there, 1.0, 0.0), preferred_element_type=F32)
        at = lax.broadcasted_iota(jnp.int32, (rows * lev, 2 * cells), 0) == spot
        found = jnp.sum(jnp.where(at, found, 0.0), axis=0, keepdims=True)
        idq_ref[w] = jnp.where(valid, found, -1.0).astype(jnp.int32)


def window_ids(place, ids, cells):
    return pl.pallas_call(
        ids_kernel,
        out_shape=(
            jax.ShapeDtypeStruct((4 * cells, 1), jnp.int32),
            jax.ShapeDtypeStruct((4, 1, 2 * cells), jnp.int32),
        ),
        in_specs=[pl.BlockSpec(memory_space=pltpu.SMEM)] + spec(1),
        out_specs=tuple(spec(2)),
        compiler_params=params(16),
        cost_estimate=SMALL,
    )(place, ids)


def join_kernel(s_ref, a0, a1, b0, b1, out_ref, grid_ref):
    offset, core = s_ref[0], s_ref[1]
    rows, lon, lev, width = out_ref.shape
    many = (rows + WLAT) // 2
    half = lon * lev // 2
    for rel, ins in ((0, (a0, a1)), (1, (b0, b1))):
        base = many * (core ^ rel)
        for s in range(2):
            for i in range(many // 4):
                v = ins[s][4 * half * i : 4 * half * (i + 1), :].astype(F32)
                for j in range(4):
                    grid_ref[base + 4 * i + j, half * (1 - s) : half * (2 - s), :] = v[
                        half * j : half * (j + 1)
                    ]

    def body(i, carry):
        for j in range(2):
            r = 2 * i + j
            out_ref[r] = grid_ref[r + offset].reshape(lon, lev, width).astype(BF)
        return carry

    lax.fori_loop(0, rows // 2, body, 0)


def join(place, parts, rows, lon, lev):
    n, width = parts[0].shape
    out = pl.pallas_call(
        join_kernel,
        out_shape=jax.ShapeDtypeStruct((rows, lon, lev, width), BF),
        in_specs=[pl.BlockSpec(memory_space=pltpu.SMEM)] + spec(4),
        out_specs=spec(1)[0],
        scratch_shapes=[pltpu.VMEM((rows + WLAT, lon * lev, width), F32)],
        compiler_params=params(16),
        cost_estimate=SMALL,
    )(place, *parts)
    return jnp.transpose(out, (0, 2, 1, 3))


def send(block, shift, flip):
    count, tp = lax.axis_size("lat"), lax.axis_size("tp")
    route = [
        (u * tp + t, ((u + shift) % count) * tp + (t ^ flip)) for u in range(count) for t in range(tp)
    ]
    return lax.ppermute(block, ("lat", "tp"), route)


def swap(block, other, flip):
    count, tp = lax.axis_size("lat"), lax.axis_size("tp")
    route = [(u * tp + t, (u ^ other) * tp + (t ^ flip)) for u in range(count) for t in range(tp)]
    return lax.ppermute(block, ("lat", "tp"), route)


def lat_terms(block, bit):
    count = lax.axis_size("lat")
    terms = [block]
    while bit < count:
        block = added(terms)
        terms = [block, swap(block, bit, 0)]
        if 4 * bit <= count:
            terms += [swap(block, 2 * bit, 0), swap(block, 3 * bit, 0)]
        bit *= len(terms)
    return terms


def added(terms):
    while len(terms) > 1:
        terms = [a + b for a, b in zip(terms[::2], terms[1::2])]
    return terms[0]


def after(block, *others):
    return lax.optimization_barrier((block, *others))[0]


def local(features, target, w_qkv, w_proj, qkv_clip, proj_clip, shift_offset, region_ids):
    rows, lev, lon, width = features.shape
    half = lon // 2
    sector = lax.axis_index("lat")
    t = lax.axis_index("tp")
    t_arr = jnp.reshape(t, (1,)).astype(jnp.int32)
    place = jnp.stack([shift_offset[0], t % 2, sector]).astype(jnp.int32)

    f_raw, t_raw = (jnp.transpose(block, (0, 2, 1, 3)) for block in (features, target))
    f_low, f_up, w_qkv, w_proj = lax.optimization_barrier((f_raw[:, :half], f_raw[:, half:], w_qkv, w_proj))
    f_low = send(f_low, -1, 0)
    f_up_y = send(f_up, 0, 2)

    w3 = jnp.transpose(w_qkv, (1, 0, 2))
    c3 = jnp.transpose(qkv_clip, (1, 0, 2))
    w3_peer = send(w3, 0, 1)
    c3_peer = send(c3, 0, 1)
    share = w_proj.shape[0] // 2
    slab = send(lax.dynamic_slice_in_dim(w_proj, share * (sector % 2), share, 0), 0, 2)
    w1 = send(w_proj, 0, 1)
    wc_own, b_own = clip_qkv(w3, c3)
    wc_peer, b_peer = clip_qkv(w3_peer, c3_peer)
    idk, idq = window_ids(place, region_ids, WLAT * lev * lon)
    f_low, f_up_y, w1, wc_own, wc_peer, idk, idq = lax.optimization_barrier(
        (f_low, f_up_y, w1, wc_own, wc_peer, idk, idq)
    )
    f_low_y = send(f_low, 0, 2)
    t_low = send(after(t_raw, f_low)[:, :half], -1, 0)
    f_low_y, t_low, slab = lax.optimization_barrier((f_low_y, t_low, slab))
    x_0, x_2, x_away = split(place, f_raw, f_low, f_up_y, f_low_y)
    pieces = (x_0, x_2, send(x_away, 0, 1))

    t_up = after(t_raw, f_low_y)[:, half:]
    t_up_y, t_low_y = send(t_up, 0, 2), send(t_low, 0, 2)
    more = swap(slab, 1, 0)

    normed, qkv, attn_0 = forward(t_arr, pieces, wc_own, wc_peer, idk, idq)
    other_0 = send(attn_0, 0, 2)
    probs_0 = probs_of(0, qkv, idk, idq)
    attn_1 = last_windows(after(qkv, probs_0, t_up_y, t_low_y, more), idk, idq)
    slab_3, more_3 = send(after(slab, attn_1), 0, 1), send(after(more, attn_1), 0, 1)
    pc, pb = clip_proj(place, [w_proj, w1, slab, more, slab_3, more_3], proj_clip)
    t_up_y, t_low_y = lax.optimization_barrier((t_up_y, t_low_y, other_0, attn_1))[:2]
    t_0, t_2, t_away = split(place, t_raw, t_low, t_up_y, t_low_y)
    targets = (t_0, t_2, send(t_away, 0, 1))
    other_1 = send(attn_1, 0, 2)
    normed_t, attn_t = turn(normed, (attn_0, attn_1))
    probs = (probs_0, probs_of(1, after(qkv, attn_1), idk, idq))

    *mixed, err_0 = output(t_arr, pieces, targets, attn_0, other_0, pc, idk)
    grads_0 = backward(0, err_0, pc, qkv, probs[0])
    other_1 = after(other_1, grads_0)
    m00, m01, m10, m11, err_1 = output(t_arr, pieces, targets, attn_1, other_1, pc, idk, mixed)
    m01 = send(m01, 0, 1)
    m10 = send(m10, 1, 0)
    m11 = send(m11, 1, 1)
    proj = proj_sums((err_0, err_1), attn_t, w_proj, w1, pb)
    proj_y = send(proj, 0, 2)
    grads_1 = backward(1, err_1, pc, qkv, probs[1])
    grads_1 = after(grads_1, m01, m10, m11, proj_y)
    grads = (grads_0, grads_1)
    own, peer = qkv_sums(grads, normed_t, w3, w3_peer, b_own, b_peer)
    proj = proj + proj_y
    own, peer = jnp.concatenate([own, proj], axis=1), jnp.concatenate([peer, proj], axis=1)
    sums = added([own, send(peer, 0, 1), swap(own, 1, 0), swap(peer, 1, 1)])
    sums = added(lat_terms(sums, 2))
    mixed = join(place, [m00, m10, m01, m11], rows, lon, lev)
    return (mixed, sums[:, : 3 * width].reshape(2, 3, width), sums[:, 3 * width :])


def solution(mesh):
    placed = (
        P(None, None, "lat", "tp"),
        P(None, None, "lat", "tp"),
        P(None, None, "tp"),
        P("tp", None),
        P(None, None, "tp"),
        P(),
        P(),
        P(),
    )
    return jax.shard_map(
        local,
        mesh=mesh,
        in_specs=placed,
        out_specs=(P(None, None, "lat", "tp"), P(None, None, "tp"), P()),
        check_vma=False,
    )
```

```python
import functools

import jax
import jax.numpy as jnp
from jax import lax
from jax.experimental import pallas as pl
from jax.experimental.pallas import tpu as pltpu
from jax.sharding import PartitionSpec as P

HD = 64
WLAT = 6
EPS = 1e-05
NEG = -1e30
F32 = jnp.float32
BF = jnp.bfloat16
SCALE = HD ** (-0.5)
NT = (((1,), (1,)), ((), ()))
TN = (((0,), (0,)), ((), ()))
LARGE = pl.CostEstimate(flops=8 * 10**9, bytes_accessed=10**7, transcendentals=10**6)
SMALL = pl.CostEstimate(flops=1, bytes_accessed=1, transcendentals=0)


def spec(n):
    return [pl.BlockSpec(memory_space=pltpu.VMEM)] * n


def params(mib):
    return pltpu.CompilerParams(vmem_limit_bytes=mib * 1024 * 1024)


def bounds_of(weight, logits_hi, logits_lo):
    top = jnp.max(weight, axis=0, keepdims=True)
    low = jnp.min(weight, axis=0, keepdims=True)
    hi = 1.0 / (1.0 + jnp.exp(-logits_hi))
    lo = 1.0 / (1.0 + jnp.exp(-logits_lo))
    return hi * top, lo * low, hi * (1.0 - hi) * top, lo * (1.0 - lo) * low


def clip_qkv_kernel(w_ref, c_ref, wc_ref, b_ref):
    def body(i, carry):
        w = w_ref[i].astype(F32)
        up, lw, fh, fl = bounds_of(w, c_ref[i, 0:1], c_ref[i, 1:2])
        wc_ref[i] = jnp.minimum(jnp.maximum(w, lw), up).astype(BF)
        b_ref[i, 0:1] = up
        b_ref[i, 1:2] = lw
        b_ref[i, 2:3] = fh
        b_ref[i, 3:4] = fl
        return carry

    lax.fori_loop(0, 3, body, 0)


def clip_qkv(w, clips):
    n, d, e = w.shape
    return pl.pallas_call(
        clip_qkv_kernel,
        out_shape=(
            jax.ShapeDtypeStruct((n, d, e), BF),
            jax.ShapeDtypeStruct((n, 8, e), F32),
        ),
        in_specs=spec(2),
        out_specs=tuple(spec(2)),
        compiler_params=params(24),
        cost_estimate=SMALL,
    )(w, clips)


def clip_proj_kernel(s_ref, w0, w1, a2, b2, a3, b3, c_ref, wc_ref, b_ref):
    second = s_ref[2] % 2 == 1

    def body(i, carry):
        cols = pl.ds(pl.multiple_of(i * 256, 256), 256)
        parts = [w0[:, cols].astype(F32), w1[:, cols].astype(F32)]
        for first_ref, other_ref in ((a2, b2), (a3, b3)):
            a, b = first_ref[:, cols].astype(F32), other_ref[:, cols].astype(F32)
            parts += [jnp.where(second, b, a), jnp.where(second, a, b)]
        w = jnp.concatenate(parts, axis=0)
        up, lw, fh, fl = bounds_of(w, c_ref[0:1, cols], c_ref[1:2, cols])
        wc = jnp.minimum(jnp.maximum(w, lw), up).astype(BF)
        wc_ref[:, cols] = wc
        b_ref[0:1, cols] = up
        b_ref[1:2, cols] = lw
        b_ref[2:3, cols] = fh
        b_ref[3:4, cols] = fl
        return carry

    lax.fori_loop(0, w0.shape[1] // 256, body, 0)


def clip_proj(place, shards, clips):
    e, d = shards[0].shape
    return pl.pallas_call(
        clip_proj_kernel,
        out_shape=(
            jax.ShapeDtypeStruct((4 * e, d), BF),
            jax.ShapeDtypeStruct((8, d), F32),
        ),
        in_specs=[pl.BlockSpec(memory_space=pltpu.SMEM)] + spec(7),
        out_specs=tuple(spec(2)),
        compiler_params=params(24),
        cost_estimate=SMALL,
    )(place, *shards, clips)


def stacked(block, mask_a, mask_b):
    return jnp.concatenate([block * mask_a, block * mask_b], axis=0)


def head_masks():
    lane = lax.broadcasted_iota(jnp.int32, (1, 2 * HD), 1)
    mask_a = jnp.where(lane < HD, 1.0, 0.0).astype(BF)
    mask_b = jnp.where(lane < HD, 0.0, 1.0).astype(BF)
    return mask_a, mask_b


def probs_t(k, q2, allowed):
    st = lax.dot_general(k, q2, NT, preferred_element_type=F32) * SCALE
    st = jnp.where(allowed, st, NEG)
    e = jnp.exp(st - jnp.max(st, axis=0, keepdims=True))
    return e * (1.0 / jnp.sum(e, axis=0, keepdims=True))


def merge_heads(t_block):
    both = t_block.T
    n = both.shape[0] // 2
    lane = lax.broadcasted_iota(jnp.int32, (n, 2 * HD), 1)
    return jnp.where(lane < HD, both[:n], both[n:])


def allowed_t(idk_ref, idq_ref, w, cells):
    rows = pl.ds(pl.multiple_of(w * cells, 16), cells)
    idk = idk_ref[rows, :]
    return (idk == idq_ref[w]) & (idk >= 0)


def blocks(refs):
    own, other, away = refs
    return own, away.at[0], other, away.at[1]


def forward_kernel(t_ref, *refs):
    pieces = blocks(refs[:3])
    wo_ref, wp_ref, idk_ref, idq_ref, normed_ref, qkv_ref, attn_ref = refs[3:]
    t = t_ref[0]
    n, width = pieces[0].shape
    d = 4 * width

    def norm(w, carry):
        rows = pl.ds(pl.multiple_of(w * 48, 16), 48)
        x = [r[rows, :].astype(F32) for r in pieces]
        mean = sum(jnp.sum(b, axis=-1, keepdims=True) for b in x) / d
        x = [b - mean for b in x]
        var = sum(jnp.sum(b * b, axis=-1, keepdims=True) for b in x) / d
        scale = lax.rsqrt(var + EPS)
        for k in range(4):
            cols = pl.ds(pl.multiple_of((t ^ k) * width, width), width)
            normed_ref[rows, cols] = (x[k] * scale).astype(BF)
        return carry

    lax.fori_loop(0, n // 48, norm, 0)

    def project(i, carry):
        for g, w_ref in enumerate((wo_ref, wp_ref)):
            qkv_ref[3 * g + i] = jnp.dot(
                normed_ref[...], w_ref[i], preferred_element_type=F32
            ).astype(BF)
        return carry

    lax.fori_loop(0, 3, project, 0)
    attend(qkv_ref, idk_ref, idq_ref, attn_ref, 0, 2)


def attend(qkv_ref, idk_ref, idq_ref, attn_ref, first, last):
    mask_a, mask_b = head_masks()
    cells = idk_ref.shape[0] // 4

    def window(w, carry):
        rows = pl.ds(pl.multiple_of(w * cells, 16), cells)
        to = pl.ds(pl.multiple_of((w - first) * cells, 16), cells)
        allowed = allowed_t(idk_ref, idq_ref, w, cells)
        for hp in range(4):
            g, lanes = hp // 2, slice(128 * (hp % 2), 128 * (hp % 2) + 128)
            q2 = stacked(qkv_ref[3 * g, rows, lanes], mask_a, mask_b)
            pt = probs_t(qkv_ref[3 * g + 1, rows, lanes], q2, allowed)
            ot = lax.dot_general(
                qkv_ref[3 * g + 2, rows, lanes], pt.astype(BF), TN, preferred_element_type=F32
            )
            attn_ref[to, 128 * hp : 128 * hp + 128] = merge_heads(ot).astype(BF)
        return carry

    lax.fori_loop(first, last, window, 0)


def last_kernel(qkv_ref, idk_ref, idq_ref, attn_ref):
    attend(qkv_ref, idk_ref, idq_ref, attn_ref, 2, 4)


def last_windows(qkv, idk, idq):
    n, width = qkv.shape[1:]
    return pl.pallas_call(
        last_kernel,
        out_shape=jax.ShapeDtypeStruct((n // 2, 2 * width), BF),
        in_specs=spec(3),
        out_specs=spec(1)[0],
        compiler_params=params(16),
        cost_estimate=pl.CostEstimate(flops=8 * 10**9, bytes_accessed=2 * 10**6, transcendentals=10**6),
    )(qkv, idk, idq)


def forward(t, pieces, wo, wp, idk, idq):
    n, width = pieces[0].shape
    d = 4 * width
    return pl.pallas_call(
        forward_kernel,
        out_shape=(
            jax.ShapeDtypeStruct((n, d), BF),
            jax.ShapeDtypeStruct((6, n, width), BF),
            jax.ShapeDtypeStruct((n // 2, 2 * width), BF),
        ),
        in_specs=[pl.BlockSpec(memory_space=pltpu.SMEM)] + spec(7),
        out_specs=tuple(spec(3)),
        compiler_params=params(20),
        cost_estimate=pl.CostEstimate(flops=8 * 10**9, bytes_accessed=10 * 10**6, transcendentals=10**6),
    )(t, *pieces, wo, wp, idk, idq)


def turn_kernel(normed_ref, a_ref, b_ref, normed_t, attn_t):
    d = normed_ref.shape[1]

    def body(i, carry):
        cols = pl.ds(pl.multiple_of(i * 256, 256), 256)
        normed_t[cols, :] = normed_ref[:, cols].T
        return carry

    lax.fori_loop(0, d // 256, body, 0)

    def body2(i, carry):
        cols = pl.ds(pl.multiple_of(i * 256, 256), 256)
        attn_t[cols, :] = jnp.concatenate([a_ref[:, cols], b_ref[:, cols]], axis=0).T
        return carry

    lax.fori_loop(0, a_ref.shape[1] // 256, body2, 0)


def turn(normed, attn):
    n, d = normed.shape
    e = attn[0].shape[1]
    return pl.pallas_call(
        turn_kernel,
        out_shape=(jax.ShapeDtypeStruct((d, n), BF), jax.ShapeDtypeStruct((e, n), BF)),
        in_specs=spec(3),
        out_specs=tuple(spec(2)),
        compiler_params=params(16),
        cost_estimate=SMALL,
    )(normed, *attn)


def output_kernel(group, t_ref, *refs):
    pieces, targets = blocks(refs[:3]), refs[3:7]
    own_ref, other_ref, wc_ref, idk_ref = refs[7:11]
    before, refs = refs[11 : 11 + 4 * group], refs[11 + 4 * group :]
    mixed, err_ref, y_ref = refs[:4], refs[4], refs[5]
    t = t_ref[0]
    n, width = pieces[0].shape
    cells = n // 4
    half = cells // 2
    e = own_ref.shape[1]
    for old, new in zip(before, mixed):
        new[: group * cells, :] = old[...]
    for k in range(4):
        x_ref, want_ref = pieces[k], targets[k]
        cols = pl.ds(pl.multiple_of((t ^ k) * width, width), width)
        y_ref[...] = jnp.dot(own_ref[...], wc_ref[:e, cols], preferred_element_type=F32) + jnp.dot(
            other_ref[...], wc_ref[e:, cols], preferred_element_type=F32
        )
        ys = []
        for i in range(2):
            at = slice(cells * i, cells * (i + 1))
            rows = slice(cells * (2 * group + i), cells * (2 * group + i + 1))
            y = x_ref[rows, :].astype(F32) + y_ref[at, :]
            ys.append(y)
            err = y - want_ref[rows, :].astype(F32)
            valid = idk_ref[rows, :] >= 0
            err_ref[at, cols] = jnp.where(valid, err, 0.0).astype(BF)
        if k < 2:
            at = slice(cells * group, cells * (group + 1))
            for s in range(2):
                part = slice(half * s, half * (s + 1))
                mixed[2 * s + k][at, :] = jnp.concatenate([y[part] for y in ys], axis=0).astype(BF)


def output(t, pieces, targets, own, other, wc, idk, before=()):
    n, width = pieces[0].shape
    group = 1 if before else 0
    piece = jax.ShapeDtypeStruct((n // 4 * (1 + group), width), BF)
    return pl.pallas_call(
        functools.partial(output_kernel, group),
        out_shape=(piece, piece, piece, piece, jax.ShapeDtypeStruct((n // 2, 4 * width), BF)),
        in_specs=[pl.BlockSpec(memory_space=pltpu.SMEM)] + spec(11 + len(before)),
        out_specs=tuple(spec(5)),
        scratch_shapes=[pltpu.VMEM((n // 2, width), F32)],
        compiler_params=params(20),
        cost_estimate=SMALL,
    )(t, *pieces, *targets, own, other, wc, idk, *before)


def probs_kernel(group, qkv_ref, idk_ref, idq_ref, p_ref):
    cells = idk_ref.shape[0] // 4
    mask_a, mask_b = head_masks()

    def window(i, carry):
        w = 2 * group + i
        rows = pl.ds(pl.multiple_of(w * cells, 16), cells)
        allowed = allowed_t(idk_ref, idq_ref, w, cells)
        for hp in range(4):
            g, lanes = hp // 2, slice(128 * (hp % 2), 128 * (hp % 2) + 128)
            q2 = stacked(qkv_ref[3 * g, rows, lanes], mask_a, mask_b)
            p_ref[4 * i + hp] = probs_t(qkv_ref[3 * g + 1, rows, lanes], q2, allowed)
        return carry

    lax.fori_loop(0, 2, window, 0)


def probs_of(group, qkv, idk, idq):
    n, width = qkv.shape[1:]
    return pl.pallas_call(
        functools.partial(probs_kernel, group),
        out_shape=jax.ShapeDtypeStruct((8, n // 4, n // 2), F32),
        in_specs=spec(3),
        out_specs=spec(1)[0],
        compiler_params=params(16),
        cost_estimate=SMALL,
    )(qkv, idk, idq)


def masked_sums(grad, w, bounds):
    g_hi = jnp.sum(jnp.where(w > bounds[0:1], grad, 0.0), axis=0, keepdims=True) * bounds[2:3]
    g_lo = jnp.sum(jnp.where(w < bounds[1:2], grad, 0.0), axis=0, keepdims=True) * bounds[3:4]
    return g_hi, g_lo


def proj_sums_kernel(e0_ref, e1_ref, attn_t, po_ref, pp_ref, pb_ref, proj_ref):
    def proj_part(i, carry):
        cols = pl.ds(pl.multiple_of(i * 256, 256), 256)
        err = jnp.concatenate([e0_ref[:, cols], e1_ref[:, cols]], axis=0)
        grad = jnp.dot(attn_t[...], err, preferred_element_type=F32)
        n = po_ref.shape[0]
        b = pb_ref[:, cols]
        h0, l0 = masked_sums(grad[:n], po_ref[:, cols].astype(F32), b)
        h1, l1 = masked_sums(grad[n:], pp_ref[:, cols].astype(F32), b)
        proj_ref[0:1, cols] = h0 + h1
        proj_ref[1:2, cols] = l0 + l1
        return carry

    lax.fori_loop(0, 4, proj_part, 0)


def proj_sums(errs, attn_t, po, pp, pb):
    return pl.pallas_call(
        proj_sums_kernel,
        out_shape=jax.ShapeDtypeStruct((2, errs[0].shape[1]), F32),
        in_specs=spec(6),
        out_specs=spec(1)[0],
        compiler_params=params(16),
        cost_estimate=pl.CostEstimate(flops=10**9, bytes_accessed=3 * 10**6, transcendentals=0),
    )(*errs, attn_t, po, pp, pb)


def backward_kernel(group, err_ref, wc_ref, qkv_ref, p_ref, g_ref, d_ref):
    e = d_ref.shape[1]
    cells = d_ref.shape[0] // 2
    d_ref[...] = lax.dot_general(err_ref[...], wc_ref[:e], NT, preferred_element_type=F32).astype(BF)
    mask_a, mask_b = head_masks()

    def window(i, carry):
        rows = pl.ds(pl.multiple_of((2 * group + i) * cells, 16), cells)
        at = pl.ds(pl.multiple_of(i * cells, 16), cells)
        for hp in range(4):
            g, lanes = hp // 2, slice(128 * (hp % 2), 128 * (hp % 2) + 128)
            q2 = stacked(qkv_ref[3 * g, rows, lanes], mask_a, mask_b)
            k = qkv_ref[3 * g + 1, rows, lanes]
            v = qkv_ref[3 * g + 2, rows, lanes]
            pt = p_ref[4 * i + hp]
            d2 = stacked(d_ref[at, 128 * hp : 128 * hp + 128], mask_a, mask_b)
            g_ref[3 * g + 2, at, lanes] = jnp.dot(
                pt.astype(BF), d2, preferred_element_type=F32
            ).astype(BF)
            dpt = lax.dot_general(v, d2, NT, preferred_element_type=F32)
            gst = (pt * (dpt - jnp.sum(pt * dpt, axis=0, keepdims=True))).astype(BF)
            g_ref[3 * g + 1, at, lanes] = (
                jnp.dot(gst, q2, preferred_element_type=F32) * SCALE
            ).astype(BF)
            gqt = lax.dot_general(k, gst, TN, preferred_element_type=F32) * SCALE
            g_ref[3 * g, at, lanes] = merge_heads(gqt).astype(BF)
        return carry

    lax.fori_loop(0, 2, window, 0)


def backward(group, err, wc, qkv, probs):
    n, width = qkv.shape[1:]
    return pl.pallas_call(
        functools.partial(backward_kernel, group),
        out_shape=jax.ShapeDtypeStruct((6, n // 2, width), BF),
        in_specs=spec(4),
        out_specs=spec(1)[0],
        scratch_shapes=[pltpu.VMEM((n // 2, 2 * width), BF)],
        compiler_params=params(20),
        cost_estimate=LARGE if group else SMALL,
    )(err, wc, qkv, probs)


def qkv_sums_kernel(side, g0_ref, g1_ref, normed_t, w_ref, b_ref, to_ref):
    width = g0_ref.shape[2]

    def qkv_part(i, carry):
        cells = jnp.concatenate([g0_ref[3 * side + i], g1_ref[3 * side + i]], axis=0)
        grad = jnp.dot(normed_t[...], cells, preferred_element_type=F32)
        hi, lo = masked_sums(grad, w_ref[i].astype(F32), b_ref[i])
        to_ref[0:1, pl.ds(pl.multiple_of(i * width, width), width)] = hi
        to_ref[1:2, pl.ds(pl.multiple_of(i * width, width), width)] = lo
        return carry

    lax.fori_loop(0, 3, qkv_part, 0)


def qkv_sums(side, g, normed_t, w, b):
    width = g[0].shape[2]
    return pl.pallas_call(
        functools.partial(qkv_sums_kernel, side),
        out_shape=jax.ShapeDtypeStruct((2, 3 * width), F32),
        in_specs=spec(5),
        out_specs=spec(1)[0],
        compiler_params=params(20),
        cost_estimate=LARGE,
    )(*g, normed_t, w, b)


def split_kernel(s_ref, *refs):
    offset, core = s_ref[0], s_ref[1]
    pairs = (len(refs) - 1) // 3
    rows, lon, lev, width = refs[1].shape
    many = (rows + WLAT) // 2
    half = lon * lev
    cells = 2 * WLAT * half
    for rel in range(2):
        base = many * (core ^ rel) - offset

        def body(w, carry):
            at = pl.ds(pl.multiple_of(w * cells, 16), cells)
            for i in range(pairs):
                up_ref, low_ref = refs[2 * i : 2 * i + 2]
                parts = []
                for ref, part in ((up_ref, slice(up_ref.shape[1] - lon, up_ref.shape[1])), (low_ref, slice(0, lon))):
                    for j in range(WLAT):
                        r = base + WLAT * w + j
                        v = ref[jnp.clip(r, 0, rows - 1), part].astype(F32).reshape(half, width)
                        parts.append(jnp.where((r >= 0) & (r < rows), v, 0.0))
                block = jnp.concatenate(parts, axis=0).astype(BF)
                if rel:
                    refs[-1][i, at, :] = block
                else:
                    refs[2 * pairs + i][at, :] = block
            return carry

        lax.fori_loop(0, many // WLAT, body, 0)


def split(place, *halves):
    rows, lon, lev, width = halves[1].shape
    pairs = len(halves) // 2
    n = (rows + WLAT) * lon * lev
    return pl.pallas_call(
        split_kernel,
        out_shape=(jax.ShapeDtypeStruct((n, width), BF),) * pairs
        + (jax.ShapeDtypeStruct((pairs, n, width), BF),),
        in_specs=[pl.BlockSpec(memory_space=pltpu.SMEM)] + spec(2 * pairs),
        out_specs=tuple(spec(pairs + 1)),
        compiler_params=params(16),
        cost_estimate=SMALL,
    )(place, *halves)


def cell_at(c, window):
    cells = 2 * WLAT * window
    w = sum((c >= i * cells).astype(jnp.int32) for i in range(1, 4))
    c = c - w * cells
    s = (c >= WLAT * window).astype(jnp.int32)
    c = c - s * WLAT * window
    r = sum((c >= i * window).astype(jnp.int32) for i in range(1, WLAT))
    c = c - r * window
    return w * WLAT + r, s * (window // 2) + (c >> 1), c & 1


def ids_kernel(s_ref, ids_ref, idk_ref, idq_ref):
    offset, core, sector = s_ref[0], s_ref[1], s_ref[2]
    rows, lev, total = ids_ref.shape
    n = idk_ref.shape[0]
    cells = n // 4
    window = cells // (2 * WLAT)
    many = (rows + WLAT) // 2
    ids = ids_ref[...].astype(F32).reshape(rows * lev, total)

    def find(c):
        r, lon, level = cell_at(c, window)
        r = r + many * core - offset
        lon = lon + sector * window + window // 2
        lon = jnp.where(lon >= total, lon - total, lon)
        valid = (r >= 0) & (r < rows)
        return jnp.where(valid, 2 * r + level, -1), lon, valid

    spot, lon, valid = find(lax.broadcasted_iota(jnp.int32, (n, 1), 0))
    at = lax.broadcasted_iota(jnp.int32, (n, rows * lev), 1) == spot
    found = jnp.dot(jnp.where(at, 1.0, 0.0), ids, preferred_element_type=F32)
    there = lax.broadcasted_iota(jnp.int32, (n, total), 1) == lon
    found = jnp.sum(jnp.where(there, found, 0.0), axis=1, keepdims=True)
    idk_ref[...] = jnp.where(valid, found, -1.0).astype(jnp.int32)
    for w in range(4):
        lane = lax.broadcasted_iota(jnp.int32, (1, 2 * cells), 1)
        spot, lon, valid = find(w * cells + jnp.where(lane >= cells, lane - cells, lane))
        there = lax.broadcasted_iota(jnp.int32, (total, 2 * cells), 0) == lon
        found = jnp.dot(ids, jnp.where(there, 1.0, 0.0), preferred_element_type=F32)
        at = lax.broadcasted_iota(jnp.int32, (rows * lev, 2 * cells), 0) == spot
        found = jnp.sum(jnp.where(at, found, 0.0), axis=0, keepdims=True)
        idq_ref[w] = jnp.where(valid, found, -1.0).astype(jnp.int32)


def window_ids(place, ids, cells):
    return pl.pallas_call(
        ids_kernel,
        out_shape=(
            jax.ShapeDtypeStruct((4 * cells, 1), jnp.int32),
            jax.ShapeDtypeStruct((4, 1, 2 * cells), jnp.int32),
        ),
        in_specs=[pl.BlockSpec(memory_space=pltpu.SMEM)] + spec(1),
        out_specs=tuple(spec(2)),
        compiler_params=params(16),
        cost_estimate=SMALL,
    )(place, ids)


def join_kernel(s_ref, a0, a1, b0, b1, out_ref, grid_ref):
    offset, core = s_ref[0], s_ref[1]
    rows, lon, lev, width = out_ref.shape
    many = (rows + WLAT) // 2
    half = lon * lev // 2
    for rel, ins in ((0, (a0, a1)), (1, (b0, b1))):
        base = many * (core ^ rel)
        for s in range(2):
            for i in range(many // 4):
                v = ins[s][4 * half * i : 4 * half * (i + 1), :].astype(F32)
                for j in range(4):
                    grid_ref[base + 4 * i + j, half * (1 - s) : half * (2 - s), :] = v[
                        half * j : half * (j + 1)
                    ]

    def body(i, carry):
        for j in range(2):
            r = 2 * i + j
            out_ref[r] = grid_ref[r + offset].reshape(lon, lev, width).astype(BF)
        return carry

    lax.fori_loop(0, rows // 2, body, 0)


def join(place, parts, rows, lon, lev):
    n, width = parts[0].shape
    out = pl.pallas_call(
        join_kernel,
        out_shape=jax.ShapeDtypeStruct((rows, lon, lev, width), BF),
        in_specs=[pl.BlockSpec(memory_space=pltpu.SMEM)] + spec(4),
        out_specs=spec(1)[0],
        scratch_shapes=[pltpu.VMEM((rows + WLAT, lon * lev, width), F32)],
        compiler_params=params(16),
        cost_estimate=SMALL,
    )(place, *parts)
    return jnp.transpose(out, (0, 2, 1, 3))


def send(block, shift, flip):
    count, tp = lax.axis_size("lat"), lax.axis_size("tp")
    route = [
        (u * tp + t, ((u + shift) % count) * tp + (t ^ flip)) for u in range(count) for t in range(tp)
    ]
    return lax.ppermute(block, ("lat", "tp"), route)


def swap(block, other, flip):
    count, tp = lax.axis_size("lat"), lax.axis_size("tp")
    route = [(u * tp + t, (u ^ other) * tp + (t ^ flip)) for u in range(count) for t in range(tp)]
    return lax.ppermute(block, ("lat", "tp"), route)


def lat_terms(block, bit):
    count = lax.axis_size("lat")
    terms = [block]
    while bit < count:
        block = added(terms)
        terms = [block, swap(block, bit, 0)]
        if 4 * bit <= count:
            terms += [swap(block, 2 * bit, 0), swap(block, 3 * bit, 0)]
        bit *= len(terms)
    return terms


def added(terms):
    while len(terms) > 1:
        terms = [a + b for a, b in zip(terms[::2], terms[1::2])]
    return terms[0]


def after(block, *others):
    return lax.optimization_barrier((block, *others))[0]


def local(features, target, w_qkv, w_proj, qkv_clip, proj_clip, shift_offset, region_ids):
    rows, lev, lon, width = features.shape
    half = lon // 2
    sector = lax.axis_index("lat")
    t = lax.axis_index("tp")
    t_arr = jnp.reshape(t, (1,)).astype(jnp.int32)
    place = jnp.stack([shift_offset[0], t % 2, sector]).astype(jnp.int32)

    f_raw, t_raw = (jnp.transpose(block, (0, 2, 1, 3)) for block in (features, target))
    f_low, w_qkv, w_proj = lax.optimization_barrier((f_raw[:, :half], w_qkv, w_proj))
    f_up_y = send(after(f_raw, f_low)[:, half:], 0, 2)
    f_low = send(f_low, -1, 0)

    w3 = jnp.transpose(w_qkv, (1, 0, 2))
    c3 = jnp.transpose(qkv_clip, (1, 0, 2))
    w3_peer = send(w3, 0, 1)
    c3_peer = send(c3, 0, 1)
    share = w_proj.shape[0] // 2
    slab = after(w_proj, c3_peer)
    slab = send(lax.dynamic_slice_in_dim(slab, share * (sector % 2), share, 0), 0, 2)
    w1 = send(w_proj, 0, 1)
    wc_own, b_own = clip_qkv(w3, c3)
    wc_peer, b_peer = clip_qkv(w3_peer, c3_peer)
    idk, idq = window_ids(place, region_ids, WLAT * lev * lon)
    f_low, f_up_y, w1, wc_own, wc_peer, idk, idq = lax.optimization_barrier(
        (f_low, f_up_y, w1, wc_own, wc_peer, idk, idq)
    )
    f_low_y = send(f_low, 0, 2)
    t_low = send(after(t_raw, f_low)[:, :half], -1, 0)
    t_own, t_away = split(place, t_raw, t_low)
    t_away = t_away.reshape(t_own.shape)
    t_1 = send(t_away, 0, 1)
    f_low_y, t_own, t_away, slab = lax.optimization_barrier((f_low_y, t_own, t_away, slab))
    x_0, x_2, x_away = split(place, f_raw, f_low, f_up_y, f_low_y)
    pieces = (x_0, x_2, send(x_away, 0, 1))

    targets = (t_own, t_1, send(t_own, 0, 2), send(t_away, 0, 3))
    more = swap(slab, 1, 0)

    normed, qkv, attn_0 = forward(t_arr, pieces, wc_own, wc_peer, idk, idq)
    other_0 = send(attn_0, 0, 2)
    probs_0 = probs_of(0, qkv, idk, idq)
    attn_1 = last_windows(after(qkv, probs_0, *targets, more), idk, idq)
    slab_3, more_3 = send(after(slab, attn_1), 0, 1), send(after(more, attn_1), 0, 1)
    pc, pb = clip_proj(place, [w_proj, w1, slab, more, slab_3, more_3], proj_clip)
    other_1 = send(attn_1, 0, 2)
    normed_t, attn_t = turn(normed, (attn_0, attn_1))
    probs = (probs_0, probs_of(1, after(qkv, attn_1), idk, idq))

    *mixed, err_0 = output(t_arr, pieces, targets, attn_0, other_0, pc, idk)
    grads_0 = backward(0, err_0, pc, qkv, probs[0])
    other_1 = after(other_1, grads_0)
    m00, m01, m10, m11, err_1 = output(t_arr, pieces, targets, attn_1, other_1, pc, idk, mixed)
    m01 = send(m01, 0, 1)
    m10 = send(m10, 1, 0)
    m11 = send(m11, 1, 1)
    proj = proj_sums((err_0, err_1), attn_t, w_proj, w1, pb)
    proj_y = send(proj, 0, 2)
    grads = (grads_0, backward(1, err_1, pc, qkv, probs[1]))
    peer = qkv_sums(1, grads, normed_t, w3_peer, b_peer)
    proj = proj + proj_y
    peer = jnp.concatenate([peer, proj], axis=1)
    terms = [send(peer, 0, 1), swap(peer, 1, 1)]
    grads = lax.optimization_barrier((*grads, m01, m10, m11, peer))[:2]
    own = qkv_sums(0, grads, normed_t, w3, b_own)
    own = jnp.concatenate([own, proj], axis=1)
    sums = added([own, terms[0], swap(own, 1, 0), terms[1]])
    sums = added(lat_terms(sums, 2))
    mixed = join(place, [m00, m10, m01, m11], rows, lon, lev)
    return (mixed, sums[:, : 3 * width].reshape(2, 3, width), sums[:, 3 * width :])


def solution(mesh):
    placed = (
        P(None, None, "lat", "tp"),
        P(None, None, "lat", "tp"),
        P(None, None, "tp"),
        P("tp", None),
        P(None, None, "tp"),
        P(),
        P(),
        P(),
    )
    return jax.shard_map(
        local,
        mesh=mesh,
        in_specs=placed,
        out_specs=(P(None, None, "lat", "tp"), P(None, None, "tp"), P()),
        check_vma=False,
    )
```

```python
import functools

import jax
import jax.numpy as jnp
from jax import lax
from jax.experimental import pallas as pl
from jax.experimental.pallas import tpu as pltpu
from jax.sharding import PartitionSpec as P

HD = 64
WLAT = 6
EPS = 1e-05
NEG = -1e30
F32 = jnp.float32
BF = jnp.bfloat16
SCALE = HD ** (-0.5)
NT = (((1,), (1,)), ((), ()))
TN = (((0,), (0,)), ((), ()))
LARGE = pl.CostEstimate(flops=8 * 10**9, bytes_accessed=10**7, transcendentals=10**6)
SMALL = pl.CostEstimate(flops=1, bytes_accessed=1, transcendentals=0)


def spec(n):
    return [pl.BlockSpec(memory_space=pltpu.VMEM)] * n


def params(mib):
    return pltpu.CompilerParams(vmem_limit_bytes=mib * 1024 * 1024)


def bounds_of(weight, logits_hi, logits_lo):
    top = jnp.max(weight, axis=0, keepdims=True)
    low = jnp.min(weight, axis=0, keepdims=True)
    hi = 1.0 / (1.0 + jnp.exp(-logits_hi))
    lo = 1.0 / (1.0 + jnp.exp(-logits_lo))
    return hi * top, lo * low, hi * (1.0 - hi) * top, lo * (1.0 - lo) * low


def clip_qkv_kernel(w_ref, c_ref, wc_ref, b_ref):
    def body(i, carry):
        w = w_ref[i].astype(F32)
        up, lw, fh, fl = bounds_of(w, c_ref[i, 0:1], c_ref[i, 1:2])
        wc_ref[i] = jnp.minimum(jnp.maximum(w, lw), up).astype(BF)
        b_ref[i, 0:1] = up
        b_ref[i, 1:2] = lw
        b_ref[i, 2:3] = fh
        b_ref[i, 3:4] = fl
        return carry

    lax.fori_loop(0, 3, body, 0)


def clip_qkv(w, clips):
    n, d, e = w.shape
    return pl.pallas_call(
        clip_qkv_kernel,
        out_shape=(
            jax.ShapeDtypeStruct((n, d, e), BF),
            jax.ShapeDtypeStruct((n, 8, e), F32),
        ),
        in_specs=spec(2),
        out_specs=tuple(spec(2)),
        compiler_params=params(24),
        cost_estimate=SMALL,
    )(w, clips)


def clip_proj_kernel(s_ref, w0, w1, a2, b2, a3, b3, c_ref, wc_ref, b_ref):
    second = s_ref[2] % 2 == 1

    def body(i, carry):
        cols = pl.ds(pl.multiple_of(i * 256, 256), 256)
        parts = [w0[:, cols].astype(F32), w1[:, cols].astype(F32)]
        for first_ref, other_ref in ((a2, b2), (a3, b3)):
            a, b = first_ref[:, cols].astype(F32), other_ref[:, cols].astype(F32)
            parts += [jnp.where(second, b, a), jnp.where(second, a, b)]
        w = jnp.concatenate(parts, axis=0)
        up, lw, fh, fl = bounds_of(w, c_ref[0:1, cols], c_ref[1:2, cols])
        wc = jnp.minimum(jnp.maximum(w, lw), up).astype(BF)
        wc_ref[:, cols] = wc
        b_ref[0:1, cols] = up
        b_ref[1:2, cols] = lw
        b_ref[2:3, cols] = fh
        b_ref[3:4, cols] = fl
        return carry

    lax.fori_loop(0, w0.shape[1] // 256, body, 0)


def clip_proj(place, shards, clips):
    e, d = shards[0].shape
    return pl.pallas_call(
        clip_proj_kernel,
        out_shape=(
            jax.ShapeDtypeStruct((4 * e, d), BF),
            jax.ShapeDtypeStruct((8, d), F32),
        ),
        in_specs=[pl.BlockSpec(memory_space=pltpu.SMEM)] + spec(7),
        out_specs=tuple(spec(2)),
        compiler_params=params(24),
        cost_estimate=SMALL,
    )(place, *shards, clips)


def stacked(block, mask_a, mask_b):
    return jnp.concatenate([block * mask_a, block * mask_b], axis=0)


def head_masks():
    lane = lax.broadcasted_iota(jnp.int32, (1, 2 * HD), 1)
    mask_a = jnp.where(lane < HD, 1.0, 0.0).astype(BF)
    mask_b = jnp.where(lane < HD, 0.0, 1.0).astype(BF)
    return mask_a, mask_b


def probs_t(k, q2, allowed):
    st = lax.dot_general(k, q2, NT, preferred_element_type=F32) * SCALE
    st = jnp.where(allowed, st, NEG)
    e = jnp.exp(st - jnp.max(st, axis=0, keepdims=True))
    return e * (1.0 / jnp.sum(e, axis=0, keepdims=True))


def merge_heads(t_block):
    both = t_block.T
    n = both.shape[0] // 2
    lane = lax.broadcasted_iota(jnp.int32, (n, 2 * HD), 1)
    return jnp.where(lane < HD, both[:n], both[n:])


def allowed_t(idk_ref, idq_ref, w, cells):
    rows = pl.ds(pl.multiple_of(w * cells, 16), cells)
    idk = idk_ref[rows, :]
    return (idk == idq_ref[w]) & (idk >= 0)


def blocks(refs):
    own, other, away = refs
    return own, away.at[0], other, away.at[1]


def forward_kernel(t_ref, *refs):
    pieces = blocks(refs[:3])
    wo_ref, wp_ref, idk_ref, idq_ref, normed_ref, qkv_ref, attn_ref = refs[3:]
    t = t_ref[0]
    n, width = pieces[0].shape
    d = 4 * width

    def norm(w, carry):
        rows = pl.ds(pl.multiple_of(w * 48, 16), 48)
        x = [r[rows, :].astype(F32) for r in pieces]
        mean = sum(jnp.sum(b, axis=-1, keepdims=True) for b in x) / d
        x = [b - mean for b in x]
        var = sum(jnp.sum(b * b, axis=-1, keepdims=True) for b in x) / d
        scale = lax.rsqrt(var + EPS)
        for k in range(4):
            cols = pl.ds(pl.multiple_of((t ^ k) * width, width), width)
            normed_ref[rows, cols] = (x[k] * scale).astype(BF)
        return carry

    lax.fori_loop(0, n // 48, norm, 0)

    def project(i, carry):
        for g, w_ref in enumerate((wo_ref, wp_ref)):
            qkv_ref[3 * g + i] = jnp.dot(
                normed_ref[...], w_ref[i], preferred_element_type=F32
            ).astype(BF)
        return carry

    lax.fori_loop(0, 3, project, 0)
    attend(qkv_ref, idk_ref, idq_ref, attn_ref, 0, 2)


def attend(qkv_ref, idk_ref, idq_ref, attn_ref, first, last):
    mask_a, mask_b = head_masks()
    cells = idk_ref.shape[0] // 4

    def window(w, carry):
        rows = pl.ds(pl.multiple_of(w * cells, 16), cells)
        to = pl.ds(pl.multiple_of((w - first) * cells, 16), cells)
        allowed = allowed_t(idk_ref, idq_ref, w, cells)
        for hp in range(4):
            g, lanes = hp // 2, slice(128 * (hp % 2), 128 * (hp % 2) + 128)
            q2 = stacked(qkv_ref[3 * g, rows, lanes], mask_a, mask_b)
            pt = probs_t(qkv_ref[3 * g + 1, rows, lanes], q2, allowed)
            ot = lax.dot_general(
                qkv_ref[3 * g + 2, rows, lanes], pt.astype(BF), TN, preferred_element_type=F32
            )
            attn_ref[to, 128 * hp : 128 * hp + 128] = merge_heads(ot).astype(BF)
        return carry

    lax.fori_loop(first, last, window, 0)


def last_kernel(qkv_ref, idk_ref, idq_ref, attn_ref):
    attend(qkv_ref, idk_ref, idq_ref, attn_ref, 2, 4)


def last_windows(qkv, idk, idq):
    n, width = qkv.shape[1:]
    return pl.pallas_call(
        last_kernel,
        out_shape=jax.ShapeDtypeStruct((n // 2, 2 * width), BF),
        in_specs=spec(3),
        out_specs=spec(1)[0],
        compiler_params=params(16),
        cost_estimate=pl.CostEstimate(flops=1, bytes_accessed=1, transcendentals=0),
    )(qkv, idk, idq)


def forward(t, pieces, wo, wp, idk, idq):
    n, width = pieces[0].shape
    d = 4 * width
    return pl.pallas_call(
        forward_kernel,
        out_shape=(
            jax.ShapeDtypeStruct((n, d), BF),
            jax.ShapeDtypeStruct((6, n, width), BF),
            jax.ShapeDtypeStruct((n // 2, 2 * width), BF),
        ),
        in_specs=[pl.BlockSpec(memory_space=pltpu.SMEM)] + spec(7),
        out_specs=tuple(spec(3)),
        compiler_params=params(20),
        cost_estimate=pl.CostEstimate(flops=8 * 10**9, bytes_accessed=10 * 10**6, transcendentals=10**6),
    )(t, *pieces, wo, wp, idk, idq)


def turn_kernel(normed_ref, a_ref, b_ref, normed_t, attn_t):
    d = normed_ref.shape[1]

    def body(i, carry):
        cols = pl.ds(pl.multiple_of(i * 256, 256), 256)
        normed_t[cols, :] = normed_ref[:, cols].T
        return carry

    lax.fori_loop(0, d // 256, body, 0)

    def body2(i, carry):
        cols = pl.ds(pl.multiple_of(i * 256, 256), 256)
        attn_t[cols, :] = jnp.concatenate([a_ref[:, cols], b_ref[:, cols]], axis=0).T
        return carry

    lax.fori_loop(0, a_ref.shape[1] // 256, body2, 0)


def turn(normed, attn):
    n, d = normed.shape
    e = attn[0].shape[1]
    return pl.pallas_call(
        turn_kernel,
        out_shape=(jax.ShapeDtypeStruct((d, n), BF), jax.ShapeDtypeStruct((e, n), BF)),
        in_specs=spec(3),
        out_specs=tuple(spec(2)),
        compiler_params=params(16),
        cost_estimate=SMALL,
    )(normed, *attn)


def output_kernel(group, t_ref, *refs):
    pieces, targets = blocks(refs[:3]), refs[3:7]
    own_ref, other_ref, wc_ref, idk_ref = refs[7:11]
    before, refs = refs[11 : 11 + 4 * group], refs[11 + 4 * group :]
    mixed, err_ref, y_ref = refs[:4], refs[4], refs[5]
    t = t_ref[0]
    n, width = pieces[0].shape
    cells = n // 4
    half = cells // 2
    e = own_ref.shape[1]
    for old, new in zip(before, mixed):
        new[: group * cells, :] = old[...]
    for k in range(4):
        x_ref, want_ref = pieces[k], targets[k]
        cols = pl.ds(pl.multiple_of((t ^ k) * width, width), width)
        y_ref[...] = jnp.dot(own_ref[...], wc_ref[:e, cols], preferred_element_type=F32) + jnp.dot(
            other_ref[...], wc_ref[e:, cols], preferred_element_type=F32
        )
        ys = []
        for i in range(2):
            at = slice(cells * i, cells * (i + 1))
            rows = slice(cells * (2 * group + i), cells * (2 * group + i + 1))
            y = x_ref[rows, :].astype(F32) + y_ref[at, :]
            ys.append(y)
            err = y - want_ref[rows, :].astype(F32)
            valid = idk_ref[rows, :] >= 0
            err_ref[at, cols] = jnp.where(valid, err, 0.0).astype(BF)
        if k < 2:
            at = slice(cells * group, cells * (group + 1))
            for s in range(2):
                part = slice(half * s, half * (s + 1))
                mixed[2 * s + k][at, :] = jnp.concatenate([y[part] for y in ys], axis=0).astype(BF)


def output(t, pieces, targets, own, other, wc, idk, before=()):
    n, width = pieces[0].shape
    group = 1 if before else 0
    piece = jax.ShapeDtypeStruct((n // 4 * (1 + group), width), BF)
    return pl.pallas_call(
        functools.partial(output_kernel, group),
        out_shape=(piece, piece, piece, piece, jax.ShapeDtypeStruct((n // 2, 4 * width), BF)),
        in_specs=[pl.BlockSpec(memory_space=pltpu.SMEM)] + spec(11 + len(before)),
        out_specs=tuple(spec(5)),
        scratch_shapes=[pltpu.VMEM((n // 2, width), F32)],
        compiler_params=params(20),
        cost_estimate=SMALL,
    )(t, *pieces, *targets, own, other, wc, idk, *before)


def probs_kernel(group, qkv_ref, idk_ref, idq_ref, p_ref):
    cells = idk_ref.shape[0] // 4
    mask_a, mask_b = head_masks()

    def window(i, carry):
        w = 2 * group + i
        rows = pl.ds(pl.multiple_of(w * cells, 16), cells)
        allowed = allowed_t(idk_ref, idq_ref, w, cells)
        for hp in range(4):
            g, lanes = hp // 2, slice(128 * (hp % 2), 128 * (hp % 2) + 128)
            q2 = stacked(qkv_ref[3 * g, rows, lanes], mask_a, mask_b)
            p_ref[4 * i + hp] = probs_t(qkv_ref[3 * g + 1, rows, lanes], q2, allowed)
        return carry

    lax.fori_loop(0, 2, window, 0)


def probs_of(group, qkv, idk, idq):
    n, width = qkv.shape[1:]
    return pl.pallas_call(
        functools.partial(probs_kernel, group),
        out_shape=jax.ShapeDtypeStruct((8, n // 4, n // 2), F32),
        in_specs=spec(3),
        out_specs=spec(1)[0],
        compiler_params=params(16),
        cost_estimate=SMALL,
    )(qkv, idk, idq)


def masked_sums(grad, w, bounds):
    g_hi = jnp.sum(jnp.where(w > bounds[0:1], grad, 0.0), axis=0, keepdims=True) * bounds[2:3]
    g_lo = jnp.sum(jnp.where(w < bounds[1:2], grad, 0.0), axis=0, keepdims=True) * bounds[3:4]
    return g_hi, g_lo


def proj_sums_kernel(e0_ref, e1_ref, attn_t, po_ref, pp_ref, pb_ref, proj_ref):
    def proj_part(i, carry):
        cols = pl.ds(pl.multiple_of(i * 256, 256), 256)
        err = jnp.concatenate([e0_ref[:, cols], e1_ref[:, cols]], axis=0)
        grad = jnp.dot(attn_t[...], err, preferred_element_type=F32)
        n = po_ref.shape[0]
        b = pb_ref[:, cols]
        h0, l0 = masked_sums(grad[:n], po_ref[:, cols].astype(F32), b)
        h1, l1 = masked_sums(grad[n:], pp_ref[:, cols].astype(F32), b)
        proj_ref[0:1, cols] = h0 + h1
        proj_ref[1:2, cols] = l0 + l1
        return carry

    lax.fori_loop(0, 4, proj_part, 0)


def proj_sums(errs, attn_t, po, pp, pb):
    return pl.pallas_call(
        proj_sums_kernel,
        out_shape=jax.ShapeDtypeStruct((2, errs[0].shape[1]), F32),
        in_specs=spec(6),
        out_specs=spec(1)[0],
        compiler_params=params(16),
        cost_estimate=pl.CostEstimate(flops=10**9, bytes_accessed=3 * 10**6, transcendentals=0),
    )(*errs, attn_t, po, pp, pb)


def backward_kernel(group, err_ref, wc_ref, qkv_ref, p_ref, g_ref, d_ref):
    e = d_ref.shape[1]
    cells = d_ref.shape[0] // 2
    d_ref[...] = lax.dot_general(err_ref[...], wc_ref[:e], NT, preferred_element_type=F32).astype(BF)
    mask_a, mask_b = head_masks()

    def window(i, carry):
        rows = pl.ds(pl.multiple_of((2 * group + i) * cells, 16), cells)
        at = pl.ds(pl.multiple_of(i * cells, 16), cells)
        for hp in range(4):
            g, lanes = hp // 2, slice(128 * (hp % 2), 128 * (hp % 2) + 128)
            q2 = stacked(qkv_ref[3 * g, rows, lanes], mask_a, mask_b)
            k = qkv_ref[3 * g + 1, rows, lanes]
            v = qkv_ref[3 * g + 2, rows, lanes]
            pt = p_ref[4 * i + hp]
            d2 = stacked(d_ref[at, 128 * hp : 128 * hp + 128], mask_a, mask_b)
            g_ref[3 * g + 2, at, lanes] = jnp.dot(
                pt.astype(BF), d2, preferred_element_type=F32
            ).astype(BF)
            dpt = lax.dot_general(v, d2, NT, preferred_element_type=F32)
            gst = (pt * (dpt - jnp.sum(pt * dpt, axis=0, keepdims=True))).astype(BF)
            g_ref[3 * g + 1, at, lanes] = (
                jnp.dot(gst, q2, preferred_element_type=F32) * SCALE
            ).astype(BF)
            gqt = lax.dot_general(k, gst, TN, preferred_element_type=F32) * SCALE
            g_ref[3 * g, at, lanes] = merge_heads(gqt).astype(BF)
        return carry

    lax.fori_loop(0, 2, window, 0)


def backward(group, err, wc, qkv, probs):
    n, width = qkv.shape[1:]
    return pl.pallas_call(
        functools.partial(backward_kernel, group),
        out_shape=jax.ShapeDtypeStruct((6, n // 2, width), BF),
        in_specs=spec(4),
        out_specs=spec(1)[0],
        scratch_shapes=[pltpu.VMEM((n // 2, 2 * width), BF)],
        compiler_params=params(20),
        cost_estimate=LARGE if group else SMALL,
    )(err, wc, qkv, probs)


def qkv_sums_kernel(side, g0_ref, g1_ref, normed_t, w_ref, b_ref, to_ref):
    width = g0_ref.shape[2]

    def qkv_part(i, carry):
        cells = jnp.concatenate([g0_ref[3 * side + i], g1_ref[3 * side + i]], axis=0)
        grad = jnp.dot(normed_t[...], cells, preferred_element_type=F32)
        hi, lo = masked_sums(grad, w_ref[i].astype(F32), b_ref[i])
        to_ref[0:1, pl.ds(pl.multiple_of(i * width, width), width)] = hi
        to_ref[1:2, pl.ds(pl.multiple_of(i * width, width), width)] = lo
        return carry

    lax.fori_loop(0, 3, qkv_part, 0)


def qkv_sums(side, g, normed_t, w, b):
    width = g[0].shape[2]
    return pl.pallas_call(
        functools.partial(qkv_sums_kernel, side),
        out_shape=jax.ShapeDtypeStruct((2, 3 * width), F32),
        in_specs=spec(5),
        out_specs=spec(1)[0],
        compiler_params=params(20),
        cost_estimate=LARGE,
    )(*g, normed_t, w, b)


def halves_kernel(x_ref, low_ref, up_ref, sems):
    half = low_ref.shape[1]
    low = pltpu.make_async_copy(x_ref.at[:, :half], low_ref, sems.at[0])
    up = pltpu.make_async_copy(x_ref.at[:, half:], up_ref, sems.at[1])
    low.start()
    up.start()
    low.wait()
    up.wait()


def halves_of(block):
    rows, lon, lev, width = block.shape
    half = jax.ShapeDtypeStruct((rows, lon // 2, lev, width), BF)
    return pl.pallas_call(
        halves_kernel,
        out_shape=(half, half),
        in_specs=[pl.BlockSpec(memory_space=pltpu.HBM)],
        out_specs=tuple(spec(2)),
        scratch_shapes=[pltpu.SemaphoreType.DMA((2,))],
        compiler_params=params(16),
        cost_estimate=SMALL,
    )(block)


def split_kernel(s_ref, *refs):
    offset, core = s_ref[0], s_ref[1]
    pairs = (len(refs) - 1) // 3
    rows, lon, lev, width = refs[1].shape
    many = (rows + WLAT) // 2
    half = lon * lev
    cells = 2 * WLAT * half
    for rel in range(2):
        base = many * (core ^ rel) - offset

        def body(w, carry):
            at = pl.ds(pl.multiple_of(w * cells, 16), cells)
            for i in range(pairs):
                up_ref, low_ref = refs[2 * i : 2 * i + 2]
                parts = []
                for ref, part in ((up_ref, slice(up_ref.shape[1] - lon, up_ref.shape[1])), (low_ref, slice(0, lon))):
                    for j in range(WLAT):
                        r = base + WLAT * w + j
                        v = ref[jnp.clip(r, 0, rows - 1), part].astype(F32).reshape(half, width)
                        parts.append(jnp.where((r >= 0) & (r < rows), v, 0.0))
                block = jnp.concatenate(parts, axis=0).astype(BF)
                if rel:
                    refs[-1][i, at, :] = block
                else:
                    refs[2 * pairs + i][at, :] = block
            return carry

        lax.fori_loop(0, many // WLAT, body, 0)


def split(place, *halves):
    rows, lon, lev, width = halves[1].shape
    pairs = len(halves) // 2
    n = (rows + WLAT) * lon * lev
    return pl.pallas_call(
        split_kernel,
        out_shape=(jax.ShapeDtypeStruct((n, width), BF),) * pairs
        + (jax.ShapeDtypeStruct((pairs, n, width), BF),),
        in_specs=[pl.BlockSpec(memory_space=pltpu.SMEM)] + spec(2 * pairs),
        out_specs=tuple(spec(pairs + 1)),
        compiler_params=params(16),
        cost_estimate=SMALL,
    )(place, *halves)


def cell_at(c, window):
    cells = 2 * WLAT * window
    w = sum((c >= i * cells).astype(jnp.int32) for i in range(1, 4))
    c = c - w * cells
    s = (c >= WLAT * window).astype(jnp.int32)
    c = c - s * WLAT * window
    r = sum((c >= i * window).astype(jnp.int32) for i in range(1, WLAT))
    c = c - r * window
    return w * WLAT + r, s * (window // 2) + (c >> 1), c & 1


def ids_kernel(s_ref, ids_ref, idk_ref, idq_ref):
    offset, core, sector = s_ref[0], s_ref[1], s_ref[2]
    rows, lev, total = ids_ref.shape
    n = idk_ref.shape[0]
    cells = n // 4
    window = cells // (2 * WLAT)
    many = (rows + WLAT) // 2
    ids = ids_ref[...].astype(F32).reshape(rows * lev, total)

    def find(c):
        r, lon, level = cell_at(c, window)
        r = r + many * core - offset
        lon = lon + sector * window + window // 2
        lon = jnp.where(lon >= total, lon - total, lon)
        valid = (r >= 0) & (r < rows)
        return jnp.where(valid, 2 * r + level, -1), lon, valid

    spot, lon, valid = find(lax.broadcasted_iota(jnp.int32, (n, 1), 0))
    at = lax.broadcasted_iota(jnp.int32, (n, rows * lev), 1) == spot
    found = jnp.dot(jnp.where(at, 1.0, 0.0), ids, preferred_element_type=F32)
    there = lax.broadcasted_iota(jnp.int32, (n, total), 1) == lon
    found = jnp.sum(jnp.where(there, found, 0.0), axis=1, keepdims=True)
    idk_ref[...] = jnp.where(valid, found, -1.0).astype(jnp.int32)
    for w in range(4):
        lane = lax.broadcasted_iota(jnp.int32, (1, 2 * cells), 1)
        spot, lon, valid = find(w * cells + jnp.where(lane >= cells, lane - cells, lane))
        there = lax.broadcasted_iota(jnp.int32, (total, 2 * cells), 0) == lon
        found = jnp.dot(ids, jnp.where(there, 1.0, 0.0), preferred_element_type=F32)
        at = lax.broadcasted_iota(jnp.int32, (rows * lev, 2 * cells), 0) == spot
        found = jnp.sum(jnp.where(at, found, 0.0), axis=0, keepdims=True)
        idq_ref[w] = jnp.where(valid, found, -1.0).astype(jnp.int32)


def window_ids(place, ids, cells):
    return pl.pallas_call(
        ids_kernel,
        out_shape=(
            jax.ShapeDtypeStruct((4 * cells, 1), jnp.int32),
            jax.ShapeDtypeStruct((4, 1, 2 * cells), jnp.int32),
        ),
        in_specs=[pl.BlockSpec(memory_space=pltpu.SMEM)] + spec(1),
        out_specs=tuple(spec(2)),
        compiler_params=params(16),
        cost_estimate=SMALL,
    )(place, ids)


def join_kernel(s_ref, a0, a1, b0, b1, out_ref, grid_ref):
    offset, core = s_ref[0], s_ref[1]
    rows, lon, lev, width = out_ref.shape
    many = (rows + WLAT) // 2
    half = lon * lev // 2
    for rel, ins in ((0, (a0, a1)), (1, (b0, b1))):
        base = many * (core ^ rel)
        for s in range(2):
            for i in range(many // 4):
                v = ins[s][4 * half * i : 4 * half * (i + 1), :].astype(F32)
                for j in range(4):
                    grid_ref[base + 4 * i + j, half * (1 - s) : half * (2 - s), :] = v[
                        half * j : half * (j + 1)
                    ]

    def body(i, carry):
        for j in range(2):
            r = 2 * i + j
            out_ref[r] = grid_ref[r + offset].reshape(lon, lev, width).astype(BF)
        return carry

    lax.fori_loop(0, rows // 2, body, 0)


def join(place, parts, rows, lon, lev):
    n, width = parts[0].shape
    out = pl.pallas_call(
        join_kernel,
        out_shape=jax.ShapeDtypeStruct((rows, lon, lev, width), BF),
        in_specs=[pl.BlockSpec(memory_space=pltpu.SMEM)] + spec(4),
        out_specs=spec(1)[0],
        scratch_shapes=[pltpu.VMEM((rows + WLAT, lon * lev, width), F32)],
        compiler_params=params(16),
        cost_estimate=SMALL,
    )(place, *parts)
    return jnp.transpose(out, (0, 2, 1, 3))


def send(block, shift, flip):
    count, tp = lax.axis_size("lat"), lax.axis_size("tp")
    route = [
        (u * tp + t, ((u + shift) % count) * tp + (t ^ flip)) for u in range(count) for t in range(tp)
    ]
    return lax.ppermute(block, ("lat", "tp"), route)


def swap(block, other, flip):
    count, tp = lax.axis_size("lat"), lax.axis_size("tp")
    route = [(u * tp + t, (u ^ other) * tp + (t ^ flip)) for u in range(count) for t in range(tp)]
    return lax.ppermute(block, ("lat", "tp"), route)


def lat_terms(block, bit):
    count = lax.axis_size("lat")
    terms = [block]
    while bit < count:
        block = added(terms)
        terms = [block, swap(block, bit, 0)]
        if 4 * bit <= count:
            terms += [swap(block, 2 * bit, 0), swap(block, 3 * bit, 0)]
        bit *= len(terms)
    return terms


def added(terms):
    while len(terms) > 1:
        terms = [a + b for a, b in zip(terms[::2], terms[1::2])]
    return terms[0]


def after(block, *others):
    return lax.optimization_barrier((block, *others))[0]


def local(features, target, w_qkv, w_proj, qkv_clip, proj_clip, shift_offset, region_ids):
    rows, lev, lon, width = features.shape
    half = lon // 2
    sector = lax.axis_index("lat")
    t = lax.axis_index("tp")
    t_arr = jnp.reshape(t, (1,)).astype(jnp.int32)
    place = jnp.stack([shift_offset[0], t % 2, sector]).astype(jnp.int32)

    f_raw, t_raw = (jnp.transpose(block, (0, 2, 1, 3)) for block in (features, target))
    f_low, f_up = halves_of(f_raw)
    f_low, f_up, w_qkv, w_proj = lax.optimization_barrier((f_low, f_up, w_qkv, w_proj))
    f_low, f_up_y = send(f_low, -1, 0), send(f_up, 0, 2)

    w3 = jnp.transpose(w_qkv, (1, 0, 2))
    c3 = jnp.transpose(qkv_clip, (1, 0, 2))
    w3_peer = send(w3, 0, 1)
    c3_peer = send(c3, 0, 1)
    share = w_proj.shape[0] // 2
    slab = after(w_proj, c3_peer)
    slab = send(lax.dynamic_slice_in_dim(slab, share * (sector % 2), share, 0), 0, 2)
    w1 = send(w_proj, 0, 1)
    wc_own, b_own = clip_qkv(w3, c3)
    wc_peer, b_peer = clip_qkv(w3_peer, c3_peer)
    idk, idq = window_ids(place, region_ids, WLAT * lev * lon)
    f_low, f_up_y, w1 = lax.optimization_barrier((f_low, f_up_y, w1))
    f_low_y = send(f_low, 0, 2)
    t_low = send(after(t_raw, f_low)[:, :half], -1, 0)
    t_own, t_away = split(place, t_raw, t_low)
    t_away = t_away.reshape(t_own.shape)
    t_1 = send(t_away, 0, 1)
    f_low_y, t_own, t_away, slab, wc_own, wc_peer, idk, idq = lax.optimization_barrier(
        (f_low_y, t_own, t_away, slab, wc_own, wc_peer, idk, idq)
    )
    x_0, x_2, x_away = split(place, f_raw, f_low, f_up_y, f_low_y)
    pieces = (x_0, x_2, send(x_away, 0, 1))

    targets = (t_own, t_1, send(t_own, 0, 2), send(t_away, 0, 3))
    more = swap(slab, 1, 0)

    normed, qkv, attn_0 = forward(t_arr, pieces, wc_own, wc_peer, idk, idq)
    other_0 = send(attn_0, 0, 2)
    probs_0 = probs_of(0, qkv, idk, idq)
    attn_1 = last_windows(after(qkv, probs_0, *targets, more), idk, idq)
    slab_3, more_3 = send(after(slab, attn_1), 0, 1), send(after(more, attn_1), 0, 1)
    pc, pb = clip_proj(place, [w_proj, w1, slab, more, slab_3, more_3], proj_clip)
    other_1 = send(attn_1, 0, 2)
    normed_t, attn_t = turn(normed, (attn_0, attn_1))
    probs = (probs_0, probs_of(1, after(qkv, attn_1), idk, idq))

    *mixed, err_0 = output(t_arr, pieces, targets, attn_0, other_0, pc, idk)
    grads_0 = backward(0, err_0, pc, qkv, probs[0])
    other_1 = after(other_1, grads_0)
    m00, m01, m10, m11, err_1 = output(t_arr, pieces, targets, attn_1, other_1, pc, idk, mixed)
    m01 = send(m01, 0, 1)
    m10 = send(m10, 1, 0)
    m11 = send(m11, 1, 1)
    proj = proj_sums((err_0, err_1), attn_t, w_proj, w1, pb)
    proj_y = send(proj, 0, 2)
    grads = (grads_0, backward(1, err_1, pc, qkv, probs[1]))
    peer = qkv_sums(1, grads, normed_t, w3_peer, b_peer)
    proj = proj + proj_y
    peer = jnp.concatenate([peer, proj], axis=1)
    terms = [send(peer, 0, 1), swap(peer, 1, 1)]
    grads = lax.optimization_barrier((*grads, m01, m10, m11, peer))[:2]
    own = qkv_sums(0, grads, normed_t, w3, b_own)
    own = jnp.concatenate([own, proj], axis=1)
    sums = added([own, terms[0], swap(own, 1, 0), terms[1]])
    sums = added(lat_terms(sums, 2))
    mixed = join(place, [m00, m10, m01, m11], rows, lon, lev)
    return (mixed, sums[:, : 3 * width].reshape(2, 3, width), sums[:, 3 * width :])


def solution(mesh):
    placed = (
        P(None, None, "lat", "tp"),
        P(None, None, "lat", "tp"),
        P(None, None, "tp"),
        P("tp", None),
        P(None, None, "tp"),
        P(),
        P(),
        P(),
    )
    return jax.shard_map(
        local,
        mesh=mesh,
        in_specs=placed,
        out_specs=(P(None, None, "lat", "tp"), P(None, None, "tp"), P()),
        check_vma=False,
    )
```

```python
import functools

import jax
import jax.numpy as jnp
from jax import lax
from jax.experimental import pallas as pl
from jax.experimental.pallas import tpu as pltpu
from jax.sharding import PartitionSpec as P

HD = 64
WLAT = 6
EPS = 1e-05
NEG = -1e30
F32 = jnp.float32
BF = jnp.bfloat16
SCALE = HD ** (-0.5)
NT = (((1,), (1,)), ((), ()))
TN = (((0,), (0,)), ((), ()))
LARGE = pl.CostEstimate(flops=8 * 10**9, bytes_accessed=10**7, transcendentals=10**6)
SMALL = pl.CostEstimate(flops=1, bytes_accessed=1, transcendentals=0)


def spec(n):
    return [pl.BlockSpec(memory_space=pltpu.VMEM)] * n


def params(mib):
    return pltpu.CompilerParams(vmem_limit_bytes=mib * 1024 * 1024)


def bounds_of(weight, logits_hi, logits_lo):
    top = jnp.max(weight, axis=0, keepdims=True)
    low = jnp.min(weight, axis=0, keepdims=True)
    hi = 1.0 / (1.0 + jnp.exp(-logits_hi))
    lo = 1.0 / (1.0 + jnp.exp(-logits_lo))
    return hi * top, lo * low, hi * (1.0 - hi) * top, lo * (1.0 - lo) * low


def clip_qkv_kernel(w_ref, c_ref, wc_ref, b_ref):
    def body(i, carry):
        w = w_ref[i].astype(F32)
        up, lw, fh, fl = bounds_of(w, c_ref[i, 0:1], c_ref[i, 1:2])
        wc_ref[i] = jnp.minimum(jnp.maximum(w, lw), up).astype(BF)
        b_ref[i, 0:1] = up
        b_ref[i, 1:2] = lw
        b_ref[i, 2:3] = fh
        b_ref[i, 3:4] = fl
        return carry

    lax.fori_loop(0, 3, body, 0)


def clip_qkv(w, clips):
    n, d, e = w.shape
    return pl.pallas_call(
        clip_qkv_kernel,
        out_shape=(
            jax.ShapeDtypeStruct((n, d, e), BF),
            jax.ShapeDtypeStruct((n, 8, e), F32),
        ),
        in_specs=spec(2),
        out_specs=tuple(spec(2)),
        compiler_params=params(24),
        cost_estimate=SMALL,
    )(w, clips)


def clip_proj_kernel(s_ref, w0, w1, a2, b2, a3, b3, c_ref, wc_ref, b_ref):
    second = s_ref[2] % 2 == 1

    def body(i, carry):
        cols = pl.ds(pl.multiple_of(i * 256, 256), 256)
        parts = [w0[:, cols].astype(F32), w1[:, cols].astype(F32)]
        for first_ref, other_ref in ((a2, b2), (a3, b3)):
            a, b = first_ref[:, cols].astype(F32), other_ref[:, cols].astype(F32)
            parts += [jnp.where(second, b, a), jnp.where(second, a, b)]
        w = jnp.concatenate(parts, axis=0)
        up, lw, fh, fl = bounds_of(w, c_ref[0:1, cols], c_ref[1:2, cols])
        wc = jnp.minimum(jnp.maximum(w, lw), up).astype(BF)
        wc_ref[:, cols] = wc
        b_ref[0:1, cols] = up
        b_ref[1:2, cols] = lw
        b_ref[2:3, cols] = fh
        b_ref[3:4, cols] = fl
        return carry

    lax.fori_loop(0, w0.shape[1] // 256, body, 0)


def clip_proj(place, shards, clips):
    e, d = shards[0].shape
    return pl.pallas_call(
        clip_proj_kernel,
        out_shape=(
            jax.ShapeDtypeStruct((4 * e, d), BF),
            jax.ShapeDtypeStruct((8, d), F32),
        ),
        in_specs=[pl.BlockSpec(memory_space=pltpu.SMEM)] + spec(7),
        out_specs=tuple(spec(2)),
        compiler_params=params(24),
        cost_estimate=SMALL,
    )(place, *shards, clips)


def stacked(block, mask_a, mask_b):
    return jnp.concatenate([block * mask_a, block * mask_b], axis=0)


def head_masks():
    lane = lax.broadcasted_iota(jnp.int32, (1, 2 * HD), 1)
    mask_a = jnp.where(lane < HD, 1.0, 0.0).astype(BF)
    mask_b = jnp.where(lane < HD, 0.0, 1.0).astype(BF)
    return mask_a, mask_b


def probs_t(k, q2, allowed):
    st = lax.dot_general(k, q2, NT, preferred_element_type=F32) * SCALE
    st = jnp.where(allowed, st, NEG)
    e = jnp.exp(st - jnp.max(st, axis=0, keepdims=True))
    return e * (1.0 / jnp.sum(e, axis=0, keepdims=True))


def merge_heads(t_block):
    both = t_block.T
    n = both.shape[0] // 2
    lane = lax.broadcasted_iota(jnp.int32, (n, 2 * HD), 1)
    return jnp.where(lane < HD, both[:n], both[n:])


def allowed_t(idk_ref, idq_ref, w, cells):
    rows = pl.ds(pl.multiple_of(w * cells, 16), cells)
    idk = idk_ref[rows, :]
    return (idk == idq_ref[w]) & (idk >= 0)


def blocks(refs):
    own, other, away = refs
    return own, away.at[0], other, away.at[1]


def forward_kernel(t_ref, *refs):
    pieces = blocks(refs[:3])
    wo_ref, wp_ref, idk_ref, idq_ref, normed_ref, qkv_ref, attn_ref = refs[3:]
    t = t_ref[0]
    n, width = pieces[0].shape
    d = 4 * width

    def norm(w, carry):
        rows = pl.ds(pl.multiple_of(w * 48, 16), 48)
        x = [r[rows, :].astype(F32) for r in pieces]
        mean = sum(jnp.sum(b, axis=-1, keepdims=True) for b in x) / d
        x = [b - mean for b in x]
        var = sum(jnp.sum(b * b, axis=-1, keepdims=True) for b in x) / d
        scale = lax.rsqrt(var + EPS)
        for k in range(4):
            cols = pl.ds(pl.multiple_of((t ^ k) * width, width), width)
            normed_ref[rows, cols] = (x[k] * scale).astype(BF)
        return carry

    lax.fori_loop(0, n // 48, norm, 0)

    def project(i, carry):
        for g, w_ref in enumerate((wo_ref, wp_ref)):
            qkv_ref[3 * g + i] = jnp.dot(
                normed_ref[...], w_ref[i], preferred_element_type=F32
            ).astype(BF)
        return carry

    lax.fori_loop(0, 3, project, 0)
    attend(qkv_ref, idk_ref, idq_ref, attn_ref, 0, 2)


def attend(qkv_ref, idk_ref, idq_ref, attn_ref, first, last):
    mask_a, mask_b = head_masks()
    cells = idk_ref.shape[0] // 4

    def window(w, carry):
        rows = pl.ds(pl.multiple_of(w * cells, 16), cells)
        to = pl.ds(pl.multiple_of((w - first) * cells, 16), cells)
        allowed = allowed_t(idk_ref, idq_ref, w, cells)
        for hp in range(4):
            g, lanes = hp // 2, slice(128 * (hp % 2), 128 * (hp % 2) + 128)
            q2 = stacked(qkv_ref[3 * g, rows, lanes], mask_a, mask_b)
            pt = probs_t(qkv_ref[3 * g + 1, rows, lanes], q2, allowed)
            ot = lax.dot_general(
                qkv_ref[3 * g + 2, rows, lanes], pt.astype(BF), TN, preferred_element_type=F32
            )
            attn_ref[to, 128 * hp : 128 * hp + 128] = merge_heads(ot).astype(BF)
        return carry

    lax.fori_loop(first, last, window, 0)


def last_kernel(qkv_ref, idk_ref, idq_ref, attn_ref):
    attend(qkv_ref, idk_ref, idq_ref, attn_ref, 2, 4)


def last_windows(qkv, idk, idq):
    n, width = qkv.shape[1:]
    return pl.pallas_call(
        last_kernel,
        out_shape=jax.ShapeDtypeStruct((n // 2, 2 * width), BF),
        in_specs=spec(3),
        out_specs=spec(1)[0],
        compiler_params=params(16),
        cost_estimate=pl.CostEstimate(flops=1, bytes_accessed=1, transcendentals=0),
    )(qkv, idk, idq)


def forward(t, pieces, wo, wp, idk, idq):
    n, width = pieces[0].shape
    d = 4 * width
    return pl.pallas_call(
        forward_kernel,
        out_shape=(
            jax.ShapeDtypeStruct((n, d), BF),
            jax.ShapeDtypeStruct((6, n, width), BF),
            jax.ShapeDtypeStruct((n // 2, 2 * width), BF),
        ),
        in_specs=[pl.BlockSpec(memory_space=pltpu.SMEM)] + spec(7),
        out_specs=tuple(spec(3)),
        compiler_params=params(20),
        cost_estimate=pl.CostEstimate(flops=8 * 10**9, bytes_accessed=10 * 10**6, transcendentals=10**6),
    )(t, *pieces, wo, wp, idk, idq)


def turn_kernel(normed_ref, a_ref, b_ref, normed_t, attn_t):
    d = normed_ref.shape[1]

    def body(i, carry):
        cols = pl.ds(pl.multiple_of(i * 256, 256), 256)
        normed_t[cols, :] = normed_ref[:, cols].T
        return carry

    lax.fori_loop(0, d // 256, body, 0)

    def body2(i, carry):
        cols = pl.ds(pl.multiple_of(i * 256, 256), 256)
        attn_t[cols, :] = jnp.concatenate([a_ref[:, cols], b_ref[:, cols]], axis=0).T
        return carry

    lax.fori_loop(0, a_ref.shape[1] // 256, body2, 0)


def turn(normed, attn):
    n, d = normed.shape
    e = attn[0].shape[1]
    return pl.pallas_call(
        turn_kernel,
        out_shape=(jax.ShapeDtypeStruct((d, n), BF), jax.ShapeDtypeStruct((e, n), BF)),
        in_specs=spec(3),
        out_specs=tuple(spec(2)),
        compiler_params=params(16),
        cost_estimate=SMALL,
    )(normed, *attn)


def output_kernel(group, t_ref, *refs):
    pieces, targets = blocks(refs[:3]), refs[3:7]
    own_ref, other_ref, wc_ref, idk_ref = refs[7:11]
    before, refs = refs[11 : 11 + 4 * group], refs[11 + 4 * group :]
    mixed, err_ref, y_ref = refs[:4], refs[4], refs[5]
    t = t_ref[0]
    n, width = pieces[0].shape
    cells = n // 4
    half = cells // 2
    e = own_ref.shape[1]
    for old, new in zip(before, mixed):
        new[: group * cells, :] = old[...]
    for k in range(4):
        x_ref, want_ref = pieces[k], targets[k]
        cols = pl.ds(pl.multiple_of((t ^ k) * width, width), width)
        y_ref[...] = jnp.dot(own_ref[...], wc_ref[:e, cols], preferred_element_type=F32) + jnp.dot(
            other_ref[...], wc_ref[e:, cols], preferred_element_type=F32
        )
        ys = []
        for i in range(2):
            at = slice(cells * i, cells * (i + 1))
            rows = slice(cells * (2 * group + i), cells * (2 * group + i + 1))
            y = x_ref[rows, :].astype(F32) + y_ref[at, :]
            ys.append(y)
            err = y - want_ref[rows, :].astype(F32)
            valid = idk_ref[rows, :] >= 0
            err_ref[at, cols] = jnp.where(valid, err, 0.0).astype(BF)
        if k < 2:
            at = slice(cells * group, cells * (group + 1))
            for s in range(2):
                part = slice(half * s, half * (s + 1))
                mixed[2 * s + k][at, :] = jnp.concatenate([y[part] for y in ys], axis=0).astype(BF)


def output(t, pieces, targets, own, other, wc, idk, before=()):
    n, width = pieces[0].shape
    group = 1 if before else 0
    piece = jax.ShapeDtypeStruct((n // 4 * (1 + group), width), BF)
    return pl.pallas_call(
        functools.partial(output_kernel, group),
        out_shape=(piece, piece, piece, piece, jax.ShapeDtypeStruct((n // 2, 4 * width), BF)),
        in_specs=[pl.BlockSpec(memory_space=pltpu.SMEM)] + spec(11 + len(before)),
        out_specs=tuple(spec(5)),
        scratch_shapes=[pltpu.VMEM((n // 2, width), F32)],
        compiler_params=params(20),
        cost_estimate=SMALL,
    )(t, *pieces, *targets, own, other, wc, idk, *before)


def probs_kernel(group, qkv_ref, idk_ref, idq_ref, p_ref):
    cells = idk_ref.shape[0] // 4
    mask_a, mask_b = head_masks()

    def window(i, carry):
        w = 2 * group + i
        rows = pl.ds(pl.multiple_of(w * cells, 16), cells)
        allowed = allowed_t(idk_ref, idq_ref, w, cells)
        for hp in range(4):
            g, lanes = hp // 2, slice(128 * (hp % 2), 128 * (hp % 2) + 128)
            q2 = stacked(qkv_ref[3 * g, rows, lanes], mask_a, mask_b)
            p_ref[4 * i + hp] = probs_t(qkv_ref[3 * g + 1, rows, lanes], q2, allowed)
        return carry

    lax.fori_loop(0, 2, window, 0)


def probs_of(group, qkv, idk, idq):
    n, width = qkv.shape[1:]
    return pl.pallas_call(
        functools.partial(probs_kernel, group),
        out_shape=jax.ShapeDtypeStruct((8, n // 4, n // 2), F32),
        in_specs=spec(3),
        out_specs=spec(1)[0],
        compiler_params=params(16),
        cost_estimate=SMALL,
    )(qkv, idk, idq)


def masked_sums(grad, w, bounds):
    g_hi = jnp.sum(jnp.where(w > bounds[0:1], grad, 0.0), axis=0, keepdims=True) * bounds[2:3]
    g_lo = jnp.sum(jnp.where(w < bounds[1:2], grad, 0.0), axis=0, keepdims=True) * bounds[3:4]
    return g_hi, g_lo


def proj_sums_kernel(e0_ref, e1_ref, attn_t, po_ref, pp_ref, pb_ref, proj_ref):
    def proj_part(i, carry):
        cols = pl.ds(pl.multiple_of(i * 256, 256), 256)
        err = jnp.concatenate([e0_ref[:, cols], e1_ref[:, cols]], axis=0)
        grad = jnp.dot(attn_t[...], err, preferred_element_type=F32)
        n = po_ref.shape[0]
        b = pb_ref[:, cols]
        h0, l0 = masked_sums(grad[:n], po_ref[:, cols].astype(F32), b)
        h1, l1 = masked_sums(grad[n:], pp_ref[:, cols].astype(F32), b)
        proj_ref[0:1, cols] = h0 + h1
        proj_ref[1:2, cols] = l0 + l1
        return carry

    lax.fori_loop(0, 4, proj_part, 0)


def proj_sums(errs, attn_t, po, pp, pb):
    return pl.pallas_call(
        proj_sums_kernel,
        out_shape=jax.ShapeDtypeStruct((2, errs[0].shape[1]), F32),
        in_specs=spec(6),
        out_specs=spec(1)[0],
        compiler_params=params(16),
        cost_estimate=pl.CostEstimate(flops=10**9, bytes_accessed=3 * 10**6, transcendentals=0),
    )(*errs, attn_t, po, pp, pb)


def backward_kernel(group, err_ref, wc_ref, qkv_ref, p_ref, g_ref, d_ref):
    e = d_ref.shape[1]
    cells = d_ref.shape[0] // 2
    d_ref[...] = lax.dot_general(err_ref[...], wc_ref[:e], NT, preferred_element_type=F32).astype(BF)
    mask_a, mask_b = head_masks()

    def window(i, carry):
        rows = pl.ds(pl.multiple_of((2 * group + i) * cells, 16), cells)
        at = pl.ds(pl.multiple_of(i * cells, 16), cells)
        for hp in range(4):
            g, lanes = hp // 2, slice(128 * (hp % 2), 128 * (hp % 2) + 128)
            q2 = stacked(qkv_ref[3 * g, rows, lanes], mask_a, mask_b)
            k = qkv_ref[3 * g + 1, rows, lanes]
            v = qkv_ref[3 * g + 2, rows, lanes]
            pt = p_ref[4 * i + hp]
            d2 = stacked(d_ref[at, 128 * hp : 128 * hp + 128], mask_a, mask_b)
            g_ref[3 * g + 2, at, lanes] = jnp.dot(
                pt.astype(BF), d2, preferred_element_type=F32
            ).astype(BF)
            dpt = lax.dot_general(v, d2, NT, preferred_element_type=F32)
            gst = (pt * (dpt - jnp.sum(pt * dpt, axis=0, keepdims=True))).astype(BF)
            g_ref[3 * g + 1, at, lanes] = (
                jnp.dot(gst, q2, preferred_element_type=F32) * SCALE
            ).astype(BF)
            gqt = lax.dot_general(k, gst, TN, preferred_element_type=F32) * SCALE
            g_ref[3 * g, at, lanes] = merge_heads(gqt).astype(BF)
        return carry

    lax.fori_loop(0, 2, window, 0)


def backward(group, err, wc, qkv, probs):
    n, width = qkv.shape[1:]
    return pl.pallas_call(
        functools.partial(backward_kernel, group),
        out_shape=jax.ShapeDtypeStruct((6, n // 2, width), BF),
        in_specs=spec(4),
        out_specs=spec(1)[0],
        scratch_shapes=[pltpu.VMEM((n // 2, 2 * width), BF)],
        compiler_params=params(20),
        cost_estimate=LARGE if group else SMALL,
    )(err, wc, qkv, probs)


def qkv_sums_kernel(side, g0_ref, g1_ref, normed_t, w_ref, b_ref, to_ref):
    width = g0_ref.shape[2]

    def qkv_part(i, carry):
        cells = jnp.concatenate([g0_ref[3 * side + i], g1_ref[3 * side + i]], axis=0)
        grad = jnp.dot(normed_t[...], cells, preferred_element_type=F32)
        hi, lo = masked_sums(grad, w_ref[i].astype(F32), b_ref[i])
        to_ref[0:1, pl.ds(pl.multiple_of(i * width, width), width)] = hi
        to_ref[1:2, pl.ds(pl.multiple_of(i * width, width), width)] = lo
        return carry

    lax.fori_loop(0, 3, qkv_part, 0)


def qkv_sums(side, g, normed_t, w, b):
    width = g[0].shape[2]
    return pl.pallas_call(
        functools.partial(qkv_sums_kernel, side),
        out_shape=jax.ShapeDtypeStruct((2, 3 * width), F32),
        in_specs=spec(5),
        out_specs=spec(1)[0],
        compiler_params=params(20),
        cost_estimate=LARGE,
    )(*g, normed_t, w, b)


def halves_kernel(x_ref, low_ref, up_ref, sems):
    half = low_ref.shape[1]
    low = pltpu.make_async_copy(x_ref.at[:, :half], low_ref, sems.at[0])
    up = pltpu.make_async_copy(x_ref.at[:, half:], up_ref, sems.at[1])
    low.start()
    up.start()
    low.wait()
    up.wait()


def halves_of(block):
    rows, lon, lev, width = block.shape
    half = jax.ShapeDtypeStruct((rows, lon // 2, lev, width), BF)
    return pl.pallas_call(
        halves_kernel,
        out_shape=(half, half),
        in_specs=[pl.BlockSpec(memory_space=pltpu.HBM)],
        out_specs=tuple(spec(2)),
        scratch_shapes=[pltpu.SemaphoreType.DMA((2,))],
        compiler_params=params(16),
        cost_estimate=SMALL,
    )(block)


def split_kernel(s_ref, *refs):
    offset, core = s_ref[0], s_ref[1]
    pairs = (len(refs) - 1) // 3
    rows, lon, lev, width = refs[1].shape
    many = (rows + WLAT) // 2
    half = lon * lev
    cells = 2 * WLAT * half
    for rel in range(2):
        base = many * (core ^ rel) - offset

        def body(w, carry):
            at = pl.ds(pl.multiple_of(w * cells, 16), cells)
            for i in range(pairs):
                up_ref, low_ref = refs[2 * i : 2 * i + 2]
                parts = []
                for ref, part in ((up_ref, slice(up_ref.shape[1] - lon, up_ref.shape[1])), (low_ref, slice(0, lon))):
                    for j in range(WLAT):
                        r = base + WLAT * w + j
                        v = ref[jnp.clip(r, 0, rows - 1), part].astype(F32).reshape(half, width)
                        parts.append(jnp.where((r >= 0) & (r < rows), v, 0.0))
                block = jnp.concatenate(parts, axis=0).astype(BF)
                if rel:
                    refs[-1][i, at, :] = block
                else:
                    refs[2 * pairs + i][at, :] = block
            return carry

        lax.fori_loop(0, many // WLAT, body, 0)


def split(place, *halves):
    rows, lon, lev, width = halves[1].shape
    pairs = len(halves) // 2
    n = (rows + WLAT) * lon * lev
    return pl.pallas_call(
        split_kernel,
        out_shape=(jax.ShapeDtypeStruct((n, width), BF),) * pairs
        + (jax.ShapeDtypeStruct((pairs, n, width), BF),),
        in_specs=[pl.BlockSpec(memory_space=pltpu.SMEM)] + spec(2 * pairs),
        out_specs=tuple(spec(pairs + 1)),
        compiler_params=params(16),
        cost_estimate=SMALL,
    )(place, *halves)


def cell_at(c, window):
    cells = 2 * WLAT * window
    w = sum((c >= i * cells).astype(jnp.int32) for i in range(1, 4))
    c = c - w * cells
    s = (c >= WLAT * window).astype(jnp.int32)
    c = c - s * WLAT * window
    r = sum((c >= i * window).astype(jnp.int32) for i in range(1, WLAT))
    c = c - r * window
    return w * WLAT + r, s * (window // 2) + (c >> 1), c & 1


def ids_kernel(s_ref, ids_ref, idk_ref, idq_ref):
    offset, core, sector = s_ref[0], s_ref[1], s_ref[2]
    rows, lev, total = ids_ref.shape
    n = idk_ref.shape[0]
    cells = n // 4
    window = cells // (2 * WLAT)
    many = (rows + WLAT) // 2
    ids = ids_ref[...].astype(F32).reshape(rows * lev, total)

    def find(c):
        r, lon, level = cell_at(c, window)
        r = r + many * core - offset
        lon = lon + sector * window + window // 2
        lon = jnp.where(lon >= total, lon - total, lon)
        valid = (r >= 0) & (r < rows)
        return jnp.where(valid, 2 * r + level, -1), lon, valid

    spot, lon, valid = find(lax.broadcasted_iota(jnp.int32, (n, 1), 0))
    at = lax.broadcasted_iota(jnp.int32, (n, rows * lev), 1) == spot
    found = jnp.dot(jnp.where(at, 1.0, 0.0), ids, preferred_element_type=F32)
    there = lax.broadcasted_iota(jnp.int32, (n, total), 1) == lon
    found = jnp.sum(jnp.where(there, found, 0.0), axis=1, keepdims=True)
    idk_ref[...] = jnp.where(valid, found, -1.0).astype(jnp.int32)
    for w in range(4):
        lane = lax.broadcasted_iota(jnp.int32, (1, 2 * cells), 1)
        spot, lon, valid = find(w * cells + jnp.where(lane >= cells, lane - cells, lane))
        there = lax.broadcasted_iota(jnp.int32, (total, 2 * cells), 0) == lon
        found = jnp.dot(ids, jnp.where(there, 1.0, 0.0), preferred_element_type=F32)
        at = lax.broadcasted_iota(jnp.int32, (rows * lev, 2 * cells), 0) == spot
        found = jnp.sum(jnp.where(at, found, 0.0), axis=0, keepdims=True)
        idq_ref[w] = jnp.where(valid, found, -1.0).astype(jnp.int32)


def window_ids(place, ids, cells):
    return pl.pallas_call(
        ids_kernel,
        out_shape=(
            jax.ShapeDtypeStruct((4 * cells, 1), jnp.int32),
            jax.ShapeDtypeStruct((4, 1, 2 * cells), jnp.int32),
        ),
        in_specs=[pl.BlockSpec(memory_space=pltpu.SMEM)] + spec(1),
        out_specs=tuple(spec(2)),
        compiler_params=params(16),
        cost_estimate=SMALL,
    )(place, ids)


def join_kernel(s_ref, a0, a1, b0, b1, out_ref, grid_ref):
    offset, core = s_ref[0], s_ref[1]
    rows, lon, lev, width = out_ref.shape
    many = (rows + WLAT) // 2
    half = lon * lev // 2
    for rel, ins in ((0, (a0, a1)), (1, (b0, b1))):
        base = many * (core ^ rel)
        for s in range(2):
            for i in range(many // 4):
                v = ins[s][4 * half * i : 4 * half * (i + 1), :].astype(F32)
                for j in range(4):
                    grid_ref[base + 4 * i + j, half * (1 - s) : half * (2 - s), :] = v[
                        half * j : half * (j + 1)
                    ]

    def body(i, carry):
        for j in range(2):
            r = 2 * i + j
            out_ref[r] = grid_ref[r + offset].reshape(lon, lev, width).astype(BF)
        return carry

    lax.fori_loop(0, rows // 2, body, 0)


def join(place, parts, rows, lon, lev):
    n, width = parts[0].shape
    out = pl.pallas_call(
        join_kernel,
        out_shape=jax.ShapeDtypeStruct((rows, lon, lev, width), BF),
        in_specs=[pl.BlockSpec(memory_space=pltpu.SMEM)] + spec(4),
        out_specs=spec(1)[0],
        scratch_shapes=[pltpu.VMEM((rows + WLAT, lon * lev, width), F32)],
        compiler_params=params(16),
        cost_estimate=SMALL,
    )(place, *parts)
    return jnp.transpose(out, (0, 2, 1, 3))


def send(block, shift, flip):
    count, tp = lax.axis_size("lat"), lax.axis_size("tp")
    route = [
        (u * tp + t, ((u + shift) % count) * tp + (t ^ flip)) for u in range(count) for t in range(tp)
    ]
    return lax.ppermute(block, ("lat", "tp"), route)


def swap(block, other, flip):
    count, tp = lax.axis_size("lat"), lax.axis_size("tp")
    route = [(u * tp + t, (u ^ other) * tp + (t ^ flip)) for u in range(count) for t in range(tp)]
    return lax.ppermute(block, ("lat", "tp"), route)


def lat_terms(block, bit):
    count = lax.axis_size("lat")
    terms = [block]
    while bit < count:
        block = added(terms)
        terms = [block, swap(block, bit, 0)]
        if 4 * bit <= count:
            terms += [swap(block, 2 * bit, 0), swap(block, 3 * bit, 0)]
        bit *= len(terms)
    return terms


def added(terms):
    while len(terms) > 1:
        terms = [a + b for a, b in zip(terms[::2], terms[1::2])]
    return terms[0]


def after(block, *others):
    return lax.optimization_barrier((block, *others))[0]


def local(features, target, w_qkv, w_proj, qkv_clip, proj_clip, shift_offset, region_ids):
    rows, lev, lon, width = features.shape
    half = lon // 2
    sector = lax.axis_index("lat")
    t = lax.axis_index("tp")
    t_arr = jnp.reshape(t, (1,)).astype(jnp.int32)
    place = jnp.stack([shift_offset[0], t % 2, sector]).astype(jnp.int32)

    f_raw, t_raw = (jnp.transpose(block, (0, 2, 1, 3)) for block in (features, target))
    f_low, f_up = halves_of(f_raw)
    f_low, f_up, w_qkv, w_proj = lax.optimization_barrier((f_low, f_up, w_qkv, w_proj))
    f_low, f_up_y = send(f_low, -1, 0), send(f_up, 0, 2)

    w3 = jnp.transpose(w_qkv, (1, 0, 2))
    c3 = jnp.transpose(qkv_clip, (1, 0, 2))
    w3_peer = send(w3, 0, 1)
    c3_peer = send(c3, 0, 1)
    share = w_proj.shape[0] // 2
    slab = after(w_proj, c3_peer)
    slab = send(lax.dynamic_slice_in_dim(slab, share * (sector % 2), share, 0), 0, 2)
    w1 = send(w_proj, 0, 1)
    wc_own, b_own = clip_qkv(w3, c3)
    wc_peer, b_peer = clip_qkv(w3_peer, c3_peer)
    idk, idq = window_ids(place, region_ids, WLAT * lev * lon)
    f_low, f_up_y, w1, t_low, wc_own = lax.optimization_barrier(
        (f_low, f_up_y, w1, t_raw[:, :half], wc_own)
    )
    f_low_y = send(f_low, 0, 2)
    t_low = send(t_low, -1, 0)
    t_own, t_away = split(place, t_raw, t_low)
    t_away = t_away.reshape(t_own.shape)
    t_1 = send(t_away, 0, 1)
    f_low_y, t_own, t_away, slab, wc_peer, idk, idq = lax.optimization_barrier(
        (f_low_y, t_own, t_away, slab, wc_peer, idk, idq)
    )
    x_0, x_2, x_away = split(place, f_raw, f_low, f_up_y, f_low_y)
    pieces = (x_0, x_2, send(x_away, 0, 1))

    targets = (t_own, t_1, send(t_own, 0, 2), send(t_away, 0, 3))
    more = swap(slab, 1, 0)

    normed, qkv, attn_0 = forward(t_arr, pieces, wc_own, wc_peer, idk, idq)
    other_0 = send(attn_0, 0, 2)
    probs_0 = probs_of(0, qkv, idk, idq)
    attn_1 = last_windows(after(qkv, probs_0, *targets, more), idk, idq)
    slab_3, more_3 = send(after(slab, attn_1), 0, 1), send(after(more, attn_1), 0, 1)
    pc, pb = clip_proj(place, [w_proj, w1, slab, more, slab_3, more_3], proj_clip)
    other_1 = send(attn_1, 0, 2)
    normed_t, attn_t = turn(normed, (attn_0, attn_1))
    probs = (probs_0, probs_of(1, after(qkv, attn_1), idk, idq))

    *mixed, err_0 = output(t_arr, pieces, targets, attn_0, other_0, pc, idk)
    grads_0 = backward(0, err_0, pc, qkv, probs[0])
    other_1 = after(other_1, grads_0)
    m00, m01, m10, m11, err_1 = output(t_arr, pieces, targets, attn_1, other_1, pc, idk, mixed)
    m01 = send(m01, 0, 1)
    m10 = send(m10, 1, 0)
    m11 = send(m11, 1, 1)
    proj = proj_sums((err_0, err_1), attn_t, w_proj, w1, pb)
    proj_y = send(proj, 0, 2)
    grads = (grads_0, backward(1, err_1, pc, qkv, probs[1]))
    peer = qkv_sums(1, grads, normed_t, w3_peer, b_peer)
    proj = proj + proj_y
    peer = jnp.concatenate([peer, proj], axis=1)
    terms = [send(peer, 0, 1), swap(peer, 1, 1)]
    grads = lax.optimization_barrier((*grads, m01, m10, m11, peer))[:2]
    own = qkv_sums(0, grads, normed_t, w3, b_own)
    own = jnp.concatenate([own, proj], axis=1)
    sums = added([own, terms[0], swap(own, 1, 0), terms[1]])
    sums = added(lat_terms(sums, 2))
    mixed = join(place, [m00, m10, m01, m11], rows, lon, lev)
    return (mixed, sums[:, : 3 * width].reshape(2, 3, width), sums[:, 3 * width :])


def solution(mesh):
    placed = (
        P(None, None, "lat", "tp"),
        P(None, None, "lat", "tp"),
        P(None, None, "tp"),
        P("tp", None),
        P(None, None, "tp"),
        P(),
        P(),
        P(),
    )
    return jax.shard_map(
        local,
        mesh=mesh,
        in_specs=placed,
        out_specs=(P(None, None, "lat", "tp"), P(None, None, "tp"), P()),
        check_vma=False,
    )
```

```python
import functools

import jax
import jax.numpy as jnp
from jax import lax
from jax.experimental import pallas as pl
from jax.experimental.pallas import tpu as pltpu
from jax.sharding import PartitionSpec as P

HD = 64
WLAT = 6
EPS = 1e-05
NEG = -1e30
F32 = jnp.float32
BF = jnp.bfloat16
SCALE = HD ** (-0.5)
NT = (((1,), (1,)), ((), ()))
TN = (((0,), (0,)), ((), ()))
LARGE = pl.CostEstimate(flops=8 * 10**9, bytes_accessed=10**7, transcendentals=10**6)
SMALL = pl.CostEstimate(flops=1, bytes_accessed=1, transcendentals=0)


def spec(n):
    return [pl.BlockSpec(memory_space=pltpu.VMEM)] * n


def params(mib):
    return pltpu.CompilerParams(vmem_limit_bytes=mib * 1024 * 1024)


def bounds_of(weight, logits_hi, logits_lo):
    top = jnp.max(weight, axis=0, keepdims=True)
    low = jnp.min(weight, axis=0, keepdims=True)
    hi = 1.0 / (1.0 + jnp.exp(-logits_hi))
    lo = 1.0 / (1.0 + jnp.exp(-logits_lo))
    return hi * top, lo * low, hi * (1.0 - hi) * top, lo * (1.0 - lo) * low


def clip_qkv_kernel(w_ref, c_ref, wc_ref, b_ref):
    def body(i, carry):
        w = w_ref[i].astype(F32)
        up, lw, fh, fl = bounds_of(w, c_ref[i, 0:1], c_ref[i, 1:2])
        wc_ref[i] = jnp.minimum(jnp.maximum(w, lw), up).astype(BF)
        b_ref[i, 0:1] = up
        b_ref[i, 1:2] = lw
        b_ref[i, 2:3] = fh
        b_ref[i, 3:4] = fl
        return carry

    lax.fori_loop(0, 3, body, 0)


def clip_qkv(w, clips):
    n, d, e = w.shape
    return pl.pallas_call(
        clip_qkv_kernel,
        out_shape=(
            jax.ShapeDtypeStruct((n, d, e), BF),
            jax.ShapeDtypeStruct((n, 8, e), F32),
        ),
        in_specs=spec(2),
        out_specs=tuple(spec(2)),
        compiler_params=params(24),
        cost_estimate=SMALL,
    )(w, clips)


def clip_proj_kernel(s_ref, w0, w1, a2, b2, a3, b3, c_ref, wc_ref, b_ref):
    second = s_ref[2] % 2 == 1

    def body(i, carry):
        cols = pl.ds(pl.multiple_of(i * 256, 256), 256)
        parts = [w0[:, cols].astype(F32), w1[:, cols].astype(F32)]
        for first_ref, other_ref in ((a2, b2), (a3, b3)):
            a, b = first_ref[:, cols].astype(F32), other_ref[:, cols].astype(F32)
            parts += [jnp.where(second, b, a), jnp.where(second, a, b)]
        w = jnp.concatenate(parts, axis=0)
        up, lw, fh, fl = bounds_of(w, c_ref[0:1, cols], c_ref[1:2, cols])
        wc = jnp.minimum(jnp.maximum(w, lw), up).astype(BF)
        wc_ref[:, cols] = wc
        b_ref[0:1, cols] = up
        b_ref[1:2, cols] = lw
        b_ref[2:3, cols] = fh
        b_ref[3:4, cols] = fl
        return carry

    lax.fori_loop(0, w0.shape[1] // 256, body, 0)


def clip_proj(place, shards, clips):
    e, d = shards[0].shape
    return pl.pallas_call(
        clip_proj_kernel,
        out_shape=(
            jax.ShapeDtypeStruct((4 * e, d), BF),
            jax.ShapeDtypeStruct((8, d), F32),
        ),
        in_specs=[pl.BlockSpec(memory_space=pltpu.SMEM)] + spec(7),
        out_specs=tuple(spec(2)),
        compiler_params=params(24),
        cost_estimate=SMALL,
    )(place, *shards, clips)


def stacked(block, mask_a, mask_b):
    return jnp.concatenate([block * mask_a, block * mask_b], axis=0)


def head_masks():
    lane = lax.broadcasted_iota(jnp.int32, (1, 2 * HD), 1)
    mask_a = jnp.where(lane < HD, 1.0, 0.0).astype(BF)
    mask_b = jnp.where(lane < HD, 0.0, 1.0).astype(BF)
    return mask_a, mask_b


def probs_t(k, q2, allowed):
    st = lax.dot_general(k, q2, NT, preferred_element_type=F32) * SCALE
    st = jnp.where(allowed, st, NEG)
    e = jnp.exp(st - jnp.max(st, axis=0, keepdims=True))
    return e * (1.0 / jnp.sum(e, axis=0, keepdims=True))


def merge_heads(t_block):
    both = t_block.T
    n = both.shape[0] // 2
    lane = lax.broadcasted_iota(jnp.int32, (n, 2 * HD), 1)
    return jnp.where(lane < HD, both[:n], both[n:])


def allowed_t(idk_ref, idq_ref, w, cells):
    rows = pl.ds(pl.multiple_of(w * cells, 16), cells)
    idk = idk_ref[rows, :]
    return (idk == idq_ref[w]) & (idk >= 0)


def blocks(refs):
    own, other, away = refs
    return own, away.at[0], other, away.at[1]


def forward_kernel(t_ref, *refs):
    pieces = blocks(refs[:3])
    wo_ref, wp_ref, idk_ref, idq_ref, normed_ref, qkv_ref, attn_ref = refs[3:]
    t = t_ref[0]
    n, width = pieces[0].shape
    d = 4 * width

    def norm(w, carry):
        rows = pl.ds(pl.multiple_of(w * 48, 16), 48)
        x = [r[rows, :].astype(F32) for r in pieces]
        mean = sum(jnp.sum(b, axis=-1, keepdims=True) for b in x) / d
        x = [b - mean for b in x]
        var = sum(jnp.sum(b * b, axis=-1, keepdims=True) for b in x) / d
        scale = lax.rsqrt(var + EPS)
        for k in range(4):
            cols = pl.ds(pl.multiple_of((t ^ k) * width, width), width)
            normed_ref[rows, cols] = (x[k] * scale).astype(BF)
        return carry

    lax.fori_loop(0, n // 48, norm, 0)

    def project(i, carry):
        for g, w_ref in enumerate((wo_ref, wp_ref)):
            qkv_ref[3 * g + i] = jnp.dot(
                normed_ref[...], w_ref[i], preferred_element_type=F32
            ).astype(BF)
        return carry

    lax.fori_loop(0, 3, project, 0)
    attend(qkv_ref, idk_ref, idq_ref, attn_ref, 0, 2)


def attend(qkv_ref, idk_ref, idq_ref, attn_ref, first, last):
    mask_a, mask_b = head_masks()
    cells = idk_ref.shape[0] // 4

    def window(w, carry):
        rows = pl.ds(pl.multiple_of(w * cells, 16), cells)
        to = pl.ds(pl.multiple_of((w - first) * cells, 16), cells)
        allowed = allowed_t(idk_ref, idq_ref, w, cells)
        for hp in range(4):
            g, lanes = hp // 2, slice(128 * (hp % 2), 128 * (hp % 2) + 128)
            q2 = stacked(qkv_ref[3 * g, rows, lanes], mask_a, mask_b)
            pt = probs_t(qkv_ref[3 * g + 1, rows, lanes], q2, allowed)
            ot = lax.dot_general(
                qkv_ref[3 * g + 2, rows, lanes], pt.astype(BF), TN, preferred_element_type=F32
            )
            attn_ref[to, 128 * hp : 128 * hp + 128] = merge_heads(ot).astype(BF)
        return carry

    lax.fori_loop(first, last, window, 0)


def last_kernel(qkv_ref, idk_ref, idq_ref, attn_ref):
    attend(qkv_ref, idk_ref, idq_ref, attn_ref, 2, 4)


def last_windows(qkv, idk, idq):
    n, width = qkv.shape[1:]
    return pl.pallas_call(
        last_kernel,
        out_shape=jax.ShapeDtypeStruct((n // 2, 2 * width), BF),
        in_specs=spec(3),
        out_specs=spec(1)[0],
        compiler_params=params(16),
        cost_estimate=pl.CostEstimate(flops=1, bytes_accessed=1, transcendentals=0),
    )(qkv, idk, idq)


def forward(t, pieces, wo, wp, idk, idq):
    n, width = pieces[0].shape
    d = 4 * width
    return pl.pallas_call(
        forward_kernel,
        out_shape=(
            jax.ShapeDtypeStruct((n, d), BF),
            jax.ShapeDtypeStruct((6, n, width), BF),
            jax.ShapeDtypeStruct((n // 2, 2 * width), BF),
        ),
        in_specs=[pl.BlockSpec(memory_space=pltpu.SMEM)] + spec(7),
        out_specs=tuple(spec(3)),
        compiler_params=params(20),
        cost_estimate=pl.CostEstimate(flops=8 * 10**9, bytes_accessed=10 * 10**6, transcendentals=10**6),
    )(t, *pieces, wo, wp, idk, idq)


def turn_kernel(normed_ref, a_ref, b_ref, normed_t, attn_t):
    d = normed_ref.shape[1]

    def body(i, carry):
        cols = pl.ds(pl.multiple_of(i * 256, 256), 256)
        normed_t[cols, :] = normed_ref[:, cols].T
        return carry

    lax.fori_loop(0, d // 256, body, 0)

    def body2(i, carry):
        cols = pl.ds(pl.multiple_of(i * 256, 256), 256)
        attn_t[cols, :] = jnp.concatenate([a_ref[:, cols], b_ref[:, cols]], axis=0).T
        return carry

    lax.fori_loop(0, a_ref.shape[1] // 256, body2, 0)


def turn(normed, attn):
    n, d = normed.shape
    e = attn[0].shape[1]
    return pl.pallas_call(
        turn_kernel,
        out_shape=(jax.ShapeDtypeStruct((d, n), BF), jax.ShapeDtypeStruct((e, n), BF)),
        in_specs=spec(3),
        out_specs=tuple(spec(2)),
        compiler_params=params(16),
        cost_estimate=SMALL,
    )(normed, *attn)


def output_kernel(group, t_ref, *refs):
    pieces, targets = blocks(refs[:3]), refs[3:7]
    own_ref, other_ref, wc_ref, idk_ref = refs[7:11]
    before, refs = refs[11 : 11 + 4 * group], refs[11 + 4 * group :]
    mixed, err_ref, y_ref = refs[:4], refs[4], refs[5]
    t = t_ref[0]
    n, width = pieces[0].shape
    cells = n // 4
    half = cells // 2
    e = own_ref.shape[1]
    for old, new in zip(before, mixed):
        new[: group * cells, :] = old[...]
    for k in range(4):
        x_ref, want_ref = pieces[k], targets[k]
        cols = pl.ds(pl.multiple_of((t ^ k) * width, width), width)
        y_ref[...] = jnp.dot(own_ref[...], wc_ref[:e, cols], preferred_element_type=F32) + jnp.dot(
            other_ref[...], wc_ref[e:, cols], preferred_element_type=F32
        )
        ys = []
        for i in range(2):
            at = slice(cells * i, cells * (i + 1))
            rows = slice(cells * (2 * group + i), cells * (2 * group + i + 1))
            y = x_ref[rows, :].astype(F32) + y_ref[at, :]
            ys.append(y)
            err = y - want_ref[rows, :].astype(F32)
            valid = idk_ref[rows, :] >= 0
            err_ref[at, cols] = jnp.where(valid, err, 0.0).astype(BF)
        if k < 2:
            at = slice(cells * group, cells * (group + 1))
            for s in range(2):
                part = slice(half * s, half * (s + 1))
                mixed[2 * s + k][at, :] = jnp.concatenate([y[part] for y in ys], axis=0).astype(BF)


def output(t, pieces, targets, own, other, wc, idk, before=()):
    n, width = pieces[0].shape
    group = 1 if before else 0
    piece = jax.ShapeDtypeStruct((n // 4 * (1 + group), width), BF)
    return pl.pallas_call(
        functools.partial(output_kernel, group),
        out_shape=(piece, piece, piece, piece, jax.ShapeDtypeStruct((n // 2, 4 * width), BF)),
        in_specs=[pl.BlockSpec(memory_space=pltpu.SMEM)] + spec(11 + len(before)),
        out_specs=tuple(spec(5)),
        scratch_shapes=[pltpu.VMEM((n // 2, width), F32)],
        compiler_params=params(20),
        cost_estimate=SMALL,
    )(t, *pieces, *targets, own, other, wc, idk, *before)


def probs_kernel(group, qkv_ref, idk_ref, idq_ref, p_ref):
    cells = idk_ref.shape[0] // 4
    mask_a, mask_b = head_masks()

    def window(i, carry):
        w = 2 * group + i
        rows = pl.ds(pl.multiple_of(w * cells, 16), cells)
        allowed = allowed_t(idk_ref, idq_ref, w, cells)
        for hp in range(4):
            g, lanes = hp // 2, slice(128 * (hp % 2), 128 * (hp % 2) + 128)
            q2 = stacked(qkv_ref[3 * g, rows, lanes], mask_a, mask_b)
            p_ref[4 * i + hp] = probs_t(qkv_ref[3 * g + 1, rows, lanes], q2, allowed)
        return carry

    lax.fori_loop(0, 2, window, 0)


def probs_of(group, qkv, idk, idq):
    n, width = qkv.shape[1:]
    return pl.pallas_call(
        functools.partial(probs_kernel, group),
        out_shape=jax.ShapeDtypeStruct((8, n // 4, n // 2), F32),
        in_specs=spec(3),
        out_specs=spec(1)[0],
        compiler_params=params(16),
        cost_estimate=SMALL,
    )(qkv, idk, idq)


def masked_sums(grad, w, bounds):
    g_hi = jnp.sum(jnp.where(w > bounds[0:1], grad, 0.0), axis=0, keepdims=True) * bounds[2:3]
    g_lo = jnp.sum(jnp.where(w < bounds[1:2], grad, 0.0), axis=0, keepdims=True) * bounds[3:4]
    return g_hi, g_lo


def proj_sums_kernel(e0_ref, e1_ref, attn_t, po_ref, pp_ref, pb_ref, proj_ref):
    def proj_part(i, carry):
        cols = pl.ds(pl.multiple_of(i * 256, 256), 256)
        err = jnp.concatenate([e0_ref[:, cols], e1_ref[:, cols]], axis=0)
        grad = jnp.dot(attn_t[...], err, preferred_element_type=F32)
        n = po_ref.shape[0]
        b = pb_ref[:, cols]
        h0, l0 = masked_sums(grad[:n], po_ref[:, cols].astype(F32), b)
        h1, l1 = masked_sums(grad[n:], pp_ref[:, cols].astype(F32), b)
        proj_ref[0:1, cols] = h0 + h1
        proj_ref[1:2, cols] = l0 + l1
        return carry

    lax.fori_loop(0, 4, proj_part, 0)


def proj_sums(errs, attn_t, po, pp, pb):
    return pl.pallas_call(
        proj_sums_kernel,
        out_shape=jax.ShapeDtypeStruct((2, errs[0].shape[1]), F32),
        in_specs=spec(6),
        out_specs=spec(1)[0],
        compiler_params=params(16),
        cost_estimate=pl.CostEstimate(flops=10**9, bytes_accessed=3 * 10**6, transcendentals=0),
    )(*errs, attn_t, po, pp, pb)


def backward_kernel(group, err_ref, wc_ref, qkv_ref, p_ref, g_ref, d_ref):
    e = d_ref.shape[1]
    cells = d_ref.shape[0] // 2
    d_ref[...] = lax.dot_general(err_ref[...], wc_ref[:e], NT, preferred_element_type=F32).astype(BF)
    mask_a, mask_b = head_masks()

    def window(i, carry):
        rows = pl.ds(pl.multiple_of((2 * group + i) * cells, 16), cells)
        at = pl.ds(pl.multiple_of(i * cells, 16), cells)
        for hp in range(4):
            g, lanes = hp // 2, slice(128 * (hp % 2), 128 * (hp % 2) + 128)
            q2 = stacked(qkv_ref[3 * g, rows, lanes], mask_a, mask_b)
            k = qkv_ref[3 * g + 1, rows, lanes]
            v = qkv_ref[3 * g + 2, rows, lanes]
            pt = p_ref[4 * i + hp]
            d2 = stacked(d_ref[at, 128 * hp : 128 * hp + 128], mask_a, mask_b)
            g_ref[3 * g + 2, at, lanes] = jnp.dot(
                pt.astype(BF), d2, preferred_element_type=F32
            ).astype(BF)
            dpt = lax.dot_general(v, d2, NT, preferred_element_type=F32)
            gst = (pt * (dpt - jnp.sum(pt * dpt, axis=0, keepdims=True))).astype(BF)
            g_ref[3 * g + 1, at, lanes] = (
                jnp.dot(gst, q2, preferred_element_type=F32) * SCALE
            ).astype(BF)
            gqt = lax.dot_general(k, gst, TN, preferred_element_type=F32) * SCALE
            g_ref[3 * g, at, lanes] = merge_heads(gqt).astype(BF)
        return carry

    lax.fori_loop(0, 2, window, 0)


def backward(group, err, wc, qkv, probs):
    n, width = qkv.shape[1:]
    return pl.pallas_call(
        functools.partial(backward_kernel, group),
        out_shape=jax.ShapeDtypeStruct((6, n // 2, width), BF),
        in_specs=spec(4),
        out_specs=spec(1)[0],
        scratch_shapes=[pltpu.VMEM((n // 2, 2 * width), BF)],
        compiler_params=params(20),
        cost_estimate=LARGE if group else SMALL,
    )(err, wc, qkv, probs)


def qkv_sums_kernel(side, g0_ref, g1_ref, normed_t, w_ref, b_ref, to_ref):
    width = g0_ref.shape[2]

    def qkv_part(i, carry):
        cells = jnp.concatenate([g0_ref[3 * side + i], g1_ref[3 * side + i]], axis=0)
        grad = jnp.dot(normed_t[...], cells, preferred_element_type=F32)
        hi, lo = masked_sums(grad, w_ref[i].astype(F32), b_ref[i])
        to_ref[0:1, pl.ds(pl.multiple_of(i * width, width), width)] = hi
        to_ref[1:2, pl.ds(pl.multiple_of(i * width, width), width)] = lo
        return carry

    lax.fori_loop(0, 3, qkv_part, 0)


def qkv_sums(side, g, normed_t, w, b):
    width = g[0].shape[2]
    return pl.pallas_call(
        functools.partial(qkv_sums_kernel, side),
        out_shape=jax.ShapeDtypeStruct((2, 3 * width), F32),
        in_specs=spec(5),
        out_specs=spec(1)[0],
        compiler_params=params(20),
        cost_estimate=LARGE,
    )(*g, normed_t, w, b)


def halves_kernel(x_ref, low_ref, up_ref, sems):
    half = low_ref.shape[1]
    low = pltpu.make_async_copy(x_ref.at[:, :half], low_ref, sems.at[0])
    up = pltpu.make_async_copy(x_ref.at[:, half:], up_ref, sems.at[1])
    low.start()
    up.start()
    low.wait()
    up.wait()


def halves_of(block):
    rows, lon, lev, width = block.shape
    half = jax.ShapeDtypeStruct((rows, lon // 2, lev, width), BF)
    return pl.pallas_call(
        halves_kernel,
        out_shape=(half, half),
        in_specs=[pl.BlockSpec(memory_space=pltpu.HBM)],
        out_specs=tuple(spec(2)),
        scratch_shapes=[pltpu.SemaphoreType.DMA((2,))],
        compiler_params=params(16),
        cost_estimate=SMALL,
    )(block)


def split_kernel(s_ref, *refs):
    offset, core = s_ref[0], s_ref[1]
    pairs = (len(refs) - 1) // 3
    rows, lon, lev, width = refs[1].shape
    many = (rows + WLAT) // 2
    half = lon * lev
    cells = 2 * WLAT * half
    for rel in range(2):
        base = many * (core ^ rel) - offset

        def body(w, carry):
            at = pl.ds(pl.multiple_of(w * cells, 16), cells)
            for i in range(pairs):
                up_ref, low_ref = refs[2 * i : 2 * i + 2]
                parts = []
                for ref, part in ((up_ref, slice(up_ref.shape[1] - lon, up_ref.shape[1])), (low_ref, slice(0, lon))):
                    for j in range(WLAT):
                        r = base + WLAT * w + j
                        v = ref[jnp.clip(r, 0, rows - 1), part].astype(F32).reshape(half, width)
                        parts.append(jnp.where((r >= 0) & (r < rows), v, 0.0))
                block = jnp.concatenate(parts, axis=0).astype(BF)
                if rel:
                    refs[-1][i, at, :] = block
                else:
                    refs[2 * pairs + i][at, :] = block
            return carry

        lax.fori_loop(0, many // WLAT, body, 0)


def split(place, *halves):
    rows, lon, lev, width = halves[1].shape
    pairs = len(halves) // 2
    n = (rows + WLAT) * lon * lev
    return pl.pallas_call(
        split_kernel,
        out_shape=(jax.ShapeDtypeStruct((n, width), BF),) * pairs
        + (jax.ShapeDtypeStruct((pairs, n, width), BF),),
        in_specs=[pl.BlockSpec(memory_space=pltpu.SMEM)] + spec(2 * pairs),
        out_specs=tuple(spec(pairs + 1)),
        compiler_params=params(16),
        cost_estimate=SMALL,
    )(place, *halves)


def cell_at(c, window):
    cells = 2 * WLAT * window
    w = sum((c >= i * cells).astype(jnp.int32) for i in range(1, 4))
    c = c - w * cells
    s = (c >= WLAT * window).astype(jnp.int32)
    c = c - s * WLAT * window
    r = sum((c >= i * window).astype(jnp.int32) for i in range(1, WLAT))
    c = c - r * window
    return w * WLAT + r, s * (window // 2) + (c >> 1), c & 1


def ids_kernel(s_ref, ids_ref, idk_ref, idq_ref):
    offset, core, sector = s_ref[0], s_ref[1], s_ref[2]
    rows, lev, total = ids_ref.shape
    n = idk_ref.shape[0]
    cells = n // 4
    window = cells // (2 * WLAT)
    many = (rows + WLAT) // 2
    ids = ids_ref[...].astype(F32).reshape(rows * lev, total)

    def find(c):
        r, lon, level = cell_at(c, window)
        r = r + many * core - offset
        lon = lon + sector * window + window // 2
        lon = jnp.where(lon >= total, lon - total, lon)
        valid = (r >= 0) & (r < rows)
        return jnp.where(valid, 2 * r + level, -1), lon, valid

    spot, lon, valid = find(lax.broadcasted_iota(jnp.int32, (n, 1), 0))
    at = lax.broadcasted_iota(jnp.int32, (n, rows * lev), 1) == spot
    found = jnp.dot(jnp.where(at, 1.0, 0.0), ids, preferred_element_type=F32)
    there = lax.broadcasted_iota(jnp.int32, (n, total), 1) == lon
    found = jnp.sum(jnp.where(there, found, 0.0), axis=1, keepdims=True)
    idk_ref[...] = jnp.where(valid, found, -1.0).astype(jnp.int32)
    for w in range(4):
        lane = lax.broadcasted_iota(jnp.int32, (1, 2 * cells), 1)
        spot, lon, valid = find(w * cells + jnp.where(lane >= cells, lane - cells, lane))
        there = lax.broadcasted_iota(jnp.int32, (total, 2 * cells), 0) == lon
        found = jnp.dot(ids, jnp.where(there, 1.0, 0.0), preferred_element_type=F32)
        at = lax.broadcasted_iota(jnp.int32, (rows * lev, 2 * cells), 0) == spot
        found = jnp.sum(jnp.where(at, found, 0.0), axis=0, keepdims=True)
        idq_ref[w] = jnp.where(valid, found, -1.0).astype(jnp.int32)


def window_ids(place, ids, cells):
    return pl.pallas_call(
        ids_kernel,
        out_shape=(
            jax.ShapeDtypeStruct((4 * cells, 1), jnp.int32),
            jax.ShapeDtypeStruct((4, 1, 2 * cells), jnp.int32),
        ),
        in_specs=[pl.BlockSpec(memory_space=pltpu.SMEM)] + spec(1),
        out_specs=tuple(spec(2)),
        compiler_params=params(16),
        cost_estimate=SMALL,
    )(place, ids)


def join_kernel(s_ref, a0, a1, b0, b1, out_ref, grid_ref):
    offset, core = s_ref[0], s_ref[1]
    rows, lon, lev, width = out_ref.shape
    many = (rows + WLAT) // 2
    half = lon * lev // 2
    for rel, ins in ((0, (a0, a1)), (1, (b0, b1))):
        base = many * (core ^ rel)
        for s in range(2):
            for i in range(many // 4):
                v = ins[s][4 * half * i : 4 * half * (i + 1), :].astype(F32)
                for j in range(4):
                    grid_ref[base + 4 * i + j, half * (1 - s) : half * (2 - s), :] = v[
                        half * j : half * (j + 1)
                    ]

    def body(i, carry):
        for j in range(2):
            r = 2 * i + j
            out_ref[r] = grid_ref[r + offset].reshape(lon, lev, width).astype(BF)
        return carry

    lax.fori_loop(0, rows // 2, body, 0)


def join(place, parts, rows, lon, lev):
    n, width = parts[0].shape
    out = pl.pallas_call(
        join_kernel,
        out_shape=jax.ShapeDtypeStruct((rows, lon, lev, width), BF),
        in_specs=[pl.BlockSpec(memory_space=pltpu.SMEM)] + spec(4),
        out_specs=spec(1)[0],
        scratch_shapes=[pltpu.VMEM((rows + WLAT, lon * lev, width), F32)],
        compiler_params=params(16),
        cost_estimate=SMALL,
    )(place, *parts)
    return jnp.transpose(out, (0, 2, 1, 3))


def send(block, shift, flip):
    count, tp = lax.axis_size("lat"), lax.axis_size("tp")
    route = [
        (u * tp + t, ((u + shift) % count) * tp + (t ^ flip)) for u in range(count) for t in range(tp)
    ]
    return lax.ppermute(block, ("lat", "tp"), route)


def swap(block, other, flip):
    count, tp = lax.axis_size("lat"), lax.axis_size("tp")
    route = [(u * tp + t, (u ^ other) * tp + (t ^ flip)) for u in range(count) for t in range(tp)]
    return lax.ppermute(block, ("lat", "tp"), route)


def lat_terms(block, bit):
    count = lax.axis_size("lat")
    terms = [block]
    while bit < count:
        block = added(terms)
        terms = [block, swap(block, bit, 0)]
        if 4 * bit <= count:
            terms += [swap(block, 2 * bit, 0), swap(block, 3 * bit, 0)]
        bit *= len(terms)
    return terms


def added(terms):
    while len(terms) > 1:
        terms = [a + b for a, b in zip(terms[::2], terms[1::2])]
    return terms[0]


def after(block, *others):
    return lax.optimization_barrier((block, *others))[0]


def local(features, target, w_qkv, w_proj, qkv_clip, proj_clip, shift_offset, region_ids):
    rows, lev, lon, width = features.shape
    half = lon // 2
    sector = lax.axis_index("lat")
    t = lax.axis_index("tp")
    t_arr = jnp.reshape(t, (1,)).astype(jnp.int32)
    place = jnp.stack([shift_offset[0], t % 2, sector]).astype(jnp.int32)

    f_raw, t_raw = (jnp.transpose(block, (0, 2, 1, 3)) for block in (features, target))
    f_low, f_up = halves_of(f_raw)
    f_low, f_up, w_qkv, w_proj = lax.optimization_barrier((f_low, f_up, w_qkv, w_proj))
    f_up_y = send(f_up, 0, 2)
    f_low = send(f_low, -1, 0)

    w3 = jnp.transpose(w_qkv, (1, 0, 2))
    c3 = jnp.transpose(qkv_clip, (1, 0, 2))
    w3_peer = send(w3, 0, 1)
    c3_peer = send(c3, 0, 1)
    share = w_proj.shape[0] // 2
    w1 = send(w_proj, 0, 1)
    wc_own, b_own = clip_qkv(w3, c3)
    slab = after(w_proj, wc_own)
    slab = send(lax.dynamic_slice_in_dim(slab, share * (sector % 2), share, 0), 0, 2)
    wc_peer, b_peer = clip_qkv(w3_peer, c3_peer)
    idk, idq = window_ids(place, region_ids, WLAT * lev * lon)
    f_up_y, f_low, w1, t_low, wc_own = lax.optimization_barrier(
        (f_up_y, f_low, w1, t_raw[:, :half], wc_own)
    )
    f_low_y = send(f_low, 0, 2)
    t_low = send(t_low, -1, 0)
    t_own, t_away = split(place, t_raw, t_low)
    t_away = t_away.reshape(t_own.shape)
    t_1 = send(t_away, 0, 1)
    f_low_y, t_own, t_away, slab, wc_peer, idk, idq = lax.optimization_barrier(
        (f_low_y, t_own, t_away, slab, wc_peer, idk, idq)
    )
    x_0, x_2, x_away = split(place, f_raw, f_low, f_up_y, f_low_y)
    pieces = (x_0, x_2, send(x_away, 0, 1))

    targets = (t_own, t_1, send(t_own, 0, 2), send(t_away, 0, 3))
    more = swap(slab, 1, 0)

    normed, qkv, attn_0 = forward(t_arr, pieces, wc_own, wc_peer, idk, idq)
    other_0 = send(attn_0, 0, 2)
    probs_0 = probs_of(0, qkv, idk, idq)
    attn_1 = last_windows(after(qkv, probs_0, *targets, more), idk, idq)
    slab_3, more_3 = send(after(slab, attn_1), 0, 1), send(after(more, attn_1), 0, 1)
    pc, pb = clip_proj(place, [w_proj, w1, slab, more, slab_3, more_3], proj_clip)
    other_1 = send(attn_1, 0, 2)
    normed_t, attn_t = turn(normed, (attn_0, attn_1))
    probs = (probs_0, probs_of(1, after(qkv, attn_1), idk, idq))

    *mixed, err_0 = output(t_arr, pieces, targets, attn_0, other_0, pc, idk)
    grads_0 = backward(0, err_0, pc, qkv, probs[0])
    other_1 = after(other_1, grads_0)
    m00, m01, m10, m11, err_1 = output(t_arr, pieces, targets, attn_1, other_1, pc, idk, mixed)
    m01 = send(m01, 0, 1)
    m10 = send(m10, 1, 0)
    m11 = send(m11, 1, 1)
    proj = proj_sums((err_0, err_1), attn_t, w_proj, w1, pb)
    proj_y = send(proj, 0, 2)
    grads = (grads_0, backward(1, err_1, pc, qkv, probs[1]))
    peer = qkv_sums(1, grads, normed_t, w3_peer, b_peer)
    proj = proj + proj_y
    peer = jnp.concatenate([peer, proj], axis=1)
    terms = [send(peer, 0, 1), swap(peer, 1, 1)]
    grads = lax.optimization_barrier((*grads, m01, m10, m11, peer))[:2]
    own = qkv_sums(0, grads, normed_t, w3, b_own)
    own = jnp.concatenate([own, proj], axis=1)
    sums = added([own, terms[0], swap(own, 1, 0), terms[1]])
    sums = added(lat_terms(sums, 2))
    mixed = join(place, [m00, m10, m01, m11], rows, lon, lev)
    return (mixed, sums[:, : 3 * width].reshape(2, 3, width), sums[:, 3 * width :])


def solution(mesh):
    placed = (
        P(None, None, "lat", "tp"),
        P(None, None, "lat", "tp"),
        P(None, None, "tp"),
        P("tp", None),
        P(None, None, "tp"),
        P(),
        P(),
        P(),
    )
    return jax.shard_map(
        local,
        mesh=mesh,
        in_specs=placed,
        out_specs=(P(None, None, "lat", "tp"), P(None, None, "tp"), P()),
        check_vma=False,
    )
```

```python
import functools

import jax
import jax.numpy as jnp
from jax import lax
from jax.experimental import pallas as pl
from jax.experimental.pallas import tpu as pltpu
from jax.sharding import PartitionSpec as P

HD = 64
WLAT = 6
EPS = 1e-05
NEG = -1e30
F32 = jnp.float32
BF = jnp.bfloat16
SCALE = HD ** (-0.5)
NT = (((1,), (1,)), ((), ()))
TN = (((0,), (0,)), ((), ()))
LARGE = pl.CostEstimate(flops=8 * 10**9, bytes_accessed=10**7, transcendentals=10**6)
SMALL = pl.CostEstimate(flops=1, bytes_accessed=1, transcendentals=0)


def spec(n):
    return [pl.BlockSpec(memory_space=pltpu.VMEM)] * n


def params(mib):
    return pltpu.CompilerParams(vmem_limit_bytes=mib * 1024 * 1024)


def bounds_of(weight, logits_hi, logits_lo):
    top = jnp.max(weight, axis=0, keepdims=True)
    low = jnp.min(weight, axis=0, keepdims=True)
    hi = 1.0 / (1.0 + jnp.exp(-logits_hi))
    lo = 1.0 / (1.0 + jnp.exp(-logits_lo))
    return hi * top, lo * low, hi * (1.0 - hi) * top, lo * (1.0 - lo) * low


def clip_qkv_kernel(w_ref, c_ref, wc_ref, b_ref):
    def body(i, carry):
        w = w_ref[i].astype(F32)
        up, lw, fh, fl = bounds_of(w, c_ref[i, 0:1], c_ref[i, 1:2])
        wc_ref[i] = jnp.minimum(jnp.maximum(w, lw), up).astype(BF)
        b_ref[i, 0:1] = up
        b_ref[i, 1:2] = lw
        b_ref[i, 2:3] = fh
        b_ref[i, 3:4] = fl
        return carry

    lax.fori_loop(0, 3, body, 0)


def clip_qkv(w, clips):
    n, d, e = w.shape
    return pl.pallas_call(
        clip_qkv_kernel,
        out_shape=(
            jax.ShapeDtypeStruct((n, d, e), BF),
            jax.ShapeDtypeStruct((n, 8, e), F32),
        ),
        in_specs=spec(2),
        out_specs=tuple(spec(2)),
        compiler_params=params(24),
        cost_estimate=SMALL,
    )(w, clips)


def clip_proj_kernel(s_ref, w0, w1, a2, b2, a3, b3, c_ref, wc_ref, b_ref):
    second = s_ref[2] % 2 == 1

    def body(i, carry):
        cols = pl.ds(pl.multiple_of(i * 256, 256), 256)
        parts = [w0[:, cols].astype(F32), w1[:, cols].astype(F32)]
        for first_ref, other_ref in ((a2, b2), (a3, b3)):
            a, b = first_ref[:, cols].astype(F32), other_ref[:, cols].astype(F32)
            parts += [jnp.where(second, b, a), jnp.where(second, a, b)]
        w = jnp.concatenate(parts, axis=0)
        up, lw, fh, fl = bounds_of(w, c_ref[0:1, cols], c_ref[1:2, cols])
        wc = jnp.minimum(jnp.maximum(w, lw), up).astype(BF)
        wc_ref[:, cols] = wc
        b_ref[0:1, cols] = up
        b_ref[1:2, cols] = lw
        b_ref[2:3, cols] = fh
        b_ref[3:4, cols] = fl
        return carry

    lax.fori_loop(0, w0.shape[1] // 256, body, 0)


def clip_proj(place, shards, clips):
    e, d = shards[0].shape
    return pl.pallas_call(
        clip_proj_kernel,
        out_shape=(
            jax.ShapeDtypeStruct((4 * e, d), BF),
            jax.ShapeDtypeStruct((8, d), F32),
        ),
        in_specs=[pl.BlockSpec(memory_space=pltpu.SMEM)] + spec(7),
        out_specs=tuple(spec(2)),
        compiler_params=params(24),
        cost_estimate=SMALL,
    )(place, *shards, clips)


def stacked(block, mask_a, mask_b):
    return jnp.concatenate([block * mask_a, block * mask_b], axis=0)


def head_masks():
    lane = lax.broadcasted_iota(jnp.int32, (1, 2 * HD), 1)
    mask_a = jnp.where(lane < HD, 1.0, 0.0).astype(BF)
    mask_b = jnp.where(lane < HD, 0.0, 1.0).astype(BF)
    return mask_a, mask_b


def probs_t(k, q2, allowed):
    st = lax.dot_general(k, q2, NT, preferred_element_type=F32) * SCALE
    st = jnp.where(allowed, st, NEG)
    e = jnp.exp(st - jnp.max(st, axis=0, keepdims=True))
    return e * (1.0 / jnp.sum(e, axis=0, keepdims=True))


def merge_heads(t_block):
    both = t_block.T
    n = both.shape[0] // 2
    lane = lax.broadcasted_iota(jnp.int32, (n, 2 * HD), 1)
    return jnp.where(lane < HD, both[:n], both[n:])


def allowed_t(idk_ref, idq_ref, w, cells):
    rows = pl.ds(pl.multiple_of(w * cells, 16), cells)
    idk = idk_ref[rows, :]
    return (idk == idq_ref[w]) & (idk >= 0)


def blocks(refs):
    own, other, away = refs
    return own, away.at[0], other, away.at[1]


def forward_kernel(t_ref, *refs):
    pieces = blocks(refs[:3])
    wo_ref, wp_ref, idk_ref, idq_ref, normed_ref, qkv_ref, attn_ref = refs[3:]
    t = t_ref[0]
    n, width = pieces[0].shape
    d = 4 * width

    def norm(w, carry):
        rows = pl.ds(pl.multiple_of(w * 48, 16), 48)
        x = [r[rows, :].astype(F32) for r in pieces]
        mean = sum(jnp.sum(b, axis=-1, keepdims=True) for b in x) / d
        x = [b - mean for b in x]
        var = sum(jnp.sum(b * b, axis=-1, keepdims=True) for b in x) / d
        scale = lax.rsqrt(var + EPS)
        for k in range(4):
            cols = pl.ds(pl.multiple_of((t ^ k) * width, width), width)
            normed_ref[rows, cols] = (x[k] * scale).astype(BF)
        return carry

    lax.fori_loop(0, n // 48, norm, 0)

    def project(i, carry):
        for g, w_ref in enumerate((wo_ref, wp_ref)):
            qkv_ref[3 * g + i] = jnp.dot(
                normed_ref[...], w_ref[i], preferred_element_type=F32
            ).astype(BF)
        return carry

    lax.fori_loop(0, 3, project, 0)
    attend(qkv_ref, idk_ref, idq_ref, attn_ref, 0, 2)


def attend(qkv_ref, idk_ref, idq_ref, attn_ref, first, last):
    mask_a, mask_b = head_masks()
    cells = idk_ref.shape[0] // 4

    def window(w, carry):
        rows = pl.ds(pl.multiple_of(w * cells, 16), cells)
        to = pl.ds(pl.multiple_of((w - first) * cells, 16), cells)
        allowed = allowed_t(idk_ref, idq_ref, w, cells)
        for hp in range(4):
            g, lanes = hp // 2, slice(128 * (hp % 2), 128 * (hp % 2) + 128)
            q2 = stacked(qkv_ref[3 * g, rows, lanes], mask_a, mask_b)
            pt = probs_t(qkv_ref[3 * g + 1, rows, lanes], q2, allowed)
            ot = lax.dot_general(
                qkv_ref[3 * g + 2, rows, lanes], pt.astype(BF), TN, preferred_element_type=F32
            )
            attn_ref[to, 128 * hp : 128 * hp + 128] = merge_heads(ot).astype(BF)
        return carry

    lax.fori_loop(first, last, window, 0)


def last_kernel(qkv_ref, idk_ref, idq_ref, attn_ref):
    attend(qkv_ref, idk_ref, idq_ref, attn_ref, 2, 4)


def last_windows(qkv, idk, idq):
    n, width = qkv.shape[1:]
    return pl.pallas_call(
        last_kernel,
        out_shape=jax.ShapeDtypeStruct((n // 2, 2 * width), BF),
        in_specs=spec(3),
        out_specs=spec(1)[0],
        compiler_params=params(16),
        cost_estimate=pl.CostEstimate(flops=1, bytes_accessed=1, transcendentals=0),
    )(qkv, idk, idq)


def forward(t, pieces, wo, wp, idk, idq):
    n, width = pieces[0].shape
    d = 4 * width
    return pl.pallas_call(
        forward_kernel,
        out_shape=(
            jax.ShapeDtypeStruct((n, d), BF),
            jax.ShapeDtypeStruct((6, n, width), BF),
            jax.ShapeDtypeStruct((n // 2, 2 * width), BF),
        ),
        in_specs=[pl.BlockSpec(memory_space=pltpu.SMEM)] + spec(7),
        out_specs=tuple(spec(3)),
        compiler_params=params(20),
        cost_estimate=pl.CostEstimate(flops=8 * 10**9, bytes_accessed=10 * 10**6, transcendentals=10**6),
    )(t, *pieces, wo, wp, idk, idq)


def turn_kernel(normed_ref, a_ref, b_ref, normed_t, attn_t):
    d = normed_ref.shape[1]

    def body(i, carry):
        cols = pl.ds(pl.multiple_of(i * 256, 256), 256)
        normed_t[cols, :] = normed_ref[:, cols].T
        return carry

    lax.fori_loop(0, d // 256, body, 0)

    def body2(i, carry):
        cols = pl.ds(pl.multiple_of(i * 256, 256), 256)
        attn_t[cols, :] = jnp.concatenate([a_ref[:, cols], b_ref[:, cols]], axis=0).T
        return carry

    lax.fori_loop(0, a_ref.shape[1] // 256, body2, 0)


def turn(normed, attn):
    n, d = normed.shape
    e = attn[0].shape[1]
    return pl.pallas_call(
        turn_kernel,
        out_shape=(jax.ShapeDtypeStruct((d, n), BF), jax.ShapeDtypeStruct((e, n), BF)),
        in_specs=spec(3),
        out_specs=tuple(spec(2)),
        compiler_params=params(16),
        cost_estimate=SMALL,
    )(normed, *attn)


def output_kernel(group, t_ref, *refs):
    pieces, targets = blocks(refs[:3]), refs[3:7]
    own_ref, other_ref, wc_ref, idk_ref = refs[7:11]
    before, refs = refs[11 : 11 + 4 * group], refs[11 + 4 * group :]
    mixed, err_ref, y_ref = refs[:4], refs[4], refs[5]
    t = t_ref[0]
    n, width = pieces[0].shape
    cells = n // 4
    half = cells // 2
    e = own_ref.shape[1]
    for old, new in zip(before, mixed):
        new[: group * cells, :] = old[...]
    for k in range(4):
        x_ref, want_ref = pieces[k], targets[k]
        cols = pl.ds(pl.multiple_of((t ^ k) * width, width), width)
        y_ref[...] = jnp.dot(own_ref[...], wc_ref[:e, cols], preferred_element_type=F32) + jnp.dot(
            other_ref[...], wc_ref[e:, cols], preferred_element_type=F32
        )
        ys = []
        for i in range(2):
            at = slice(cells * i, cells * (i + 1))
            rows = slice(cells * (2 * group + i), cells * (2 * group + i + 1))
            y = x_ref[rows, :].astype(F32) + y_ref[at, :]
            ys.append(y)
            err = y - want_ref[rows, :].astype(F32)
            valid = idk_ref[rows, :] >= 0
            err_ref[at, cols] = jnp.where(valid, err, 0.0).astype(BF)
        if k < 2:
            at = slice(cells * group, cells * (group + 1))
            for s in range(2):
                part = slice(half * s, half * (s + 1))
                mixed[2 * s + k][at, :] = jnp.concatenate([y[part] for y in ys], axis=0).astype(BF)


def output(t, pieces, targets, own, other, wc, idk, before=()):
    n, width = pieces[0].shape
    group = 1 if before else 0
    piece = jax.ShapeDtypeStruct((n // 4 * (1 + group), width), BF)
    return pl.pallas_call(
        functools.partial(output_kernel, group),
        out_shape=(piece, piece, piece, piece, jax.ShapeDtypeStruct((n // 2, 4 * width), BF)),
        in_specs=[pl.BlockSpec(memory_space=pltpu.SMEM)] + spec(11 + len(before)),
        out_specs=tuple(spec(5)),
        scratch_shapes=[pltpu.VMEM((n // 2, width), F32)],
        compiler_params=params(20),
        cost_estimate=SMALL,
    )(t, *pieces, *targets, own, other, wc, idk, *before)


def probs_kernel(group, qkv_ref, idk_ref, idq_ref, p_ref):
    cells = idk_ref.shape[0] // 4
    mask_a, mask_b = head_masks()

    def window(i, carry):
        w = 2 * group + i
        rows = pl.ds(pl.multiple_of(w * cells, 16), cells)
        allowed = allowed_t(idk_ref, idq_ref, w, cells)
        for hp in range(4):
            g, lanes = hp // 2, slice(128 * (hp % 2), 128 * (hp % 2) + 128)
            q2 = stacked(qkv_ref[3 * g, rows, lanes], mask_a, mask_b)
            p_ref[4 * i + hp] = probs_t(qkv_ref[3 * g + 1, rows, lanes], q2, allowed)
        return carry

    lax.fori_loop(0, 2, window, 0)


def probs_of(group, qkv, idk, idq):
    n, width = qkv.shape[1:]
    return pl.pallas_call(
        functools.partial(probs_kernel, group),
        out_shape=jax.ShapeDtypeStruct((8, n // 4, n // 2), F32),
        in_specs=spec(3),
        out_specs=spec(1)[0],
        compiler_params=params(16),
        cost_estimate=SMALL,
    )(qkv, idk, idq)


def masked_sums(grad, w, bounds):
    g_hi = jnp.sum(jnp.where(w > bounds[0:1], grad, 0.0), axis=0, keepdims=True) * bounds[2:3]
    g_lo = jnp.sum(jnp.where(w < bounds[1:2], grad, 0.0), axis=0, keepdims=True) * bounds[3:4]
    return g_hi, g_lo


def proj_sums_kernel(e0_ref, e1_ref, attn_t, po_ref, pp_ref, pb_ref, proj_ref):
    def proj_part(i, carry):
        cols = pl.ds(pl.multiple_of(i * 256, 256), 256)
        err = jnp.concatenate([e0_ref[:, cols], e1_ref[:, cols]], axis=0)
        grad = jnp.dot(attn_t[...], err, preferred_element_type=F32)
        n = po_ref.shape[0]
        b = pb_ref[:, cols]
        h0, l0 = masked_sums(grad[:n], po_ref[:, cols].astype(F32), b)
        h1, l1 = masked_sums(grad[n:], pp_ref[:, cols].astype(F32), b)
        proj_ref[0:1, cols] = h0 + h1
        proj_ref[1:2, cols] = l0 + l1
        return carry

    lax.fori_loop(0, 4, proj_part, 0)


def proj_sums(errs, attn_t, po, pp, pb):
    return pl.pallas_call(
        proj_sums_kernel,
        out_shape=jax.ShapeDtypeStruct((2, errs[0].shape[1]), F32),
        in_specs=spec(6),
        out_specs=spec(1)[0],
        compiler_params=params(16),
        cost_estimate=pl.CostEstimate(flops=10**9, bytes_accessed=3 * 10**6, transcendentals=0),
    )(*errs, attn_t, po, pp, pb)


def backward_kernel(group, err_ref, wc_ref, qkv_ref, p_ref, g_ref, d_ref):
    e = d_ref.shape[1]
    cells = d_ref.shape[0] // 2
    d_ref[...] = lax.dot_general(err_ref[...], wc_ref[:e], NT, preferred_element_type=F32).astype(BF)
    mask_a, mask_b = head_masks()

    def window(i, carry):
        rows = pl.ds(pl.multiple_of((2 * group + i) * cells, 16), cells)
        at = pl.ds(pl.multiple_of(i * cells, 16), cells)
        for hp in range(4):
            g, lanes = hp // 2, slice(128 * (hp % 2), 128 * (hp % 2) + 128)
            q2 = stacked(qkv_ref[3 * g, rows, lanes], mask_a, mask_b)
            k = qkv_ref[3 * g + 1, rows, lanes]
            v = qkv_ref[3 * g + 2, rows, lanes]
            pt = p_ref[4 * i + hp]
            d2 = stacked(d_ref[at, 128 * hp : 128 * hp + 128], mask_a, mask_b)
            g_ref[3 * g + 2, at, lanes] = jnp.dot(
                pt.astype(BF), d2, preferred_element_type=F32
            ).astype(BF)
            dpt = lax.dot_general(v, d2, NT, preferred_element_type=F32)
            gst = (pt * (dpt - jnp.sum(pt * dpt, axis=0, keepdims=True))).astype(BF)
            g_ref[3 * g + 1, at, lanes] = (
                jnp.dot(gst, q2, preferred_element_type=F32) * SCALE
            ).astype(BF)
            gqt = lax.dot_general(k, gst, TN, preferred_element_type=F32) * SCALE
            g_ref[3 * g, at, lanes] = merge_heads(gqt).astype(BF)
        return carry

    lax.fori_loop(0, 2, window, 0)


def backward(group, err, wc, qkv, probs):
    n, width = qkv.shape[1:]
    return pl.pallas_call(
        functools.partial(backward_kernel, group),
        out_shape=jax.ShapeDtypeStruct((6, n // 2, width), BF),
        in_specs=spec(4),
        out_specs=spec(1)[0],
        scratch_shapes=[pltpu.VMEM((n // 2, 2 * width), BF)],
        compiler_params=params(20),
        cost_estimate=LARGE if group else SMALL,
    )(err, wc, qkv, probs)


def qkv_sums_kernel(side, g0_ref, g1_ref, normed_t, w_ref, b_ref, to_ref):
    width = g0_ref.shape[2]

    def qkv_part(i, carry):
        cells = jnp.concatenate([g0_ref[3 * side + i], g1_ref[3 * side + i]], axis=0)
        grad = jnp.dot(normed_t[...], cells, preferred_element_type=F32)
        hi, lo = masked_sums(grad, w_ref[i].astype(F32), b_ref[i])
        to_ref[0:1, pl.ds(pl.multiple_of(i * width, width), width)] = hi
        to_ref[1:2, pl.ds(pl.multiple_of(i * width, width), width)] = lo
        return carry

    lax.fori_loop(0, 3, qkv_part, 0)


def qkv_sums(side, g, normed_t, w, b):
    width = g[0].shape[2]
    return pl.pallas_call(
        functools.partial(qkv_sums_kernel, side),
        out_shape=jax.ShapeDtypeStruct((2, 3 * width), F32),
        in_specs=spec(5),
        out_specs=spec(1)[0],
        compiler_params=params(20),
        cost_estimate=LARGE,
    )(*g, normed_t, w, b)


def halves_kernel(x_ref, low_ref, up_ref, sems):
    half = low_ref.shape[1]
    low = pltpu.make_async_copy(x_ref.at[:, :half], low_ref, sems.at[0])
    up = pltpu.make_async_copy(x_ref.at[:, half:], up_ref, sems.at[1])
    low.start()
    up.start()
    low.wait()
    up.wait()


def halves_of(block):
    rows, lon, lev, width = block.shape
    half = jax.ShapeDtypeStruct((rows, lon // 2, lev, width), BF)
    return pl.pallas_call(
        halves_kernel,
        out_shape=(half, half),
        in_specs=[pl.BlockSpec(memory_space=pltpu.HBM)],
        out_specs=tuple(spec(2)),
        scratch_shapes=[pltpu.SemaphoreType.DMA((2,))],
        compiler_params=params(16),
        cost_estimate=SMALL,
    )(block)


def split_kernel(s_ref, *refs):
    offset, core = s_ref[0], s_ref[1]
    pairs = (len(refs) - 1) // 3
    rows, lon, lev, width = refs[1].shape
    many = (rows + WLAT) // 2
    half = lon * lev
    cells = 2 * WLAT * half
    for rel in range(2):
        base = many * (core ^ rel) - offset

        def body(w, carry):
            at = pl.ds(pl.multiple_of(w * cells, 16), cells)
            for i in range(pairs):
                up_ref, low_ref = refs[2 * i : 2 * i + 2]
                parts = []
                for ref, part in ((up_ref, slice(up_ref.shape[1] - lon, up_ref.shape[1])), (low_ref, slice(0, lon))):
                    for j in range(WLAT):
                        r = base + WLAT * w + j
                        v = ref[jnp.clip(r, 0, rows - 1), part].astype(F32).reshape(half, width)
                        parts.append(jnp.where((r >= 0) & (r < rows), v, 0.0))
                block = jnp.concatenate(parts, axis=0).astype(BF)
                if rel:
                    refs[-1][i, at, :] = block
                else:
                    refs[2 * pairs + i][at, :] = block
            return carry

        lax.fori_loop(0, many // WLAT, body, 0)


def split(place, *halves):
    rows, lon, lev, width = halves[1].shape
    pairs = len(halves) // 2
    n = (rows + WLAT) * lon * lev
    return pl.pallas_call(
        split_kernel,
        out_shape=(jax.ShapeDtypeStruct((n, width), BF),) * pairs
        + (jax.ShapeDtypeStruct((pairs, n, width), BF),),
        in_specs=[pl.BlockSpec(memory_space=pltpu.SMEM)] + spec(2 * pairs),
        out_specs=tuple(spec(pairs + 1)),
        compiler_params=params(16),
        cost_estimate=SMALL,
    )(place, *halves)


def cell_at(c, window):
    cells = 2 * WLAT * window
    w = sum((c >= i * cells).astype(jnp.int32) for i in range(1, 4))
    c = c - w * cells
    s = (c >= WLAT * window).astype(jnp.int32)
    c = c - s * WLAT * window
    r = sum((c >= i * window).astype(jnp.int32) for i in range(1, WLAT))
    c = c - r * window
    return w * WLAT + r, s * (window // 2) + (c >> 1), c & 1


def ids_kernel(s_ref, ids_ref, idk_ref, idq_ref):
    offset, core, sector = s_ref[0], s_ref[1], s_ref[2]
    rows, lev, total = ids_ref.shape
    n = idk_ref.shape[0]
    cells = n // 4
    window = cells // (2 * WLAT)
    many = (rows + WLAT) // 2
    ids = ids_ref[...].astype(F32).reshape(rows * lev, total)

    def find(c):
        r, lon, level = cell_at(c, window)
        r = r + many * core - offset
        lon = lon + sector * window + window // 2
        lon = jnp.where(lon >= total, lon - total, lon)
        valid = (r >= 0) & (r < rows)
        return jnp.where(valid, 2 * r + level, -1), lon, valid

    spot, lon, valid = find(lax.broadcasted_iota(jnp.int32, (n, 1), 0))
    at = lax.broadcasted_iota(jnp.int32, (n, rows * lev), 1) == spot
    found = jnp.dot(jnp.where(at, 1.0, 0.0), ids, preferred_element_type=F32)
    there = lax.broadcasted_iota(jnp.int32, (n, total), 1) == lon
    found = jnp.sum(jnp.where(there, found, 0.0), axis=1, keepdims=True)
    idk_ref[...] = jnp.where(valid, found, -1.0).astype(jnp.int32)
    for w in range(4):
        lane = lax.broadcasted_iota(jnp.int32, (1, 2 * cells), 1)
        spot, lon, valid = find(w * cells + jnp.where(lane >= cells, lane - cells, lane))
        there = lax.broadcasted_iota(jnp.int32, (total, 2 * cells), 0) == lon
        found = jnp.dot(ids, jnp.where(there, 1.0, 0.0), preferred_element_type=F32)
        at = lax.broadcasted_iota(jnp.int32, (rows * lev, 2 * cells), 0) == spot
        found = jnp.sum(jnp.where(at, found, 0.0), axis=0, keepdims=True)
        idq_ref[w] = jnp.where(valid, found, -1.0).astype(jnp.int32)


def window_ids(place, ids, cells):
    return pl.pallas_call(
        ids_kernel,
        out_shape=(
            jax.ShapeDtypeStruct((4 * cells, 1), jnp.int32),
            jax.ShapeDtypeStruct((4, 1, 2 * cells), jnp.int32),
        ),
        in_specs=[pl.BlockSpec(memory_space=pltpu.SMEM)] + spec(1),
        out_specs=tuple(spec(2)),
        compiler_params=params(16),
        cost_estimate=SMALL,
    )(place, ids)


def join_kernel(s_ref, a0, a1, b0, b1, out_ref, grid_ref):
    offset, core = s_ref[0], s_ref[1]
    rows, lon, lev, width = out_ref.shape
    many = (rows + WLAT) // 2
    half = lon * lev // 2
    for rel, ins in ((0, (a0, a1)), (1, (b0, b1))):
        base = many * (core ^ rel)
        for s in range(2):
            for i in range(many // 4):
                v = ins[s][4 * half * i : 4 * half * (i + 1), :].astype(F32)
                for j in range(4):
                    grid_ref[base + 4 * i + j, half * (1 - s) : half * (2 - s), :] = v[
                        half * j : half * (j + 1)
                    ]

    def body(i, carry):
        for j in range(2):
            r = 2 * i + j
            out_ref[r] = grid_ref[r + offset].reshape(lon, lev, width).astype(BF)
        return carry

    lax.fori_loop(0, rows // 2, body, 0)


def join(place, parts, rows, lon, lev):
    n, width = parts[0].shape
    out = pl.pallas_call(
        join_kernel,
        out_shape=jax.ShapeDtypeStruct((rows, lon, lev, width), BF),
        in_specs=[pl.BlockSpec(memory_space=pltpu.SMEM)] + spec(4),
        out_specs=spec(1)[0],
        scratch_shapes=[pltpu.VMEM((rows + WLAT, lon * lev, width), F32)],
        compiler_params=params(16),
        cost_estimate=SMALL,
    )(place, *parts)
    return jnp.transpose(out, (0, 2, 1, 3))


def send(block, shift, flip):
    count, tp = lax.axis_size("lat"), lax.axis_size("tp")
    route = [
        (u * tp + t, ((u + shift) % count) * tp + (t ^ flip)) for u in range(count) for t in range(tp)
    ]
    return lax.ppermute(block, ("lat", "tp"), route)


def swap(block, other, flip):
    count, tp = lax.axis_size("lat"), lax.axis_size("tp")
    route = [(u * tp + t, (u ^ other) * tp + (t ^ flip)) for u in range(count) for t in range(tp)]
    return lax.ppermute(block, ("lat", "tp"), route)


def lat_terms(block, bit):
    count = lax.axis_size("lat")
    terms = [block]
    while bit < count:
        block = added(terms)
        terms = [block, swap(block, bit, 0)]
        if 4 * bit <= count:
            terms += [swap(block, 2 * bit, 0), swap(block, 3 * bit, 0)]
        bit *= len(terms)
    return terms


def added(terms):
    while len(terms) > 1:
        terms = [a + b for a, b in zip(terms[::2], terms[1::2])]
    return terms[0]


def after(block, *others):
    return lax.optimization_barrier((block, *others))[0]


def local(features, target, w_qkv, w_proj, qkv_clip, proj_clip, shift_offset, region_ids):
    rows, lev, lon, width = features.shape
    half = lon // 2
    sector = lax.axis_index("lat")
    t = lax.axis_index("tp")
    t_arr = jnp.reshape(t, (1,)).astype(jnp.int32)
    place = jnp.stack([shift_offset[0], t % 2, sector]).astype(jnp.int32)

    f_raw, t_raw = (jnp.transpose(block, (0, 2, 1, 3)) for block in (features, target))
    f_low, f_up = halves_of(f_raw)
    f_low, f_up, w_qkv, w_proj = lax.optimization_barrier((f_low, f_up, w_qkv, w_proj))
    f_up_y = send(f_up, 0, 2)
    f_low = send(f_low, -1, 0)

    w3 = jnp.transpose(w_qkv, (1, 0, 2))
    c3 = jnp.transpose(qkv_clip, (1, 0, 2))
    w3_peer = send(w3, 0, 1)
    c3_peer = send(c3, 0, 1)
    share = w_proj.shape[0] // 2
    w1 = send(w_proj, 0, 1)
    wc_own, b_own = clip_qkv(w3, c3)
    slab = after(w_proj, wc_own)
    slab = send(lax.dynamic_slice_in_dim(slab, share * (sector % 2), share, 0), 0, 2)
    wc_peer, b_peer = clip_qkv(w3_peer, c3_peer)
    idk, idq = window_ids(place, region_ids, WLAT * lev * lon)
    f_up_y, f_low, w1, t_low, wc_own = lax.optimization_barrier(
        (f_up_y, f_low, w1, t_raw[:, :half], wc_own)
    )
    f_low_y = send(f_low, 0, 2)
    t_low = send(t_low, -1, 0)
    f_low_y, t_low, slab, wc_peer, idk, idq = lax.optimization_barrier(
        (f_low_y, t_low, slab, wc_peer, idk, idq)
    )
    x_0, x_2, x_away = split(place, f_raw, f_low, f_up_y, f_low_y)
    pieces = (x_0, x_2, send(x_away, 0, 1))

    t_own, t_away = split(place, after(t_raw, x_0), t_low)
    t_away = t_away.reshape(t_own.shape)
    targets = (t_own, send(t_away, 0, 1), send(t_own, 0, 2), send(t_away, 0, 3))
    more = swap(slab, 1, 0)

    normed, qkv, attn_0 = forward(t_arr, pieces, wc_own, wc_peer, idk, idq)
    other_0 = send(attn_0, 0, 2)
    probs_0 = probs_of(0, qkv, idk, idq)
    attn_1 = last_windows(after(qkv, probs_0, *targets, more), idk, idq)
    slab_3, more_3 = send(after(slab, attn_1), 0, 1), send(after(more, attn_1), 0, 1)
    pc, pb = clip_proj(place, [w_proj, w1, slab, more, slab_3, more_3], proj_clip)
    other_1 = send(attn_1, 0, 2)
    normed_t, attn_t = turn(normed, (attn_0, attn_1))
    probs = (probs_0, probs_of(1, after(qkv, attn_1), idk, idq))

    *mixed, err_0 = output(t_arr, pieces, targets, attn_0, other_0, pc, idk)
    grads_0 = backward(0, err_0, pc, qkv, probs[0])
    other_1 = after(other_1, grads_0)
    m00, m01, m10, m11, err_1 = output(t_arr, pieces, targets, attn_1, other_1, pc, idk, mixed)
    m01 = send(m01, 0, 1)
    m10 = send(m10, 1, 0)
    m11 = send(m11, 1, 1)
    proj = proj_sums((err_0, err_1), attn_t, w_proj, w1, pb)
    proj_y = send(proj, 0, 2)
    grads = (grads_0, backward(1, err_1, pc, qkv, probs[1]))
    peer = qkv_sums(1, grads, normed_t, w3_peer, b_peer)
    proj = proj + proj_y
    peer = jnp.concatenate([peer, proj], axis=1)
    terms = [send(peer, 0, 1), swap(peer, 1, 1)]
    grads = lax.optimization_barrier((*grads, m01, m10, m11, peer))[:2]
    own = qkv_sums(0, grads, normed_t, w3, b_own)
    own = jnp.concatenate([own, proj], axis=1)
    sums = added([own, terms[0], swap(own, 1, 0), terms[1]])
    sums = added(lat_terms(sums, 2))
    mixed = join(place, [m00, m10, m01, m11], rows, lon, lev)
    return (mixed, sums[:, : 3 * width].reshape(2, 3, width), sums[:, 3 * width :])


def solution(mesh):
    placed = (
        P(None, None, "lat", "tp"),
        P(None, None, "lat", "tp"),
        P(None, None, "tp"),
        P("tp", None),
        P(None, None, "tp"),
        P(),
        P(),
        P(),
    )
    return jax.shard_map(
        local,
        mesh=mesh,
        in_specs=placed,
        out_specs=(P(None, None, "lat", "tp"), P(None, None, "tp"), P()),
        check_vma=False,
    )
```

```python
import functools

import jax
import jax.numpy as jnp
from jax import lax
from jax.experimental import pallas as pl
from jax.experimental.pallas import tpu as pltpu
from jax.sharding import PartitionSpec as P

HD = 64
WLAT = 6
EPS = 1e-05
NEG = -1e30
F32 = jnp.float32
BF = jnp.bfloat16
SCALE = HD ** (-0.5)
NT = (((1,), (1,)), ((), ()))
TN = (((0,), (0,)), ((), ()))
LARGE = pl.CostEstimate(flops=8 * 10**9, bytes_accessed=10**7, transcendentals=10**6)
SMALL = pl.CostEstimate(flops=1, bytes_accessed=1, transcendentals=0)


def spec(n):
    return [pl.BlockSpec(memory_space=pltpu.VMEM)] * n


def params(mib):
    return pltpu.CompilerParams(vmem_limit_bytes=mib * 1024 * 1024)


def bounds_of(weight, logits_hi, logits_lo):
    top = jnp.max(weight, axis=0, keepdims=True)
    low = jnp.min(weight, axis=0, keepdims=True)
    hi = 1.0 / (1.0 + jnp.exp(-logits_hi))
    lo = 1.0 / (1.0 + jnp.exp(-logits_lo))
    return hi * top, lo * low, hi * (1.0 - hi) * top, lo * (1.0 - lo) * low


def clip_qkv_kernel(w_ref, c_ref, wc_ref, b_ref):
    def body(i, carry):
        w = w_ref[i].astype(F32)
        up, lw, fh, fl = bounds_of(w, c_ref[i, 0:1], c_ref[i, 1:2])
        wc_ref[i] = jnp.minimum(jnp.maximum(w, lw), up).astype(BF)
        b_ref[i, 0:1] = up
        b_ref[i, 1:2] = lw
        b_ref[i, 2:3] = fh
        b_ref[i, 3:4] = fl
        return carry

    lax.fori_loop(0, 3, body, 0)


def clip_qkv(w, clips):
    n, d, e = w.shape
    return pl.pallas_call(
        clip_qkv_kernel,
        out_shape=(
            jax.ShapeDtypeStruct((n, d, e), BF),
            jax.ShapeDtypeStruct((n, 8, e), F32),
        ),
        in_specs=spec(2),
        out_specs=tuple(spec(2)),
        compiler_params=params(24),
        cost_estimate=SMALL,
    )(w, clips)


def clip_proj_kernel(s_ref, w0, w1, a2, b2, a3, b3, c_ref, wc_ref, b_ref):
    second = s_ref[2] % 2 == 1

    def body(i, carry):
        cols = pl.ds(pl.multiple_of(i * 256, 256), 256)
        parts = [w0[:, cols].astype(F32), w1[:, cols].astype(F32)]
        for first_ref, other_ref in ((a2, b2), (a3, b3)):
            a, b = first_ref[:, cols].astype(F32), other_ref[:, cols].astype(F32)
            parts += [jnp.where(second, b, a), jnp.where(second, a, b)]
        w = jnp.concatenate(parts, axis=0)
        up, lw, fh, fl = bounds_of(w, c_ref[0:1, cols], c_ref[1:2, cols])
        wc = jnp.minimum(jnp.maximum(w, lw), up).astype(BF)
        wc_ref[:, cols] = wc
        b_ref[0:1, cols] = up
        b_ref[1:2, cols] = lw
        b_ref[2:3, cols] = fh
        b_ref[3:4, cols] = fl
        return carry

    lax.fori_loop(0, w0.shape[1] // 256, body, 0)


def clip_proj(place, shards, clips):
    e, d = shards[0].shape
    return pl.pallas_call(
        clip_proj_kernel,
        out_shape=(
            jax.ShapeDtypeStruct((4 * e, d), BF),
            jax.ShapeDtypeStruct((8, d), F32),
        ),
        in_specs=[pl.BlockSpec(memory_space=pltpu.SMEM)] + spec(7),
        out_specs=tuple(spec(2)),
        compiler_params=params(24),
        cost_estimate=SMALL,
    )(place, *shards, clips)


def stacked(block, mask_a, mask_b):
    return jnp.concatenate([block * mask_a, block * mask_b], axis=0)


def head_masks():
    lane = lax.broadcasted_iota(jnp.int32, (1, 2 * HD), 1)
    mask_a = jnp.where(lane < HD, 1.0, 0.0).astype(BF)
    mask_b = jnp.where(lane < HD, 0.0, 1.0).astype(BF)
    return mask_a, mask_b


def probs_t(k, q2, allowed):
    st = lax.dot_general(k, q2, NT, preferred_element_type=F32) * SCALE
    st = jnp.where(allowed, st, NEG)
    e = jnp.exp(st - jnp.max(st, axis=0, keepdims=True))
    return e * (1.0 / jnp.sum(e, axis=0, keepdims=True))


def merge_heads(t_block):
    both = t_block.T
    n = both.shape[0] // 2
    lane = lax.broadcasted_iota(jnp.int32, (n, 2 * HD), 1)
    return jnp.where(lane < HD, both[:n], both[n:])


def allowed_t(idk_ref, idq_ref, w, cells):
    rows = pl.ds(pl.multiple_of(w * cells, 16), cells)
    idk = idk_ref[rows, :]
    return (idk == idq_ref[w]) & (idk >= 0)


def blocks(refs):
    own, other, away = refs
    return own, away.at[0], other, away.at[1]


def forward_kernel(t_ref, *refs):
    pieces = blocks(refs[:3])
    wo_ref, wp_ref, idk_ref, idq_ref, normed_ref, qkv_ref, attn_ref = refs[3:]
    t = t_ref[0]
    n, width = pieces[0].shape
    d = 4 * width

    def norm(w, carry):
        rows = pl.ds(pl.multiple_of(w * 48, 16), 48)
        x = [r[rows, :].astype(F32) for r in pieces]
        mean = sum(jnp.sum(b, axis=-1, keepdims=True) for b in x) / d
        x = [b - mean for b in x]
        var = sum(jnp.sum(b * b, axis=-1, keepdims=True) for b in x) / d
        scale = lax.rsqrt(var + EPS)
        for k in range(4):
            cols = pl.ds(pl.multiple_of((t ^ k) * width, width), width)
            normed_ref[rows, cols] = (x[k] * scale).astype(BF)
        return carry

    lax.fori_loop(0, n // 48, norm, 0)

    def project(i, carry):
        for g, w_ref in enumerate((wo_ref, wp_ref)):
            qkv_ref[3 * g + i] = jnp.dot(
                normed_ref[...], w_ref[i], preferred_element_type=F32
            ).astype(BF)
        return carry

    lax.fori_loop(0, 3, project, 0)
    attend(qkv_ref, idk_ref, idq_ref, attn_ref, 0, 2)


def attend(qkv_ref, idk_ref, idq_ref, attn_ref, first, last):
    mask_a, mask_b = head_masks()
    cells = idk_ref.shape[0] // 4

    def window(w, carry):
        rows = pl.ds(pl.multiple_of(w * cells, 16), cells)
        to = pl.ds(pl.multiple_of((w - first) * cells, 16), cells)
        allowed = allowed_t(idk_ref, idq_ref, w, cells)
        for hp in range(4):
            g, lanes = hp // 2, slice(128 * (hp % 2), 128 * (hp % 2) + 128)
            q2 = stacked(qkv_ref[3 * g, rows, lanes], mask_a, mask_b)
            pt = probs_t(qkv_ref[3 * g + 1, rows, lanes], q2, allowed)
            ot = lax.dot_general(
                qkv_ref[3 * g + 2, rows, lanes], pt.astype(BF), TN, preferred_element_type=F32
            )
            attn_ref[to, 128 * hp : 128 * hp + 128] = merge_heads(ot).astype(BF)
        return carry

    lax.fori_loop(first, last, window, 0)


def last_kernel(qkv_ref, idk_ref, idq_ref, attn_ref):
    attend(qkv_ref, idk_ref, idq_ref, attn_ref, 2, 4)


def last_windows(qkv, idk, idq):
    n, width = qkv.shape[1:]
    return pl.pallas_call(
        last_kernel,
        out_shape=jax.ShapeDtypeStruct((n // 2, 2 * width), BF),
        in_specs=spec(3),
        out_specs=spec(1)[0],
        compiler_params=params(16),
        cost_estimate=pl.CostEstimate(flops=1, bytes_accessed=1, transcendentals=0),
    )(qkv, idk, idq)


def forward(t, pieces, wo, wp, idk, idq):
    n, width = pieces[0].shape
    d = 4 * width
    return pl.pallas_call(
        forward_kernel,
        out_shape=(
            jax.ShapeDtypeStruct((n, d), BF),
            jax.ShapeDtypeStruct((6, n, width), BF),
            jax.ShapeDtypeStruct((n // 2, 2 * width), BF),
        ),
        in_specs=[pl.BlockSpec(memory_space=pltpu.SMEM)] + spec(7),
        out_specs=tuple(spec(3)),
        compiler_params=params(20),
        cost_estimate=pl.CostEstimate(flops=8 * 10**9, bytes_accessed=10 * 10**6, transcendentals=10**6),
    )(t, *pieces, wo, wp, idk, idq)


def turn_kernel(normed_ref, a_ref, b_ref, normed_t, attn_t):
    d = normed_ref.shape[1]

    def body(i, carry):
        cols = pl.ds(pl.multiple_of(i * 256, 256), 256)
        normed_t[cols, :] = normed_ref[:, cols].T
        return carry

    lax.fori_loop(0, d // 256, body, 0)

    def body2(i, carry):
        cols = pl.ds(pl.multiple_of(i * 256, 256), 256)
        attn_t[cols, :] = jnp.concatenate([a_ref[:, cols], b_ref[:, cols]], axis=0).T
        return carry

    lax.fori_loop(0, a_ref.shape[1] // 256, body2, 0)


def turn(normed, attn):
    n, d = normed.shape
    e = attn[0].shape[1]
    return pl.pallas_call(
        turn_kernel,
        out_shape=(jax.ShapeDtypeStruct((d, n), BF), jax.ShapeDtypeStruct((e, n), BF)),
        in_specs=spec(3),
        out_specs=tuple(spec(2)),
        compiler_params=params(16),
        cost_estimate=SMALL,
    )(normed, *attn)


def output_kernel(group, t_ref, *refs):
    pieces, targets = blocks(refs[:3]), refs[3:7]
    own_ref, other_ref, wc_ref, idk_ref = refs[7:11]
    before, refs = refs[11 : 11 + 4 * group], refs[11 + 4 * group :]
    mixed, err_ref, y_ref = refs[:4], refs[4], refs[5]
    t = t_ref[0]
    n, width = pieces[0].shape
    cells = n // 4
    half = cells // 2
    e = own_ref.shape[1]
    for old, new in zip(before, mixed):
        new[: group * cells, :] = old[...]
    for k in range(4):
        x_ref, want_ref = pieces[k], targets[k]
        cols = pl.ds(pl.multiple_of((t ^ k) * width, width), width)
        y_ref[...] = jnp.dot(own_ref[...], wc_ref[:e, cols], preferred_element_type=F32) + jnp.dot(
            other_ref[...], wc_ref[e:, cols], preferred_element_type=F32
        )
        ys = []
        for i in range(2):
            at = slice(cells * i, cells * (i + 1))
            rows = slice(cells * (2 * group + i), cells * (2 * group + i + 1))
            y = x_ref[rows, :].astype(F32) + y_ref[at, :]
            ys.append(y)
            err = y - want_ref[rows, :].astype(F32)
            valid = idk_ref[rows, :] >= 0
            err_ref[at, cols] = jnp.where(valid, err, 0.0).astype(BF)
        if k < 2:
            at = slice(cells * group, cells * (group + 1))
            for s in range(2):
                part = slice(half * s, half * (s + 1))
                mixed[2 * s + k][at, :] = jnp.concatenate([y[part] for y in ys], axis=0).astype(BF)


def output(t, pieces, targets, own, other, wc, idk, before=()):
    n, width = pieces[0].shape
    group = 1 if before else 0
    piece = jax.ShapeDtypeStruct((n // 4 * (1 + group), width), BF)
    return pl.pallas_call(
        functools.partial(output_kernel, group),
        out_shape=(piece, piece, piece, piece, jax.ShapeDtypeStruct((n // 2, 4 * width), BF)),
        in_specs=[pl.BlockSpec(memory_space=pltpu.SMEM)] + spec(11 + len(before)),
        out_specs=tuple(spec(5)),
        scratch_shapes=[pltpu.VMEM((n // 2, width), F32)],
        compiler_params=params(20),
        cost_estimate=SMALL,
    )(t, *pieces, *targets, own, other, wc, idk, *before)


def probs_kernel(group, qkv_ref, idk_ref, idq_ref, p_ref):
    cells = idk_ref.shape[0] // 4
    mask_a, mask_b = head_masks()

    def window(i, carry):
        w = 2 * group + i
        rows = pl.ds(pl.multiple_of(w * cells, 16), cells)
        allowed = allowed_t(idk_ref, idq_ref, w, cells)
        for hp in range(4):
            g, lanes = hp // 2, slice(128 * (hp % 2), 128 * (hp % 2) + 128)
            q2 = stacked(qkv_ref[3 * g, rows, lanes], mask_a, mask_b)
            p_ref[4 * i + hp] = probs_t(qkv_ref[3 * g + 1, rows, lanes], q2, allowed)
        return carry

    lax.fori_loop(0, 2, window, 0)


def probs_of(group, qkv, idk, idq):
    n, width = qkv.shape[1:]
    return pl.pallas_call(
        functools.partial(probs_kernel, group),
        out_shape=jax.ShapeDtypeStruct((8, n // 4, n // 2), F32),
        in_specs=spec(3),
        out_specs=spec(1)[0],
        compiler_params=params(16),
        cost_estimate=SMALL,
    )(qkv, idk, idq)


def masked_sums(grad, w, bounds):
    g_hi = jnp.sum(jnp.where(w > bounds[0:1], grad, 0.0), axis=0, keepdims=True) * bounds[2:3]
    g_lo = jnp.sum(jnp.where(w < bounds[1:2], grad, 0.0), axis=0, keepdims=True) * bounds[3:4]
    return g_hi, g_lo


def proj_sums_kernel(e0_ref, e1_ref, attn_t, po_ref, pp_ref, pb_ref, proj_ref):
    def proj_part(i, carry):
        cols = pl.ds(pl.multiple_of(i * 256, 256), 256)
        err = jnp.concatenate([e0_ref[:, cols], e1_ref[:, cols]], axis=0)
        grad = jnp.dot(attn_t[...], err, preferred_element_type=F32)
        n = po_ref.shape[0]
        b = pb_ref[:, cols]
        h0, l0 = masked_sums(grad[:n], po_ref[:, cols].astype(F32), b)
        h1, l1 = masked_sums(grad[n:], pp_ref[:, cols].astype(F32), b)
        proj_ref[0:1, cols] = h0 + h1
        proj_ref[1:2, cols] = l0 + l1
        return carry

    lax.fori_loop(0, 4, proj_part, 0)


def proj_sums(errs, attn_t, po, pp, pb):
    return pl.pallas_call(
        proj_sums_kernel,
        out_shape=jax.ShapeDtypeStruct((2, errs[0].shape[1]), F32),
        in_specs=spec(6),
        out_specs=spec(1)[0],
        compiler_params=params(16),
        cost_estimate=pl.CostEstimate(flops=10**9, bytes_accessed=3 * 10**6, transcendentals=0),
    )(*errs, attn_t, po, pp, pb)


def backward_kernel(group, err_ref, wc_ref, qkv_ref, p_ref, g_ref, d_ref):
    e = d_ref.shape[1]
    cells = d_ref.shape[0] // 2
    d_ref[...] = lax.dot_general(err_ref[...], wc_ref[:e], NT, preferred_element_type=F32).astype(BF)
    mask_a, mask_b = head_masks()

    def window(i, carry):
        rows = pl.ds(pl.multiple_of((2 * group + i) * cells, 16), cells)
        at = pl.ds(pl.multiple_of(i * cells, 16), cells)
        for hp in range(4):
            g, lanes = hp // 2, slice(128 * (hp % 2), 128 * (hp % 2) + 128)
            q2 = stacked(qkv_ref[3 * g, rows, lanes], mask_a, mask_b)
            k = qkv_ref[3 * g + 1, rows, lanes]
            v = qkv_ref[3 * g + 2, rows, lanes]
            pt = p_ref[4 * i + hp]
            d2 = stacked(d_ref[at, 128 * hp : 128 * hp + 128], mask_a, mask_b)
            g_ref[3 * g + 2, at, lanes] = jnp.dot(
                pt.astype(BF), d2, preferred_element_type=F32
            ).astype(BF)
            dpt = lax.dot_general(v, d2, NT, preferred_element_type=F32)
            gst = (pt * (dpt - jnp.sum(pt * dpt, axis=0, keepdims=True))).astype(BF)
            g_ref[3 * g + 1, at, lanes] = (
                jnp.dot(gst, q2, preferred_element_type=F32) * SCALE
            ).astype(BF)
            gqt = lax.dot_general(k, gst, TN, preferred_element_type=F32) * SCALE
            g_ref[3 * g, at, lanes] = merge_heads(gqt).astype(BF)
        return carry

    lax.fori_loop(0, 2, window, 0)


def backward(group, err, wc, qkv, probs):
    n, width = qkv.shape[1:]
    return pl.pallas_call(
        functools.partial(backward_kernel, group),
        out_shape=jax.ShapeDtypeStruct((6, n // 2, width), BF),
        in_specs=spec(4),
        out_specs=spec(1)[0],
        scratch_shapes=[pltpu.VMEM((n // 2, 2 * width), BF)],
        compiler_params=params(20),
        cost_estimate=LARGE if group else SMALL,
    )(err, wc, qkv, probs)


def qkv_sums_kernel(side, g0_ref, g1_ref, normed_t, w_ref, b_ref, to_ref):
    width = g0_ref.shape[2]

    def qkv_part(i, carry):
        cells = jnp.concatenate([g0_ref[3 * side + i], g1_ref[3 * side + i]], axis=0)
        grad = jnp.dot(normed_t[...], cells, preferred_element_type=F32)
        hi, lo = masked_sums(grad, w_ref[i].astype(F32), b_ref[i])
        to_ref[0:1, pl.ds(pl.multiple_of(i * width, width), width)] = hi
        to_ref[1:2, pl.ds(pl.multiple_of(i * width, width), width)] = lo
        return carry

    lax.fori_loop(0, 3, qkv_part, 0)


def qkv_sums(side, g, normed_t, w, b):
    width = g[0].shape[2]
    return pl.pallas_call(
        functools.partial(qkv_sums_kernel, side),
        out_shape=jax.ShapeDtypeStruct((2, 3 * width), F32),
        in_specs=spec(5),
        out_specs=spec(1)[0],
        compiler_params=params(20),
        cost_estimate=LARGE,
    )(*g, normed_t, w, b)


def halves_kernel(x_ref, low_ref, up_ref, sems):
    half = low_ref.shape[1]
    low = pltpu.make_async_copy(x_ref.at[:, :half], low_ref, sems.at[0])
    up = pltpu.make_async_copy(x_ref.at[:, half:], up_ref, sems.at[1])
    low.start()
    up.start()
    low.wait()
    up.wait()


def halves_of(block):
    rows, lon, lev, width = block.shape
    half = jax.ShapeDtypeStruct((rows, lon // 2, lev, width), BF)
    return pl.pallas_call(
        halves_kernel,
        out_shape=(half, half),
        in_specs=[pl.BlockSpec(memory_space=pltpu.HBM)],
        out_specs=tuple(spec(2)),
        scratch_shapes=[pltpu.SemaphoreType.DMA((2,))],
        compiler_params=params(16),
        cost_estimate=SMALL,
    )(block)


def split_kernel(s_ref, *refs):
    offset, core = s_ref[0], s_ref[1]
    pairs = (len(refs) - 1) // 3
    rows, lon, lev, width = refs[1].shape
    many = (rows + WLAT) // 2
    half = lon * lev
    cells = 2 * WLAT * half
    for rel in range(2):
        base = many * (core ^ rel) - offset

        def body(w, carry):
            at = pl.ds(pl.multiple_of(w * cells, 16), cells)
            for i in range(pairs):
                up_ref, low_ref = refs[2 * i : 2 * i + 2]
                parts = []
                for ref, part in ((up_ref, slice(up_ref.shape[1] - lon, up_ref.shape[1])), (low_ref, slice(0, lon))):
                    for j in range(WLAT):
                        r = base + WLAT * w + j
                        v = ref[jnp.clip(r, 0, rows - 1), part].astype(F32).reshape(half, width)
                        parts.append(jnp.where((r >= 0) & (r < rows), v, 0.0))
                block = jnp.concatenate(parts, axis=0).astype(BF)
                if rel:
                    refs[-1][i, at, :] = block
                else:
                    refs[2 * pairs + i][at, :] = block
            return carry

        lax.fori_loop(0, many // WLAT, body, 0)


def split(place, *halves):
    rows, lon, lev, width = halves[1].shape
    pairs = len(halves) // 2
    n = (rows + WLAT) * lon * lev
    return pl.pallas_call(
        split_kernel,
        out_shape=(jax.ShapeDtypeStruct((n, width), BF),) * pairs
        + (jax.ShapeDtypeStruct((pairs, n, width), BF),),
        in_specs=[pl.BlockSpec(memory_space=pltpu.SMEM)] + spec(2 * pairs),
        out_specs=tuple(spec(pairs + 1)),
        compiler_params=params(16),
        cost_estimate=SMALL,
    )(place, *halves)


def cell_at(c, window):
    cells = 2 * WLAT * window
    w = sum((c >= i * cells).astype(jnp.int32) for i in range(1, 4))
    c = c - w * cells
    s = (c >= WLAT * window).astype(jnp.int32)
    c = c - s * WLAT * window
    r = sum((c >= i * window).astype(jnp.int32) for i in range(1, WLAT))
    c = c - r * window
    return w * WLAT + r, s * (window // 2) + (c >> 1), c & 1


def ids_kernel(s_ref, ids_ref, idk_ref, idq_ref):
    offset, core, sector = s_ref[0], s_ref[1], s_ref[2]
    rows, lev, total = ids_ref.shape
    n = idk_ref.shape[0]
    cells = n // 4
    window = cells // (2 * WLAT)
    many = (rows + WLAT) // 2
    ids = ids_ref[...].astype(F32).reshape(rows * lev, total)

    def find(c):
        r, lon, level = cell_at(c, window)
        r = r + many * core - offset
        lon = lon + sector * window + window // 2
        lon = jnp.where(lon >= total, lon - total, lon)
        valid = (r >= 0) & (r < rows)
        return jnp.where(valid, 2 * r + level, -1), lon, valid

    spot, lon, valid = find(lax.broadcasted_iota(jnp.int32, (n, 1), 0))
    at = lax.broadcasted_iota(jnp.int32, (n, rows * lev), 1) == spot
    found = jnp.dot(jnp.where(at, 1.0, 0.0), ids, preferred_element_type=F32)
    there = lax.broadcasted_iota(jnp.int32, (n, total), 1) == lon
    found = jnp.sum(jnp.where(there, found, 0.0), axis=1, keepdims=True)
    idk_ref[...] = jnp.where(valid, found, -1.0).astype(jnp.int32)
    for w in range(4):
        lane = lax.broadcasted_iota(jnp.int32, (1, 2 * cells), 1)
        spot, lon, valid = find(w * cells + jnp.where(lane >= cells, lane - cells, lane))
        there = lax.broadcasted_iota(jnp.int32, (total, 2 * cells), 0) == lon
        found = jnp.dot(ids, jnp.where(there, 1.0, 0.0), preferred_element_type=F32)
        at = lax.broadcasted_iota(jnp.int32, (rows * lev, 2 * cells), 0) == spot
        found = jnp.sum(jnp.where(at, found, 0.0), axis=0, keepdims=True)
        idq_ref[w] = jnp.where(valid, found, -1.0).astype(jnp.int32)


def window_ids(place, ids, cells):
    return pl.pallas_call(
        ids_kernel,
        out_shape=(
            jax.ShapeDtypeStruct((4 * cells, 1), jnp.int32),
            jax.ShapeDtypeStruct((4, 1, 2 * cells), jnp.int32),
        ),
        in_specs=[pl.BlockSpec(memory_space=pltpu.SMEM)] + spec(1),
        out_specs=tuple(spec(2)),
        compiler_params=params(16),
        cost_estimate=SMALL,
    )(place, ids)


def join_kernel(s_ref, a0, a1, b0, b1, out_ref, grid_ref):
    offset, core = s_ref[0], s_ref[1]
    rows, lon, lev, width = out_ref.shape
    many = (rows + WLAT) // 2
    half = lon * lev // 2
    for rel, ins in ((0, (a0, a1)), (1, (b0, b1))):
        base = many * (core ^ rel)
        for s in range(2):
            for i in range(many // 4):
                v = ins[s][4 * half * i : 4 * half * (i + 1), :].astype(F32)
                for j in range(4):
                    grid_ref[base + 4 * i + j, half * (1 - s) : half * (2 - s), :] = v[
                        half * j : half * (j + 1)
                    ]

    def body(i, carry):
        for j in range(2):
            r = 2 * i + j
            out_ref[r] = grid_ref[r + offset].reshape(lon, lev, width).astype(BF)
        return carry

    lax.fori_loop(0, rows // 2, body, 0)


def join(place, parts, rows, lon, lev):
    n, width = parts[0].shape
    out = pl.pallas_call(
        join_kernel,
        out_shape=jax.ShapeDtypeStruct((rows, lon, lev, width), BF),
        in_specs=[pl.BlockSpec(memory_space=pltpu.SMEM)] + spec(4),
        out_specs=spec(1)[0],
        scratch_shapes=[pltpu.VMEM((rows + WLAT, lon * lev, width), F32)],
        compiler_params=params(16),
        cost_estimate=SMALL,
    )(place, *parts)
    return jnp.transpose(out, (0, 2, 1, 3))


def send(block, shift, flip):
    count, tp = lax.axis_size("lat"), lax.axis_size("tp")
    route = [
        (u * tp + t, ((u + shift) % count) * tp + (t ^ flip)) for u in range(count) for t in range(tp)
    ]
    return lax.ppermute(block, ("lat", "tp"), route)


def swap(block, other, flip):
    count, tp = lax.axis_size("lat"), lax.axis_size("tp")
    route = [(u * tp + t, (u ^ other) * tp + (t ^ flip)) for u in range(count) for t in range(tp)]
    return lax.ppermute(block, ("lat", "tp"), route)


def lat_terms(block, bit):
    count = lax.axis_size("lat")
    terms = [block]
    while bit < count:
        block = added(terms)
        terms = [block, swap(block, bit, 0)]
        if 4 * bit <= count:
            terms += [swap(block, 2 * bit, 0), swap(block, 3 * bit, 0)]
        bit *= len(terms)
    return terms


def added(terms):
    while len(terms) > 1:
        terms = [a + b for a, b in zip(terms[::2], terms[1::2])]
    return terms[0]


def after(block, *others):
    return lax.optimization_barrier((block, *others))[0]


def local(features, target, w_qkv, w_proj, qkv_clip, proj_clip, shift_offset, region_ids):
    rows, lev, lon, width = features.shape
    half = lon // 2
    sector = lax.axis_index("lat")
    t = lax.axis_index("tp")
    t_arr = jnp.reshape(t, (1,)).astype(jnp.int32)
    place = jnp.stack([shift_offset[0], t % 2, sector]).astype(jnp.int32)

    f_raw, t_raw = (jnp.transpose(block, (0, 2, 1, 3)) for block in (features, target))
    f_low, f_up = halves_of(f_raw)
    f_low, f_up, w_qkv, w_proj = lax.optimization_barrier((f_low, f_up, w_qkv, w_proj))
    f_up_y = send(f_up, 0, 2)
    f_low = send(f_low, -1, 0)

    w3 = jnp.transpose(w_qkv, (1, 0, 2))
    c3 = jnp.transpose(qkv_clip, (1, 0, 2))
    w3_peer = send(w3, 0, 1)
    c3_peer = send(c3, 0, 1)
    share = w_proj.shape[0] // 2
    w1 = send(w_proj, 0, 1)
    wc_own, b_own = clip_qkv(w3, c3)
    slab = lax.dynamic_slice_in_dim(after(w_proj, wc_own), share * (sector % 2), share, 0)
    wc_peer, b_peer = clip_qkv(w3_peer, c3_peer)
    idk, idq = window_ids(place, region_ids, WLAT * lev * lon)
    f_up_y, f_low, w1, t_low, slab, wc_own = lax.optimization_barrier(
        (f_up_y, f_low, w1, t_raw[:, :half], slab, wc_own)
    )
    f_low_y = send(f_low, 0, 2)
    t_low = send(t_low, -1, 0)
    f_low_y, t_low, wc_peer, idk, idq = lax.optimization_barrier((f_low_y, t_low, wc_peer, idk, idq))
    slab = send(slab, 0, 2)
    x_0, x_2, x_away = split(place, f_raw, f_low, f_up_y, f_low_y)
    pieces = (x_0, x_2, send(x_away, 0, 1))

    t_own, t_away = split(place, after(t_raw, x_0), t_low)
    t_away = t_away.reshape(t_own.shape)
    targets = (t_own, send(t_away, 0, 1), send(t_own, 0, 2), send(t_away, 0, 3))

    normed, qkv, attn_0 = forward(t_arr, pieces, wc_own, wc_peer, idk, idq)
    other_0 = send(attn_0, 0, 2)
    probs_0 = probs_of(0, qkv, idk, idq)
    slab = after(slab, probs_0)
    more = swap(slab, 1, 0)
    attn_1 = last_windows(after(qkv, probs_0, *targets, more), idk, idq)
    slab_3, more_3 = send(after(slab, attn_1), 0, 1), send(after(more, attn_1), 0, 1)
    pc, pb = clip_proj(place, [w_proj, w1, slab, more, slab_3, more_3], proj_clip)
    other_1 = send(attn_1, 0, 2)
    normed_t, attn_t = turn(normed, (attn_0, attn_1))
    probs = (probs_0, probs_of(1, after(qkv, attn_1), idk, idq))

    *mixed, err_0 = output(t_arr, pieces, targets, attn_0, other_0, pc, idk)
    grads_0 = backward(0, err_0, pc, qkv, probs[0])
    other_1 = after(other_1, grads_0)
    m00, m01, m10, m11, err_1 = output(t_arr, pieces, targets, attn_1, other_1, pc, idk, mixed)
    m01 = send(m01, 0, 1)
    m10 = send(m10, 1, 0)
    m11 = send(m11, 1, 1)
    proj = proj_sums((err_0, err_1), attn_t, w_proj, w1, pb)
    proj_y = send(proj, 0, 2)
    grads = (grads_0, backward(1, err_1, pc, qkv, probs[1]))
    peer = qkv_sums(1, grads, normed_t, w3_peer, b_peer)
    proj = proj + proj_y
    peer = jnp.concatenate([peer, proj], axis=1)
    terms = [send(peer, 0, 1), swap(peer, 1, 1)]
    grads = lax.optimization_barrier((*grads, m01, m10, m11, peer))[:2]
    own = qkv_sums(0, grads, normed_t, w3, b_own)
    own = jnp.concatenate([own, proj], axis=1)
    sums = added([own, terms[0], swap(own, 1, 0), terms[1]])
    sums = added(lat_terms(sums, 2))
    mixed = join(place, [m00, m10, m01, m11], rows, lon, lev)
    return (mixed, sums[:, : 3 * width].reshape(2, 3, width), sums[:, 3 * width :])


def solution(mesh):
    placed = (
        P(None, None, "lat", "tp"),
        P(None, None, "lat", "tp"),
        P(None, None, "tp"),
        P("tp", None),
        P(None, None, "tp"),
        P(),
        P(),
        P(),
    )
    return jax.shard_map(
        local,
        mesh=mesh,
        in_specs=placed,
        out_specs=(P(None, None, "lat", "tp"), P(None, None, "tp"), P()),
        check_vma=False,
    )
```

```python
import functools

import jax
import jax.numpy as jnp
from jax import lax
from jax.experimental import pallas as pl
from jax.experimental.pallas import tpu as pltpu
from jax.sharding import PartitionSpec as P

HD = 64
WLAT = 6
EPS = 1e-05
NEG = -1e30
F32 = jnp.float32
BF = jnp.bfloat16
SCALE = HD ** (-0.5)
NT = (((1,), (1,)), ((), ()))
TN = (((0,), (0,)), ((), ()))
LARGE = pl.CostEstimate(flops=8 * 10**9, bytes_accessed=10**7, transcendentals=10**6)
SMALL = pl.CostEstimate(flops=1, bytes_accessed=1, transcendentals=0)


def spec(n):
    return [pl.BlockSpec(memory_space=pltpu.VMEM)] * n


def params(mib):
    return pltpu.CompilerParams(vmem_limit_bytes=mib * 1024 * 1024)


def bounds_of(weight, logits_hi, logits_lo):
    top = jnp.max(weight, axis=0, keepdims=True)
    low = jnp.min(weight, axis=0, keepdims=True)
    hi = 1.0 / (1.0 + jnp.exp(-logits_hi))
    lo = 1.0 / (1.0 + jnp.exp(-logits_lo))
    return hi * top, lo * low, hi * (1.0 - hi) * top, lo * (1.0 - lo) * low


def clip_qkv_kernel(w_ref, c_ref, wc_ref, b_ref):
    def body(i, carry):
        w = w_ref[i].astype(F32)
        up, lw, fh, fl = bounds_of(w, c_ref[i, 0:1], c_ref[i, 1:2])
        wc_ref[i] = jnp.minimum(jnp.maximum(w, lw), up).astype(BF)
        b_ref[i, 0:1] = up
        b_ref[i, 1:2] = lw
        b_ref[i, 2:3] = fh
        b_ref[i, 3:4] = fl
        return carry

    lax.fori_loop(0, 3, body, 0)


def clip_qkv(w, clips):
    n, d, e = w.shape
    return pl.pallas_call(
        clip_qkv_kernel,
        out_shape=(
            jax.ShapeDtypeStruct((n, d, e), BF),
            jax.ShapeDtypeStruct((n, 8, e), F32),
        ),
        in_specs=spec(2),
        out_specs=tuple(spec(2)),
        compiler_params=params(24),
        cost_estimate=SMALL,
    )(w, clips)


def clip_proj_kernel(s_ref, w0, w1, a2, b2, a3, b3, c_ref, wc_ref, b_ref):
    second = s_ref[2] % 2 == 1

    def body(i, carry):
        cols = pl.ds(pl.multiple_of(i * 256, 256), 256)
        parts = [w0[:, cols].astype(F32), w1[:, cols].astype(F32)]
        for first_ref, other_ref in ((a2, b2), (a3, b3)):
            a, b = first_ref[:, cols].astype(F32), other_ref[:, cols].astype(F32)
            parts += [jnp.where(second, b, a), jnp.where(second, a, b)]
        w = jnp.concatenate(parts, axis=0)
        up, lw, fh, fl = bounds_of(w, c_ref[0:1, cols], c_ref[1:2, cols])
        wc = jnp.minimum(jnp.maximum(w, lw), up).astype(BF)
        wc_ref[:, cols] = wc
        b_ref[0:1, cols] = up
        b_ref[1:2, cols] = lw
        b_ref[2:3, cols] = fh
        b_ref[3:4, cols] = fl
        return carry

    lax.fori_loop(0, w0.shape[1] // 256, body, 0)


def clip_proj(place, shards, clips):
    e, d = shards[0].shape
    return pl.pallas_call(
        clip_proj_kernel,
        out_shape=(
            jax.ShapeDtypeStruct((4 * e, d), BF),
            jax.ShapeDtypeStruct((8, d), F32),
        ),
        in_specs=[pl.BlockSpec(memory_space=pltpu.SMEM)] + spec(7),
        out_specs=tuple(spec(2)),
        compiler_params=params(24),
        cost_estimate=SMALL,
    )(place, *shards, clips)


def stacked(block, mask_a, mask_b):
    return jnp.concatenate([block * mask_a, block * mask_b], axis=0)


def head_masks():
    lane = lax.broadcasted_iota(jnp.int32, (1, 2 * HD), 1)
    mask_a = jnp.where(lane < HD, 1.0, 0.0).astype(BF)
    mask_b = jnp.where(lane < HD, 0.0, 1.0).astype(BF)
    return mask_a, mask_b


def probs_t(k, q2, allowed):
    st = lax.dot_general(k, q2, NT, preferred_element_type=F32) * SCALE
    st = jnp.where(allowed, st, NEG)
    e = jnp.exp(st - jnp.max(st, axis=0, keepdims=True))
    return e * (1.0 / jnp.sum(e, axis=0, keepdims=True))


def merge_heads(t_block):
    both = t_block.T
    n = both.shape[0] // 2
    lane = lax.broadcasted_iota(jnp.int32, (n, 2 * HD), 1)
    return jnp.where(lane < HD, both[:n], both[n:])


def allowed_t(idk_ref, idq_ref, w, cells):
    rows = pl.ds(pl.multiple_of(w * cells, 16), cells)
    idk = idk_ref[rows, :]
    return (idk == idq_ref[w]) & (idk >= 0)


def blocks(refs):
    own, other, away = refs
    return own, away.at[0], other, away.at[1]


def forward_kernel(t_ref, *refs):
    pieces = blocks(refs[:3])
    wo_ref, wp_ref, idk_ref, idq_ref, normed_ref, qkv_ref, attn_ref = refs[3:]
    t = t_ref[0]
    n, width = pieces[0].shape
    d = 4 * width

    def norm(w, carry):
        rows = pl.ds(pl.multiple_of(w * 48, 16), 48)
        x = [r[rows, :].astype(F32) for r in pieces]
        mean = sum(jnp.sum(b, axis=-1, keepdims=True) for b in x) / d
        x = [b - mean for b in x]
        var = sum(jnp.sum(b * b, axis=-1, keepdims=True) for b in x) / d
        scale = lax.rsqrt(var + EPS)
        for k in range(4):
            cols = pl.ds(pl.multiple_of((t ^ k) * width, width), width)
            normed_ref[rows, cols] = (x[k] * scale).astype(BF)
        return carry

    lax.fori_loop(0, n // 48, norm, 0)

    def project(i, carry):
        for g, w_ref in enumerate((wo_ref, wp_ref)):
            qkv_ref[3 * g + i] = jnp.dot(
                normed_ref[...], w_ref[i], preferred_element_type=F32
            ).astype(BF)
        return carry

    lax.fori_loop(0, 3, project, 0)
    attend(qkv_ref, idk_ref, idq_ref, attn_ref, 0, 2)


def attend(qkv_ref, idk_ref, idq_ref, attn_ref, first, last):
    mask_a, mask_b = head_masks()
    cells = idk_ref.shape[0] // 4

    def window(w, carry):
        rows = pl.ds(pl.multiple_of(w * cells, 16), cells)
        to = pl.ds(pl.multiple_of((w - first) * cells, 16), cells)
        allowed = allowed_t(idk_ref, idq_ref, w, cells)
        for hp in range(4):
            g, lanes = hp // 2, slice(128 * (hp % 2), 128 * (hp % 2) + 128)
            q2 = stacked(qkv_ref[3 * g, rows, lanes], mask_a, mask_b)
            pt = probs_t(qkv_ref[3 * g + 1, rows, lanes], q2, allowed)
            ot = lax.dot_general(
                qkv_ref[3 * g + 2, rows, lanes], pt.astype(BF), TN, preferred_element_type=F32
            )
            attn_ref[to, 128 * hp : 128 * hp + 128] = merge_heads(ot).astype(BF)
        return carry

    lax.fori_loop(first, last, window, 0)


def last_kernel(qkv_ref, idk_ref, idq_ref, attn_ref):
    attend(qkv_ref, idk_ref, idq_ref, attn_ref, 2, 4)


def last_windows(qkv, idk, idq):
    n, width = qkv.shape[1:]
    return pl.pallas_call(
        last_kernel,
        out_shape=jax.ShapeDtypeStruct((n // 2, 2 * width), BF),
        in_specs=spec(3),
        out_specs=spec(1)[0],
        compiler_params=params(16),
        cost_estimate=pl.CostEstimate(flops=1, bytes_accessed=1, transcendentals=0),
    )(qkv, idk, idq)


def forward(t, pieces, wo, wp, idk, idq):
    n, width = pieces[0].shape
    d = 4 * width
    return pl.pallas_call(
        forward_kernel,
        out_shape=(
            jax.ShapeDtypeStruct((n, d), BF),
            jax.ShapeDtypeStruct((6, n, width), BF),
            jax.ShapeDtypeStruct((n // 2, 2 * width), BF),
        ),
        in_specs=[pl.BlockSpec(memory_space=pltpu.SMEM)] + spec(7),
        out_specs=tuple(spec(3)),
        compiler_params=params(20),
        cost_estimate=pl.CostEstimate(flops=8 * 10**9, bytes_accessed=10 * 10**6, transcendentals=10**6),
    )(t, *pieces, wo, wp, idk, idq)


def turn_kernel(normed_ref, a_ref, b_ref, normed_t, attn_t):
    d = normed_ref.shape[1]

    def body(i, carry):
        cols = pl.ds(pl.multiple_of(i * 256, 256), 256)
        normed_t[cols, :] = normed_ref[:, cols].T
        return carry

    lax.fori_loop(0, d // 256, body, 0)

    def body2(i, carry):
        cols = pl.ds(pl.multiple_of(i * 256, 256), 256)
        attn_t[cols, :] = jnp.concatenate([a_ref[:, cols], b_ref[:, cols]], axis=0).T
        return carry

    lax.fori_loop(0, a_ref.shape[1] // 256, body2, 0)


def turn(normed, attn):
    n, d = normed.shape
    e = attn[0].shape[1]
    return pl.pallas_call(
        turn_kernel,
        out_shape=(jax.ShapeDtypeStruct((d, n), BF), jax.ShapeDtypeStruct((e, n), BF)),
        in_specs=spec(3),
        out_specs=tuple(spec(2)),
        compiler_params=params(16),
        cost_estimate=SMALL,
    )(normed, *attn)


def output_kernel(group, t_ref, *refs):
    pieces, targets = blocks(refs[:3]), refs[3:7]
    own_ref, other_ref, wc_ref, idk_ref = refs[7:11]
    before, refs = refs[11 : 11 + 4 * group], refs[11 + 4 * group :]
    mixed, err_ref, y_ref = refs[:4], refs[4], refs[5]
    t = t_ref[0]
    n, width = pieces[0].shape
    cells = n // 4
    half = cells // 2
    e = own_ref.shape[1]
    for old, new in zip(before, mixed):
        new[: group * cells, :] = old[...]
    for k in range(4):
        x_ref, want_ref = pieces[k], targets[k]
        cols = pl.ds(pl.multiple_of((t ^ k) * width, width), width)
        y_ref[...] = jnp.dot(own_ref[...], wc_ref[:e, cols], preferred_element_type=F32) + jnp.dot(
            other_ref[...], wc_ref[e:, cols], preferred_element_type=F32
        )
        ys = []
        for i in range(2):
            at = slice(cells * i, cells * (i + 1))
            rows = slice(cells * (2 * group + i), cells * (2 * group + i + 1))
            y = x_ref[rows, :].astype(F32) + y_ref[at, :]
            ys.append(y)
            err = y - want_ref[rows, :].astype(F32)
            valid = idk_ref[rows, :] >= 0
            err_ref[at, cols] = jnp.where(valid, err, 0.0).astype(BF)
        if k < 2:
            at = slice(cells * group, cells * (group + 1))
            for s in range(2):
                part = slice(half * s, half * (s + 1))
                mixed[2 * s + k][at, :] = jnp.concatenate([y[part] for y in ys], axis=0).astype(BF)


def output(t, pieces, targets, own, other, wc, idk, before=()):
    n, width = pieces[0].shape
    group = 1 if before else 0
    piece = jax.ShapeDtypeStruct((n // 4 * (1 + group), width), BF)
    return pl.pallas_call(
        functools.partial(output_kernel, group),
        out_shape=(piece, piece, piece, piece, jax.ShapeDtypeStruct((n // 2, 4 * width), BF)),
        in_specs=[pl.BlockSpec(memory_space=pltpu.SMEM)] + spec(11 + len(before)),
        out_specs=tuple(spec(5)),
        scratch_shapes=[pltpu.VMEM((n // 2, width), F32)],
        compiler_params=params(20),
        cost_estimate=SMALL,
    )(t, *pieces, *targets, own, other, wc, idk, *before)


def probs_kernel(group, qkv_ref, idk_ref, idq_ref, p_ref):
    cells = idk_ref.shape[0] // 4
    mask_a, mask_b = head_masks()

    def window(i, carry):
        w = 2 * group + i
        rows = pl.ds(pl.multiple_of(w * cells, 16), cells)
        allowed = allowed_t(idk_ref, idq_ref, w, cells)
        for hp in range(4):
            g, lanes = hp // 2, slice(128 * (hp % 2), 128 * (hp % 2) + 128)
            q2 = stacked(qkv_ref[3 * g, rows, lanes], mask_a, mask_b)
            p_ref[4 * i + hp] = probs_t(qkv_ref[3 * g + 1, rows, lanes], q2, allowed)
        return carry

    lax.fori_loop(0, 2, window, 0)


def probs_of(group, qkv, idk, idq):
    n, width = qkv.shape[1:]
    return pl.pallas_call(
        functools.partial(probs_kernel, group),
        out_shape=jax.ShapeDtypeStruct((8, n // 4, n // 2), F32),
        in_specs=spec(3),
        out_specs=spec(1)[0],
        compiler_params=params(16),
        cost_estimate=SMALL,
    )(qkv, idk, idq)


def masked_sums(grad, w, bounds):
    g_hi = jnp.sum(jnp.where(w > bounds[0:1], grad, 0.0), axis=0, keepdims=True) * bounds[2:3]
    g_lo = jnp.sum(jnp.where(w < bounds[1:2], grad, 0.0), axis=0, keepdims=True) * bounds[3:4]
    return g_hi, g_lo


def proj_sums_kernel(e0_ref, e1_ref, attn_t, po_ref, pp_ref, pb_ref, proj_ref):
    def proj_part(i, carry):
        cols = pl.ds(pl.multiple_of(i * 256, 256), 256)
        err = jnp.concatenate([e0_ref[:, cols], e1_ref[:, cols]], axis=0)
        grad = jnp.dot(attn_t[...], err, preferred_element_type=F32)
        n = po_ref.shape[0]
        b = pb_ref[:, cols]
        h0, l0 = masked_sums(grad[:n], po_ref[:, cols].astype(F32), b)
        h1, l1 = masked_sums(grad[n:], pp_ref[:, cols].astype(F32), b)
        proj_ref[0:1, cols] = h0 + h1
        proj_ref[1:2, cols] = l0 + l1
        return carry

    lax.fori_loop(0, 4, proj_part, 0)


def proj_sums(errs, attn_t, po, pp, pb):
    return pl.pallas_call(
        proj_sums_kernel,
        out_shape=jax.ShapeDtypeStruct((2, errs[0].shape[1]), F32),
        in_specs=spec(6),
        out_specs=spec(1)[0],
        compiler_params=params(16),
        cost_estimate=pl.CostEstimate(flops=10**9, bytes_accessed=3 * 10**6, transcendentals=0),
    )(*errs, attn_t, po, pp, pb)


def backward_kernel(group, err_ref, wc_ref, qkv_ref, p_ref, g_ref, d_ref):
    e = d_ref.shape[1]
    cells = d_ref.shape[0] // 2
    d_ref[...] = lax.dot_general(err_ref[...], wc_ref[:e], NT, preferred_element_type=F32).astype(BF)
    mask_a, mask_b = head_masks()

    def window(i, carry):
        rows = pl.ds(pl.multiple_of((2 * group + i) * cells, 16), cells)
        at = pl.ds(pl.multiple_of(i * cells, 16), cells)
        for hp in range(4):
            g, lanes = hp // 2, slice(128 * (hp % 2), 128 * (hp % 2) + 128)
            q2 = stacked(qkv_ref[3 * g, rows, lanes], mask_a, mask_b)
            k = qkv_ref[3 * g + 1, rows, lanes]
            v = qkv_ref[3 * g + 2, rows, lanes]
            pt = p_ref[4 * i + hp]
            d2 = stacked(d_ref[at, 128 * hp : 128 * hp + 128], mask_a, mask_b)
            g_ref[3 * g + 2, at, lanes] = jnp.dot(
                pt.astype(BF), d2, preferred_element_type=F32
            ).astype(BF)
            dpt = lax.dot_general(v, d2, NT, preferred_element_type=F32)
            gst = (pt * (dpt - jnp.sum(pt * dpt, axis=0, keepdims=True))).astype(BF)
            g_ref[3 * g + 1, at, lanes] = (
                jnp.dot(gst, q2, preferred_element_type=F32) * SCALE
            ).astype(BF)
            gqt = lax.dot_general(k, gst, TN, preferred_element_type=F32) * SCALE
            g_ref[3 * g, at, lanes] = merge_heads(gqt).astype(BF)
        return carry

    lax.fori_loop(0, 2, window, 0)


def backward(group, err, wc, qkv, probs):
    n, width = qkv.shape[1:]
    return pl.pallas_call(
        functools.partial(backward_kernel, group),
        out_shape=jax.ShapeDtypeStruct((6, n // 2, width), BF),
        in_specs=spec(4),
        out_specs=spec(1)[0],
        scratch_shapes=[pltpu.VMEM((n // 2, 2 * width), BF)],
        compiler_params=params(20),
        cost_estimate=LARGE if group else SMALL,
    )(err, wc, qkv, probs)


def qkv_sums_kernel(side, g0_ref, g1_ref, normed_t, w_ref, b_ref, to_ref):
    width = g0_ref.shape[2]

    def qkv_part(i, carry):
        cells = jnp.concatenate([g0_ref[3 * side + i], g1_ref[3 * side + i]], axis=0)
        grad = jnp.dot(normed_t[...], cells, preferred_element_type=F32)
        hi, lo = masked_sums(grad, w_ref[i].astype(F32), b_ref[i])
        to_ref[0:1, pl.ds(pl.multiple_of(i * width, width), width)] = hi
        to_ref[1:2, pl.ds(pl.multiple_of(i * width, width), width)] = lo
        return carry

    lax.fori_loop(0, 3, qkv_part, 0)


def qkv_sums(side, g, normed_t, w, b):
    width = g[0].shape[2]
    return pl.pallas_call(
        functools.partial(qkv_sums_kernel, side),
        out_shape=jax.ShapeDtypeStruct((2, 3 * width), F32),
        in_specs=spec(5),
        out_specs=spec(1)[0],
        compiler_params=params(20),
        cost_estimate=LARGE,
    )(*g, normed_t, w, b)


def halves_kernel(x_ref, low_ref, up_ref, sems):
    half = low_ref.shape[1]
    low = pltpu.make_async_copy(x_ref.at[:, :half], low_ref, sems.at[0])
    up = pltpu.make_async_copy(x_ref.at[:, half:], up_ref, sems.at[1])
    low.start()
    up.start()
    low.wait()
    up.wait()


def halves_of(block):
    rows, lon, lev, width = block.shape
    half = jax.ShapeDtypeStruct((rows, lon // 2, lev, width), BF)
    return pl.pallas_call(
        halves_kernel,
        out_shape=(half, half),
        in_specs=[pl.BlockSpec(memory_space=pltpu.HBM)],
        out_specs=tuple(spec(2)),
        scratch_shapes=[pltpu.SemaphoreType.DMA((2,))],
        compiler_params=params(16),
        cost_estimate=SMALL,
    )(block)


def split_kernel(s_ref, *refs):
    offset, core = s_ref[0], s_ref[1]
    pairs = (len(refs) - 1) // 3
    rows, lon, lev, width = refs[1].shape
    many = (rows + WLAT) // 2
    half = lon * lev
    cells = 2 * WLAT * half
    for rel in range(2):
        base = many * (core ^ rel) - offset

        def body(w, carry):
            at = pl.ds(pl.multiple_of(w * cells, 16), cells)
            for i in range(pairs):
                up_ref, low_ref = refs[2 * i : 2 * i + 2]
                parts = []
                for ref, part in ((up_ref, slice(up_ref.shape[1] - lon, up_ref.shape[1])), (low_ref, slice(0, lon))):
                    for j in range(WLAT):
                        r = base + WLAT * w + j
                        v = ref[jnp.clip(r, 0, rows - 1), part].astype(F32).reshape(half, width)
                        parts.append(jnp.where((r >= 0) & (r < rows), v, 0.0))
                block = jnp.concatenate(parts, axis=0).astype(BF)
                if rel:
                    refs[-1][i, at, :] = block
                else:
                    refs[2 * pairs + i][at, :] = block
            return carry

        lax.fori_loop(0, many // WLAT, body, 0)


def split(place, *halves):
    rows, lon, lev, width = halves[1].shape
    pairs = len(halves) // 2
    n = (rows + WLAT) * lon * lev
    return pl.pallas_call(
        split_kernel,
        out_shape=(jax.ShapeDtypeStruct((n, width), BF),) * pairs
        + (jax.ShapeDtypeStruct((pairs, n, width), BF),),
        in_specs=[pl.BlockSpec(memory_space=pltpu.SMEM)] + spec(2 * pairs),
        out_specs=tuple(spec(pairs + 1)),
        compiler_params=params(16),
        cost_estimate=SMALL,
    )(place, *halves)


def cell_at(c, window):
    cells = 2 * WLAT * window
    w = sum((c >= i * cells).astype(jnp.int32) for i in range(1, 4))
    c = c - w * cells
    s = (c >= WLAT * window).astype(jnp.int32)
    c = c - s * WLAT * window
    r = sum((c >= i * window).astype(jnp.int32) for i in range(1, WLAT))
    c = c - r * window
    return w * WLAT + r, s * (window // 2) + (c >> 1), c & 1


def ids_kernel(s_ref, ids_ref, idk_ref, idq_ref):
    offset, core, sector = s_ref[0], s_ref[1], s_ref[2]
    rows, lev, total = ids_ref.shape
    n = idk_ref.shape[0]
    cells = n // 4
    window = cells // (2 * WLAT)
    many = (rows + WLAT) // 2
    ids = ids_ref[...].astype(F32).reshape(rows * lev, total)

    def find(c):
        r, lon, level = cell_at(c, window)
        r = r + many * core - offset
        lon = lon + sector * window + window // 2
        lon = jnp.where(lon >= total, lon - total, lon)
        valid = (r >= 0) & (r < rows)
        return jnp.where(valid, 2 * r + level, -1), lon, valid

    spot, lon, valid = find(lax.broadcasted_iota(jnp.int32, (n, 1), 0))
    at = lax.broadcasted_iota(jnp.int32, (n, rows * lev), 1) == spot
    found = jnp.dot(jnp.where(at, 1.0, 0.0), ids, preferred_element_type=F32)
    there = lax.broadcasted_iota(jnp.int32, (n, total), 1) == lon
    found = jnp.sum(jnp.where(there, found, 0.0), axis=1, keepdims=True)
    idk_ref[...] = jnp.where(valid, found, -1.0).astype(jnp.int32)
    for w in range(4):
        lane = lax.broadcasted_iota(jnp.int32, (1, 2 * cells), 1)
        spot, lon, valid = find(w * cells + jnp.where(lane >= cells, lane - cells, lane))
        there = lax.broadcasted_iota(jnp.int32, (total, 2 * cells), 0) == lon
        found = jnp.dot(ids, jnp.where(there, 1.0, 0.0), preferred_element_type=F32)
        at = lax.broadcasted_iota(jnp.int32, (rows * lev, 2 * cells), 0) == spot
        found = jnp.sum(jnp.where(at, found, 0.0), axis=0, keepdims=True)
        idq_ref[w] = jnp.where(valid, found, -1.0).astype(jnp.int32)


def window_ids(place, ids, cells):
    return pl.pallas_call(
        ids_kernel,
        out_shape=(
            jax.ShapeDtypeStruct((4 * cells, 1), jnp.int32),
            jax.ShapeDtypeStruct((4, 1, 2 * cells), jnp.int32),
        ),
        in_specs=[pl.BlockSpec(memory_space=pltpu.SMEM)] + spec(1),
        out_specs=tuple(spec(2)),
        compiler_params=params(16),
        cost_estimate=SMALL,
    )(place, ids)


def join_kernel(s_ref, a0, a1, b0, b1, out_ref, grid_ref):
    offset, core = s_ref[0], s_ref[1]
    rows, lon, lev, width = out_ref.shape
    many = (rows + WLAT) // 2
    half = lon * lev // 2
    for rel, ins in ((0, (a0, a1)), (1, (b0, b1))):
        base = many * (core ^ rel)
        for s in range(2):
            for i in range(many // 4):
                v = ins[s][4 * half * i : 4 * half * (i + 1), :].astype(F32)
                for j in range(4):
                    grid_ref[base + 4 * i + j, half * (1 - s) : half * (2 - s), :] = v[
                        half * j : half * (j + 1)
                    ]

    def body(i, carry):
        for j in range(2):
            r = 2 * i + j
            out_ref[r] = grid_ref[r + offset].reshape(lon, lev, width).astype(BF)
        return carry

    lax.fori_loop(0, rows // 2, body, 0)


def join(place, parts, rows, lon, lev):
    n, width = parts[0].shape
    out = pl.pallas_call(
        join_kernel,
        out_shape=jax.ShapeDtypeStruct((rows, lon, lev, width), BF),
        in_specs=[pl.BlockSpec(memory_space=pltpu.SMEM)] + spec(4),
        out_specs=spec(1)[0],
        scratch_shapes=[pltpu.VMEM((rows + WLAT, lon * lev, width), F32)],
        compiler_params=params(16),
        cost_estimate=SMALL,
    )(place, *parts)
    return jnp.transpose(out, (0, 2, 1, 3))


def send(block, shift, flip):
    count, tp = lax.axis_size("lat"), lax.axis_size("tp")
    route = [
        (u * tp + t, ((u + shift) % count) * tp + (t ^ flip)) for u in range(count) for t in range(tp)
    ]
    return lax.ppermute(block, ("lat", "tp"), route)


def swap(block, other, flip):
    count, tp = lax.axis_size("lat"), lax.axis_size("tp")
    route = [(u * tp + t, (u ^ other) * tp + (t ^ flip)) for u in range(count) for t in range(tp)]
    return lax.ppermute(block, ("lat", "tp"), route)


def lat_terms(block, bit):
    count = lax.axis_size("lat")
    terms = [block]
    while bit < count:
        block = added(terms)
        terms = [block, swap(block, bit, 0)]
        if 4 * bit <= count:
            terms += [swap(block, 2 * bit, 0), swap(block, 3 * bit, 0)]
        bit *= len(terms)
    return terms


def added(terms):
    while len(terms) > 1:
        terms = [a + b for a, b in zip(terms[::2], terms[1::2])]
    return terms[0]


def after(block, *others):
    return lax.optimization_barrier((block, *others))[0]


def local(features, target, w_qkv, w_proj, qkv_clip, proj_clip, shift_offset, region_ids):
    rows, lev, lon, width = features.shape
    half = lon // 2
    sector = lax.axis_index("lat")
    t = lax.axis_index("tp")
    t_arr = jnp.reshape(t, (1,)).astype(jnp.int32)
    place = jnp.stack([shift_offset[0], t % 2, sector]).astype(jnp.int32)

    f_raw, t_raw = (jnp.transpose(block, (0, 2, 1, 3)) for block in (features, target))
    f_low, f_up = halves_of(f_raw)
    f_low, f_up, w_qkv, w_proj = lax.optimization_barrier((f_low, f_up, w_qkv, w_proj))
    f_low, f_up_y = send(f_low, -1, 0), send(f_up, 0, 2)

    w3 = jnp.transpose(w_qkv, (1, 0, 2))
    c3 = jnp.transpose(qkv_clip, (1, 0, 2))
    w3_peer = send(w3, 0, 1)
    c3_peer = send(c3, 0, 1)
    share = w_proj.shape[0] // 2
    w1 = send(w_proj, 0, 1)
    wc_own, b_own = clip_qkv(w3, c3)
    slab = after(w_proj, wc_own)
    slab = send(lax.dynamic_slice_in_dim(slab, share * (sector % 2), share, 0), 0, 2)
    wc_peer, b_peer = clip_qkv(w3_peer, c3_peer)
    idk, idq = window_ids(place, region_ids, WLAT * lev * lon)
    f_low, f_up_y, w1, t_low, wc_own = lax.optimization_barrier(
        (f_low, f_up_y, w1, t_raw[:, :half], wc_own)
    )
    f_low_y = send(f_low, 0, 2)
    t_low = send(t_low, -1, 0)
    t_own, t_away = split(place, t_raw, t_low)
    t_away = t_away.reshape(t_own.shape)
    t_1 = send(t_away, 0, 1)
    f_low_y, t_own, t_away, slab, wc_peer, idk, idq = lax.optimization_barrier(
        (f_low_y, t_own, t_away, slab, wc_peer, idk, idq)
    )
    x_0, x_2, x_away = split(place, f_raw, f_low, f_up_y, f_low_y)
    pieces = (x_0, x_2, send(x_away, 0, 1))

    targets = (t_own, t_1, send(t_own, 0, 2), send(t_away, 0, 3))
    more = swap(slab, 1, 0)

    normed, qkv, attn_0 = forward(t_arr, pieces, wc_own, wc_peer, idk, idq)
    other_0 = send(attn_0, 0, 2)
    probs_0 = probs_of(0, qkv, idk, idq)
    attn_1 = last_windows(after(qkv, probs_0, *targets, more), idk, idq)
    slab_3, more_3 = send(after(slab, attn_1), 0, 1), send(after(more, attn_1), 0, 1)
    pc, pb = clip_proj(place, [w_proj, w1, slab, more, slab_3, more_3], proj_clip)
    other_1 = send(attn_1, 0, 2)
    normed_t, attn_t = turn(normed, (attn_0, attn_1))
    probs = (probs_0, probs_of(1, after(qkv, attn_1), idk, idq))

    *mixed, err_0 = output(t_arr, pieces, targets, attn_0, other_0, pc, idk)
    grads_0 = backward(0, err_0, pc, qkv, probs[0])
    other_1 = after(other_1, grads_0)
    m00, m01, m10, m11, err_1 = output(t_arr, pieces, targets, attn_1, other_1, pc, idk, mixed)
    m01 = send(m01, 0, 1)
    m10 = send(m10, 1, 0)
    m11 = send(m11, 1, 1)
    proj = proj_sums((err_0, err_1), attn_t, w_proj, w1, pb)
    proj_y = send(proj, 0, 2)
    grads = (grads_0, backward(1, err_1, pc, qkv, probs[1]))
    peer = qkv_sums(1, grads, normed_t, w3_peer, b_peer)
    proj = proj + proj_y
    peer = jnp.concatenate([peer, proj], axis=1)
    terms = [send(peer, 0, 1), swap(peer, 1, 1)]
    grads = lax.optimization_barrier((*grads, m01, m10, m11, peer))[:2]
    own = qkv_sums(0, grads, normed_t, w3, b_own)
    own = jnp.concatenate([own, proj], axis=1)
    sums = added([own, terms[0], swap(own, 1, 0), terms[1]])
    sums = added(lat_terms(sums, 2))
    mixed = join(place, [m00, m10, m01, m11], rows, lon, lev)
    return (mixed, sums[:, : 3 * width].reshape(2, 3, width), sums[:, 3 * width :])


def solution(mesh):
    placed = (
        P(None, None, "lat", "tp"),
        P(None, None, "lat", "tp"),
        P(None, None, "tp"),
        P("tp", None),
        P(None, None, "tp"),
        P(),
        P(),
        P(),
    )
    return jax.shard_map(
        local,
        mesh=mesh,
        in_specs=placed,
        out_specs=(P(None, None, "lat", "tp"), P(None, None, "tp"), P()),
        check_vma=False,
    )
```
